256 devices in a mesh: dp: 32 (over x_hi, z, core), tensor: 8 (over y, x_lo).
Axes of the slice: x: 4 (x_hi: 2, x_lo: 2; x = x_hi * 2 + x_lo), y: 4, z: 8, core: 2. Of those that a mesh axis runs over, the one named last changes fastest.
Arguments:
- grads: bfloat16 [32, 8192, 2, 1024], P('dp', None, None, 'tensor'), may hold values from -41 to 41
- errors: bfloat16 [32, 8192, 2, 1024], P('dp', None, None, 'tensor'), may hold values from -1.1953125 to 1.1953125
- q_prev: float32 [2, 1024, 64], P(None, 'tensor'), may hold values from -6 to 6
Outputs:
- new_errors: bfloat16 [32, 8192, 2, 1024], P('dp', None, None, 'tensor')
- p_factors: bfloat16 [2, 8192, 64], P(None, 'dp')
- q_factors: float32 [2, 1024, 64], P(None, 'tensor')
The draws below stay inside these ranges and needn't reach their ends.
All inputs are finite; a program needn't handle non-finite values.
Results may differ from the reference program's by a relative error of at most 0.001.
Values sent between devices are 32-bit elements; how exact they have to be, the bound alone decides.
No kernel may reach another device: no remote copies, remote signals or barrier semaphores. Data moves between devices by JAX's collectives and lax.ppermute only.
A program may use at most 128 MiB of HBM per device.

```python
import jax
import jax.numpy as jnp
from jax import lax

D = 8192
KVW = 1024
R = 64
REPLICAS = 32


def draw_grads(key, part):
    key = jax.random.fold_in(key, 11)
    keys = jax.random.split(key, 4)
    log_ten = jnp.log(jnp.float32(10.0))
    row_scale = jnp.exp(jax.random.uniform(keys[0], (1, D, 1, 1), jnp.float32) * log_ten)
    rising = 1.0 + 2.0 * jnp.arange(KVW, dtype=jnp.float32) / (KVW - 1)
    col_scale = jnp.exp(jax.random.uniform(keys[1], (1, 1, 2, KVW), jnp.float32) * log_ten) * rising
    shared = jnp.clip(jax.random.normal(keys[2], (1, D, 2, KVW), jnp.float32), -4.0, 4.0)
    own = jnp.clip(jax.random.normal(keys[3], (REPLICAS, D, 2, KVW), jnp.float32), -4.0, 4.0)
    values = 0.02 * row_scale * col_scale * (shared + 0.7 * own)
    return values.astype(jnp.bfloat16)


def shard_levels(rng, extent, pieces, smallest, largest):
    def one(position, blocks):
        draws = jax.random.uniform(jax.random.fold_in(jax.random.fold_in(rng, 6), position), (blocks,), jnp.float32, smallest / len(pieces), largest / len(pieces))
        return jnp.repeat(jnp.exp(draws), extent[position] // blocks).reshape((-1,) + (1,) * (len(extent) - position - 1))

    factor_of = one(*pieces[0])
    for cut in pieces[1:]:
        factor_of = factor_of * one(*cut)
    return factor_of


def centred(key, shape, deviation, bound, shards=(), held_as=jnp.bfloat16):
    drawn = deviation * jax.random.normal(key, shape, jnp.float32)
    if shards:
        drawn = drawn * shard_levels(key, shape, shards, -0.22, 0.18)
    return jnp.clip(drawn, -bound, bound).astype(held_as)


def setup_inputs(seed: int = 0) -> dict:
    key_list = jax.random.split(jax.random.key(seed), 4)
    return {
        "grads": draw_grads(jax.random.fold_in(key_list[3], 71), 0),
        "errors": centred(key_list[1], (REPLICAS, D, 2, KVW), 0.2, 1.1953125, ((0, 32), (3, 8))),
        "q_prev": centred(key_list[2], (2, KVW, R), 1.0, 6.0, ((1, 8),), jnp.float32),
    }


def orthonormal(p_sum):
    columns = []
    for which in range(2):
        block = p_sum[which]
        gram_matrix = jnp.dot(block.T, block, precision=lax.Precision.HIGHEST)
        lower = jnp.linalg.cholesky(gram_matrix)
        columns.append(jax.scipy.linalg.solve_triangular(lower, block.T, lower=True).T)
    return jnp.stack(columns)

def reference(grads, errors, q_prev):

    def add_left(running, replica_pair):
        compensated = replica_pair[0].astype(jnp.float32) + replica_pair[1].astype(jnp.float32)
        return (running + jnp.einsum('dkc,kcr->kdr', compensated, q_prev, precision=lax.Precision.HIGHEST), None)
    p_sum, _ = lax.scan(add_left, jnp.zeros((2, D, R), jnp.float32), (grads, errors))
    p_hat = orthonormal(p_sum)

    def add_right(running, replica_pair):
        compensated = replica_pair[0].astype(jnp.float32) + replica_pair[1].astype(jnp.float32)
        return (running + jnp.einsum('dkc,kdr->kcr', compensated, p_hat, precision=lax.Precision.HIGHEST), None)
    q_sum, _ = lax.scan(add_right, jnp.zeros((2, KVW, R), jnp.float32), (grads, errors))
    q_mean = q_sum / REPLICAS
    norm_value = jnp.sqrt(jnp.sum(q_mean * q_mean))
    clip_limit = 0.5 * jnp.sqrt(jnp.float32(2 * KVW * R))
    clip_scale = jnp.minimum(jnp.float32(1.0), clip_limit / norm_value)
    approx = jnp.einsum('kdr,kcr->dkc', p_hat, q_mean, precision=lax.Precision.HIGHEST)

    def new_one(replica_pair):
        compensated = replica_pair[0].astype(jnp.float32) + replica_pair[1].astype(jnp.float32)
        return (compensated - approx).astype(jnp.bfloat16)
    new_errors = lax.map(new_one, (grads, errors))
    return (new_errors, p_hat.astype(jnp.bfloat16), q_mean * clip_scale)
```

```python
import jax
import jax.numpy as jnp
from jax import lax
from jax.experimental import pallas as pl
from jax.experimental.pallas import tpu as pltpu
from jax.sharding import Mesh
from jax.sharding import PartitionSpec as P

D = 8192
KVW = 1024
R = 64
REPLICAS = 32
F32 = jnp.float32
BF16 = jnp.bfloat16

PLANE = ("x_hi", "y", "x_lo")
COLUMN = ("x_hi", "z")
TENSOR = ("y", "x_lo")

BLOCKS = 16
ROWS = 256
STEP = 4
LIMIT = 16 * 1024 * 1024


def split(value):
    high = value.astype(BF16)
    low = (value - high.astype(F32)).astype(BF16)
    return high, low


def exact_dot(a, b, contract):
    return lax.dot_general(
        a, b, (contract, ((), ())), precision=lax.Precision.HIGHEST, preferred_element_type=F32
    )


def first_projection(shape):
    return lax.broadcasted_iota(jnp.int32, shape, len(shape) - 1) < R


def left_kernel(which, g_ref, e_ref, qt_ref, out_ref, weights, rows):
    @pl.when(pl.program_id(0) == 0)
    def _():
        high, low = split(qt_ref[...])
        weights[...] = jnp.concatenate(
            [jnp.concatenate([high, high], 1), jnp.concatenate([low, low], 1)], 0
        )

    mask = first_projection((ROWS, 2 * R))
    for j in range(STEP):
        x = jnp.concatenate([g_ref[j, 0], e_ref[j, 0]], 1)
        both = lax.dot_general(
            x, weights[...], (((1,), (1,)), ((), ())), preferred_element_type=F32
        )
        rows[j] = both[:, : 2 * R] + both[:, 2 * R :]
        even = rows[j, pl.ds(0, ROWS, stride=2), :]
        odd = rows[j, pl.ds(1, ROWS, stride=2), :]
        out_ref[j] = jnp.where(mask, even, odd)


def left_half(which, g, e, qt):
    spec = pl.BlockSpec((STEP, 1, 2 * ROWS, 128), lambda i, w: (i, w[0], 0, 0))
    return pl.pallas_call(
        left_kernel,
        grid_spec=pltpu.PrefetchScalarGridSpec(
            num_scalar_prefetch=1,
            grid=(BLOCKS // STEP,),
            in_specs=[spec, spec, pl.BlockSpec((2 * R, 128), lambda i, w: (0, 0))],
            out_specs=pl.BlockSpec((STEP, ROWS, 128), lambda i, w: (i, 0, 0)),
            scratch_shapes=[
                pltpu.VMEM((256, 256), BF16),
                pltpu.VMEM((STEP, 2 * ROWS, 128), F32),
            ],
        ),
        out_shape=jax.ShapeDtypeStruct((BLOCKS, ROWS, 128), F32),
        compiler_params=pltpu.CompilerParams(vmem_limit_bytes=LIMIT),
        cost_estimate=pl.CostEstimate(
            flops=2 * 8192 * 256 * 256, bytes_accessed=6 * 2**20, transcendentals=0
        ),
        name="left_half",
    )(which, g, e, qt)


def interleave(p, rows, mask):
    rows[pl.ds(0, ROWS, stride=2), :] = jnp.where(mask, p, 0.0)
    rows[pl.ds(1, ROWS, stride=2), :] = jnp.where(mask, 0.0, p)
    return jnp.concatenate(split(rows[...]), 1)


def quadrants(total):
    n = total.shape[0] // 2
    return total[:n, :n] + total[:n, n:] + total[n:, :n] + total[n:, n:]


def right_kernel(which, p_ref, g_ref, e_ref, *rest):
    if len(rest) == 7:
        q_in, gram_in, q_ref, gram_ref, q_total, gram_total, rows = rest
    else:
        q_ref, gram_ref, q_total, gram_total, rows = rest
    step = pl.program_id(0)

    @pl.when(step == 0)
    def _():
        q_total[...] = jnp.zeros_like(q_total)
        gram_total[...] = jnp.zeros_like(gram_total)

    mask = first_projection((ROWS, 2 * R))
    over_rows = (((0,), (0,)), ((), ()))
    for j in range(STEP):
        p = p_ref[j]
        plain = jnp.concatenate(split(p), 1)
        both = interleave(p, rows.at[j], mask)
        x = jnp.concatenate([g_ref[j, 0], e_ref[j, 0]], 1)
        q_total[...] += lax.dot_general(both, x, over_rows, preferred_element_type=F32)
        gram_total[...] += lax.dot_general(plain, plain, over_rows, preferred_element_type=F32)

    @pl.when(step == pl.num_programs(0) - 1)
    def _():
        q = quadrants(q_total[...])
        gram = quadrants(gram_total[...])
        if len(rest) == 7:
            q += q_in[...]
            gram += gram_in[...]
        q_ref[...] = q
        gram_ref[...] = gram


def right_half(which, p, g, e, *before):
    spec = pl.BlockSpec((STEP, 1, 2 * ROWS, 128), lambda i, w: (i, w[0], 0, 0))
    whole = pl.BlockSpec((128, 128), lambda i, w: (0, 0))
    square = jax.ShapeDtypeStruct((128, 128), F32)
    return pl.pallas_call(
        right_kernel,
        grid_spec=pltpu.PrefetchScalarGridSpec(
            num_scalar_prefetch=1,
            grid=(BLOCKS // STEP,),
            in_specs=[
                pl.BlockSpec((STEP, ROWS, 128), lambda i, w: (i, 0, 0)),
                spec,
                spec,
                *[whole] * len(before),
            ],
            out_specs=[whole, whole],
            scratch_shapes=[
                pltpu.VMEM((256, 256), F32),
                pltpu.VMEM((256, 256), F32),
                pltpu.VMEM((STEP, 2 * ROWS, 128), F32),
            ],
        ),
        out_shape=[square, square],
        compiler_params=pltpu.CompilerParams(vmem_limit_bytes=LIMIT),
        cost_estimate=pl.CostEstimate(
            flops=3 * 8192 * 256 * 256, bytes_accessed=6 * 2**20, transcendentals=0
        ),
        name="right_half",
    )(which, p, g, e, *before)


def factor_kernel(gram_ref, out_ref):
    mask = first_projection((R, 2 * R))
    lane = lax.broadcasted_iota(jnp.int32, (R, 2 * R), 1)
    row = lax.broadcasted_iota(jnp.int32, (R, 2 * R), 0)
    rest = jnp.where(mask, gram_ref[:R, :], gram_ref[R:, :])
    inverse = jnp.where(lane % R == row, 1.0, 0.0).astype(F32)
    pivots = jnp.ones((R, 2 * R), F32)
    for j in range(R):
        column = jnp.where(mask, rest[:, j : j + 1], rest[:, R + j : R + j + 1])
        pivot = column[j : j + 1, :]
        pivots = jnp.where(row == j, pivot, pivots)
        if j < R - 1:
            factor = jnp.where(row > j, column * (1.0 / pivot), 0.0)
            inverse = inverse - factor * inverse[j : j + 1, :]
            rest = rest - factor * rest[j : j + 1, :]
    inverse = inverse * lax.rsqrt(pivots)
    out_ref[:R, :] = jnp.where(mask, inverse, 0.0)
    out_ref[R:, :] = jnp.where(mask, 0.0, inverse)


def inverse_factor(gram):
    return pl.pallas_call(
        factor_kernel,
        out_shape=jax.ShapeDtypeStruct((2 * R, 2 * R), F32),
        cost_estimate=pl.CostEstimate(
            flops=2 * 128 * 128 * 128, bytes_accessed=2**17, transcendentals=0
        ),
        name="inverse_factor",
    )(gram)


def middle_kernel(place, inverse_ref, q_mine, q_other, p_ref, q_ref, w_ref, norm_ref, factors_ref):
    inverse = inverse_ref[...]
    mine, other = q_mine[...], q_other[...]
    low = place[0] == 0
    q_sum = jnp.concatenate([jnp.where(low, mine, other), jnp.where(low, other, mine)], 0)
    q_mean = exact_dot(inverse, q_sum, ((1,), (0,))) * (1.0 / REPLICAS)
    q_ref[...] = q_mean
    w_ref[...] = exact_dot(inverse, q_mean, ((0,), (0,)))
    norm_ref[...] = jnp.full(norm_ref.shape, jnp.sum(q_mean * q_mean), F32)
    factors_ref[...] = exact_dot(inverse, p_ref[0], ((1,), (1,))).astype(BF16)


def middle(place, inverse, q_mine, q_other, p_mine):
    square = pl.BlockSpec((128, 128), lambda i, w: (0, 0))
    half = pl.BlockSpec((R, 128), lambda i, w: (0, 0))
    return pl.pallas_call(
        middle_kernel,
        grid_spec=pltpu.PrefetchScalarGridSpec(
            num_scalar_prefetch=1,
            grid=(1,),
            in_specs=[square, half, half, pl.BlockSpec((1, ROWS, 128), lambda i, w: (w[1], 0, 0))],
            out_specs=[
                square,
                square,
                pl.BlockSpec((8, 128), lambda i, w: (0, 0)),
                pl.BlockSpec((128, ROWS), lambda i, w: (0, 0)),
            ],
        ),
        out_shape=[
            jax.ShapeDtypeStruct((128, 128), F32),
            jax.ShapeDtypeStruct((128, 128), F32),
            jax.ShapeDtypeStruct((8, 128), F32),
            jax.ShapeDtypeStruct((128, ROWS), BF16),
        ],
        cost_estimate=pl.CostEstimate(
            flops=2 * 128 * 128 * 512, bytes_accessed=2**19, transcendentals=0
        ),
        name="middle",
    )(place, inverse, q_mine, q_other, p_mine)


def error_kernel(which, mine, other, g_ref, e_ref, w_ref, out_ref, weights, rows):
    half = pl.program_id(0)

    @pl.when((half == 0) & (pl.program_id(1) == 0))
    def _():
        high, low = split(w_ref[...])
        line = jnp.concatenate([high, low], 1)
        weights[...] = jnp.concatenate([line, line], 0)

    mask = first_projection((ROWS, 2 * R))

    def subtract(p_ref):
        for j in range(STEP):
            both = interleave(p_ref[j], rows.at[j], mask)
            approx = jnp.dot(both, weights[...], preferred_element_type=F32)
            compensated = g_ref[j, 0].astype(F32) + e_ref[j, 0].astype(F32)
            out_ref[j, 0] = (compensated - (approx[:, :128] + approx[:, 128:])).astype(BF16)

    @pl.when(half == 0)
    def _():
        subtract(mine)

    @pl.when(half == 1)
    def _():
        subtract(other)


def errors_out(which, mine, other, g, e, w):
    last = BLOCKS // STEP - 1
    spec = pl.BlockSpec((STEP, 1, 2 * ROWS, 128), lambda h, i, c: (i, c[h], 0, 0))
    return pl.pallas_call(
        error_kernel,
        grid_spec=pltpu.PrefetchScalarGridSpec(
            num_scalar_prefetch=1,
            grid=(2, BLOCKS // STEP),
            in_specs=[
                pl.BlockSpec((STEP, ROWS, 128), lambda h, i, c: (jnp.where(h == 0, i, last), 0, 0)),
                pl.BlockSpec((STEP, ROWS, 128), lambda h, i, c: (jnp.where(h == 0, 0, i), 0, 0)),
                spec,
                spec,
                pl.BlockSpec((128, 128), lambda h, i, c: (0, 0)),
            ],
            out_specs=spec,
            scratch_shapes=[
                pltpu.VMEM((256, 256), BF16),
                pltpu.VMEM((STEP, 2 * ROWS, 128), F32),
            ],
        ),
        out_shape=jax.ShapeDtypeStruct((BLOCKS, 2, 2 * ROWS, 128), BF16),
        compiler_params=pltpu.CompilerParams(vmem_limit_bytes=LIMIT),
        cost_estimate=pl.CostEstimate(
            flops=2 * 16384 * 256 * 256, bytes_accessed=16 * 2**20, transcendentals=0
        ),
        name="new_errors",
    )(which, mine, other, g, e, w)


def to_each(block, count):
    return jnp.broadcast_to(block[None], (count, *block.shape))


def swap(value):
    return lax.ppermute(value, "core", [(0, 1), (1, 0)])


def per_device(grads, errors, q_prev):
    g = grads.reshape(BLOCKS, 2, 2 * ROWS, 128)
    e = errors.reshape(BLOCKS, 2, 2 * ROWS, 128)
    qt = q_prev.transpose(0, 2, 1).reshape(2 * R, 128)
    core = lax.axis_index("core").astype(jnp.int32)
    mine, other = core[None], (1 - core)[None]

    sent = swap(left_half(other, g, e, qt))
    part = left_half(mine, g, e, qt) + sent
    part = jnp.sum(lax.all_to_all(part, PLANE, 0, 0, tiled=True), 0)
    part = part.reshape(8, 32, 128)
    part = jnp.sum(lax.all_to_all(part, "z", 0, 0, tiled=True), 0)
    part = lax.all_to_all(to_each(part, 8), "z", 0, 0, tiled=True).reshape(ROWS, 128)
    p_mine = lax.all_to_all(to_each(part, BLOCKS), PLANE, 0, 0, tiled=True)
    p_other = swap(p_mine)

    q_part, gram_part = right_half(mine, p_mine, g, e)
    q_part, gram = right_half(other, p_other, g, e, q_part, gram_part)
    inverse = inverse_factor(gram)

    q_part = q_part.reshape(2, R, 128)
    q_sent = swap(lax.dynamic_index_in_dim(q_part, 1 - core, 0, keepdims=False))
    q_half = lax.dynamic_index_in_dim(q_part, core, 0, keepdims=False) + q_sent
    q_half = lax.all_to_all(q_half.reshape(16, 4, 128), COLUMN, 0, 0, tiled=True)
    q_half = to_each(jnp.sum(q_half, 0), 16)
    q_mine = lax.all_to_all(q_half, COLUMN, 0, 0, tiled=True).reshape(R, 128)
    q_other = swap(q_mine)

    block = lax.axis_index(COLUMN).astype(jnp.int32)
    q_mean, w, norm_part, p_factors = middle(
        jnp.stack([core, block]), inverse, q_mine, q_other, p_mine
    )
    norm_parts = lax.all_to_all(norm_part.reshape(8, 1, 128), TENSOR, 0, 0, tiled=True)
    new_errors = errors_out(jnp.stack([core, 1 - core]), p_mine, p_other, g, e, w)
    norm_square = jnp.sum(norm_parts, 0)
    clip_limit = 0.5 * jnp.sqrt(F32(2 * KVW * R))
    clip_scale = jnp.minimum(F32(1.0), clip_limit / jnp.sqrt(norm_square))
    q_factors = q_mean * clip_scale
    return (
        new_errors.reshape(1, D, 2, 128),
        p_factors.reshape(2, R, ROWS).transpose(0, 2, 1),
        q_factors.reshape(2, R, 128).transpose(0, 2, 1),
    )


def solution(mesh):
    axes = ("x_hi", "z", "core", "y", "x_lo")
    named = Mesh(mesh.devices.reshape(2, 8, 2, 4, 2), axes)
    replica = ("x_hi", "z", "core")
    in_specs = (
        P(replica, None, None, TENSOR),
        P(replica, None, None, TENSOR),
        P(None, TENSOR, None),
    )
    out_specs = (P(replica, None, None, TENSOR), P(None, replica, None), P(None, TENSOR, None))
    return jax.shard_map(
        per_device, mesh=named, in_specs=in_specs, out_specs=out_specs, check_vma=False
    )
```

```python
import functools

import jax
import jax.numpy as jnp
from jax import lax
from jax.experimental import pallas as pl
from jax.experimental.pallas import tpu as pltpu
from jax.sharding import Mesh
from jax.sharding import PartitionSpec as P

D = 8192
KVW = 1024
R = 64
REPLICAS = 32
F32 = jnp.float32
BF16 = jnp.bfloat16

PLANE = ("x_hi", "y", "x_lo")
COLUMN = ("x_hi", "z")
REPLICA = ("x_hi", "z", "core")
TENSOR = ("y", "x_lo")

BLOCKS = 16
ROWS = 256
STEP = 4
PANEL = 8
LIMIT = 16 * 1024 * 1024


def in_hbm(value):
    return pltpu.with_memory_space_constraint(value, pltpu.HBM)


def split(value):
    high = value.astype(BF16)
    low = (value - high.astype(F32)).astype(BF16)
    return high, low


def split_dot(a, b, a_dim, b_dim):
    line = jnp.concatenate(split(b), 1 - b_dim)
    both = lax.dot_general(
        jnp.concatenate(split(a), a_dim),
        jnp.concatenate([line, line], b_dim),
        (((a_dim,), (b_dim,)), ((), ())),
        preferred_element_type=F32,
    )
    n = both.shape[1] // 2
    return both[:, :n] + both[:, n:]


def first_projection(shape):
    return lax.broadcasted_iota(jnp.int32, shape, len(shape) - 1) < R


VMEM = pl.BlockSpec(memory_space=pltpu.VMEM)
SMEM = pl.BlockSpec(memory_space=pltpu.SMEM)
ANY = pl.BlockSpec(memory_space=pl.ANY)
HALF_P = (BLOCKS, ROWS, 128)
HALF_X = (BLOCKS, 2 * ROWS, 128)


def in_vmem(value):
    return pltpu.with_memory_space_constraint(value, pltpu.VMEM)


def left_kernel(half, g_hbm, e_hbm, qt_ref, p_ref, g_ref, e_ref, weights, rows, arrived):
    copies = []
    for c in range(BLOCKS // STEP):
        blocks = pl.ds(c * STEP, STEP)
        pair = (
            pltpu.make_async_copy(g_hbm.at[blocks, half[0]], g_ref.at[blocks], arrived.at[0, c]),
            pltpu.make_async_copy(e_hbm.at[blocks, half[0]], e_ref.at[blocks], arrived.at[1, c]),
        )
        for copy in pair:
            copy.start()
        copies.append(pair)
    high, low = split(qt_ref[...])
    weights[...] = jnp.concatenate(
        [jnp.concatenate([high, high], 1), jnp.concatenate([low, low], 1)], 0
    )
    mask = first_projection((ROWS, 2 * R))
    for c, pair in enumerate(copies):
        for copy in pair:
            copy.wait()
        for j in range(STEP):
            block = c * STEP + j
            x = jnp.concatenate([g_ref[block], e_ref[block]], 1)
            both = lax.dot_general(
                x, weights[...], (((1,), (1,)), ((), ())), preferred_element_type=F32
            )
            rows[j] = both[:, : 2 * R] + both[:, 2 * R :]
            even = rows[j, pl.ds(0, ROWS, stride=2), :]
            odd = rows[j, pl.ds(1, ROWS, stride=2), :]
            p_ref[block] = jnp.where(mask, even, odd)


def left_half(half, g, e, qt):
    return pl.pallas_call(
        left_kernel,
        in_specs=[SMEM, ANY, ANY, VMEM],
        out_specs=[VMEM, VMEM, VMEM],
        out_shape=[
            pltpu.VMEM(HALF_P, F32),
            pltpu.VMEM(HALF_X, BF16),
            pltpu.VMEM(HALF_X, BF16),
        ],
        scratch_shapes=[
            pltpu.VMEM((256, 256), BF16),
            pltpu.VMEM((STEP, 2 * ROWS, 128), F32),
            pltpu.SemaphoreType.DMA((2, BLOCKS // STEP)),
        ],
        compiler_params=pltpu.CompilerParams(vmem_limit_bytes=LIMIT),
        cost_estimate=pl.CostEstimate(
            flops=2 * 8192 * 256 * 256, bytes_accessed=8 * 2**20, transcendentals=0
        ),
        name="left_half",
    )(half, in_hbm(g), in_hbm(e), qt)


def interleave(p, rows, mask):
    rows[pl.ds(0, ROWS, stride=2), :] = jnp.where(mask, p, 0.0)
    rows[pl.ds(1, ROWS, stride=2), :] = jnp.where(mask, 0.0, p)
    return jnp.concatenate(split(rows[...]), 1)


def quadrants(total):
    n = total.shape[0] // 2
    return total[:n, :n] + total[:n, n:] + total[n:, :n] + total[n:, n:]


def add_rows(total, a, b):
    total[...] += lax.dot_general(
        a, b, (((0,), (0,)), ((), ())), preferred_element_type=F32
    )


def right_kernel(with_gram, p_ref, g_ref, e_ref, *rest):
    if with_gram:
        q_ref, gram_ref, q_total, gram_total, rows, sides = rest
        gram_total[...] = jnp.zeros_like(gram_total)
    else:
        q_in, q_ref, q_total, rows, sides = rest
    q_total[...] = jnp.zeros_like(q_total)
    mask = first_projection((ROWS, 2 * R))

    @pl.loop(0, BLOCKS // STEP)
    def _(c):
        for j in range(STEP):
            p = p_ref[c * STEP + j]
            sides[j] = interleave(p, rows.at[j], mask)
            if with_gram:
                plain = jnp.concatenate(split(p), 1)
                add_rows(gram_total, plain, plain)
        blocks = pl.ds(c * STEP, STEP)
        depth = STEP * 2 * ROWS
        x = jnp.concatenate(
            [g_ref[blocks].reshape(depth, 128), e_ref[blocks].reshape(depth, 128)], 1
        )
        add_rows(q_total, sides[...].reshape(depth, 256), x)

    q = quadrants(q_total[...])
    if with_gram:
        gram_ref[...] = quadrants(gram_total[...])
        q_ref[...] = q
    else:
        q_ref[...] = q + q_in[...]


def right_half(p, g, e, before=None):
    square = jax.ShapeDtypeStruct((128, 128), F32)
    with_gram = before is None
    totals = [pltpu.VMEM((256, 256), F32)] * (2 if with_gram else 1)
    return pl.pallas_call(
        functools.partial(right_kernel, with_gram),
        in_specs=[VMEM] * (3 if with_gram else 4),
        out_specs=[VMEM, VMEM] if with_gram else VMEM,
        out_shape=[square, square] if with_gram else square,
        scratch_shapes=[
            *totals,
            pltpu.VMEM((STEP, 2 * ROWS, 128), F32),
            pltpu.VMEM((STEP, 2 * ROWS, 256), BF16),
        ],
        compiler_params=pltpu.CompilerParams(vmem_limit_bytes=LIMIT),
        cost_estimate=pl.CostEstimate(
            flops=3 * 8192 * 256 * 256, bytes_accessed=6 * 2**20, transcendentals=0
        ),
        name="right_half",
    )(in_vmem(p), in_vmem(g), in_vmem(e), *([] if with_gram else [before]))


def factor_kernel(mine_ref, other_ref, out_ref):
    mask = first_projection((R, 2 * R))
    lane = lax.broadcasted_iota(jnp.int32, (R, 2 * R), 1)
    row = lax.broadcasted_iota(jnp.int32, (R, 2 * R), 0)
    gram = mine_ref[...] + other_ref[...]
    rest = jnp.where(mask, gram[:R], gram[R:])
    inverse = jnp.where(lane % R == row, 1.0, 0.0).astype(F32)
    pivots = jnp.ones((R, 2 * R), F32)
    for start in range(0, R, PANEL):
        panel = [
            jnp.where(mask, rest[:, j : j + 1], rest[:, R + j : R + j + 1])
            for j in range(start, start + PANEL)
        ]
        for i in range(PANEL):
            j = start + i
            pivot = panel[i][j : j + 1, :]
            pivots = jnp.where(row == j, pivot, pivots)
            factor = jnp.where(row > j, panel[i] * (1.0 / pivot), 0.0)
            for m in range(i + 1, PANEL):
                panel[m] = panel[m] - factor * panel[m][j : j + 1, :]
            inverse = inverse - factor * inverse[j : j + 1, :]
            rest = rest - factor * rest[j : j + 1, :]
    inverse = inverse * lax.rsqrt(pivots)
    out_ref[:R, :] = jnp.where(mask, inverse, 0.0)
    out_ref[R:, :] = jnp.where(mask, 0.0, inverse)


def inverse_factor(gram, gram_other):
    return pl.pallas_call(
        factor_kernel,
        out_shape=jax.ShapeDtypeStruct((2 * R, 2 * R), F32),
        cost_estimate=pl.CostEstimate(
            flops=2 * 128 * 128 * 128, bytes_accessed=2**17, transcendentals=0
        ),
        name="inverse_factor",
    )(gram, gram_other)


def middle_kernel(place, inverse_ref, q_sum, p_ref, q_ref, w_ref, norm_ref, factors_ref):
    inverse = inverse_ref[...]
    q_mean = split_dot(inverse, q_sum[...], 1, 0) * (1.0 / REPLICAS)
    q_ref[...] = q_mean
    w_ref[...] = split_dot(inverse, q_mean, 0, 0)
    norm_ref[...] = jnp.full(norm_ref.shape, jnp.sum(q_mean * q_mean), F32)
    factors_ref[...] = split_dot(inverse, p_ref[place[0]], 1, 1).astype(BF16)


def middle(place, inverse, q_sum, p_mine):
    return pl.pallas_call(
        middle_kernel,
        in_specs=[SMEM, VMEM, VMEM, VMEM],
        out_specs=[VMEM] * 4,
        out_shape=[
            jax.ShapeDtypeStruct((128, 128), F32),
            jax.ShapeDtypeStruct((128, 128), F32),
            jax.ShapeDtypeStruct((8, 128), F32),
            jax.ShapeDtypeStruct((128, ROWS), BF16),
        ],
        cost_estimate=pl.CostEstimate(
            flops=2 * 128 * 128 * 512, bytes_accessed=2**19, transcendentals=0
        ),
        name="middle",
    )(place, inverse, q_sum, in_vmem(p_mine))


def error_kernel(core, w_ref, *rest):
    halves, (out_hbm, weights, rows, staged, sent) = (rest[:3], rest[3:6]), rest[6:]
    high, low = split(w_ref[...])
    line = jnp.concatenate([high, low], 1)
    weights[...] = jnp.concatenate([line, line], 0)
    mask = first_projection((ROWS, 2 * R))
    copies = []
    for h, (p_ref, g_ref, e_ref) in enumerate(halves):
        place = core[0] if h == 0 else 1 - core[0]
        for c in range(BLOCKS // STEP):
            for j in range(STEP):
                block = c * STEP + j
                both = interleave(p_ref[block], rows.at[j], mask)
                approx = jnp.dot(both, weights[...], preferred_element_type=F32)
                compensated = g_ref[block].astype(F32) + e_ref[block].astype(F32)
                left = compensated - (approx[:, :128] + approx[:, 128:])
                staged[h, block] = left.astype(BF16)
            blocks = pl.ds(c * STEP, STEP)
            copies.append(
                pltpu.make_async_copy(
                    staged.at[h, blocks], out_hbm.at[blocks, place], sent.at[h, c]
                )
            )
            copies[-1].start()
    for copy in copies:
        copy.wait()


def errors_out(core, w, mine, other):
    return pl.pallas_call(
        error_kernel,
        in_specs=[SMEM] + [VMEM] * 7,
        out_specs=ANY,
        out_shape=jax.ShapeDtypeStruct((BLOCKS, 2, 2 * ROWS, 128), BF16),
        scratch_shapes=[
            pltpu.VMEM((256, 256), BF16),
            pltpu.VMEM((STEP, 2 * ROWS, 128), F32),
            pltpu.VMEM((2, *HALF_X), BF16),
            pltpu.SemaphoreType.DMA((2, BLOCKS // STEP)),
        ],
        compiler_params=pltpu.CompilerParams(vmem_limit_bytes=LIMIT),
        cost_estimate=pl.CostEstimate(
            flops=2 * 16384 * 256 * 256, bytes_accessed=16 * 2**20, transcendentals=0
        ),
        name="new_errors",
    )(core, w, *[in_vmem(a) for a in (*mine, *other)])


def to_each(block, count):
    return jnp.broadcast_to(block[None], (count, *block.shape))


def swap(value):
    return lax.ppermute(value, "core", [(0, 1), (1, 0)])


def per_device(grads, errors, q_prev):
    g = grads.reshape(BLOCKS, 2, 2 * ROWS, 128)
    e = errors.reshape(BLOCKS, 2, 2 * ROWS, 128)
    qt = q_prev.transpose(0, 2, 1).reshape(2 * R, 128)
    core = lax.axis_index("core").astype(jnp.int32)
    mine, other = core[None], (1 - core)[None]

    part_other, g_other, e_other = left_half(other, g, e, qt)
    sent = swap(part_other)
    part, g_mine, e_mine = left_half(mine, g, e, qt)
    part = jnp.sum(lax.all_to_all(part + sent, PLANE, 0, 0, tiled=True), 0)
    part = part.reshape(8, 32, 128)
    part = jnp.sum(lax.all_to_all(part, "z", 0, 0, tiled=True), 0)
    part = lax.all_to_all(to_each(part, 8), "z", 0, 0, tiled=True).reshape(ROWS, 128)
    p_mine = lax.all_to_all(to_each(part, BLOCKS), PLANE, 0, 0, tiled=True)
    p_other = swap(p_mine)

    q_part, gram = right_half(p_mine, g_mine, e_mine)
    gram_other = swap(gram)
    q_part = right_half(p_other, g_other, e_other, q_part)
    inverse = inverse_factor(gram, gram_other)

    q_part = lax.all_to_all(q_part.reshape(REPLICAS, 4, 128), REPLICA, 0, 0, tiled=True)
    q_part = to_each(jnp.sum(q_part, 0), REPLICAS)
    q_sum = lax.all_to_all(q_part, REPLICA, 0, 0, tiled=True).reshape(2 * R, 128)

    block = lax.axis_index(COLUMN).astype(jnp.int32)[None]
    q_mean, w, norm_part, p_factors = middle(block, inverse, q_sum, p_mine)
    norm_parts = lax.all_to_all(norm_part.reshape(8, 1, 128), TENSOR, 0, 0, tiled=True)
    new_errors = errors_out(mine, w, (p_mine, g_mine, e_mine), (p_other, g_other, e_other))
    norm_square = jnp.sum(norm_parts, 0)
    clip_limit = 0.5 * jnp.sqrt(F32(2 * KVW * R))
    clip_scale = jnp.minimum(F32(1.0), clip_limit / jnp.sqrt(norm_square))
    q_factors = q_mean * clip_scale
    return (
        new_errors.reshape(1, D, 2, 128),
        p_factors.reshape(2, R, ROWS).transpose(0, 2, 1),
        q_factors.reshape(2, R, 128).transpose(0, 2, 1),
    )


def solution(mesh):
    axes = ("x_hi", "z", "core", "y", "x_lo")
    named = Mesh(mesh.devices.reshape(2, 8, 2, 4, 2), axes)
    in_specs = (
        P(REPLICA, None, None, TENSOR),
        P(REPLICA, None, None, TENSOR),
        P(None, TENSOR, None),
    )
    out_specs = (P(REPLICA, None, None, TENSOR), P(None, REPLICA, None), P(None, TENSOR, None))
    return jax.shard_map(
        per_device, mesh=named, in_specs=in_specs, out_specs=out_specs, check_vma=False
    )
```

```python
import functools

import jax
import jax.numpy as jnp
from jax import lax
from jax.experimental import pallas as pl
from jax.experimental.pallas import tpu as pltpu
from jax.sharding import Mesh
from jax.sharding import PartitionSpec as P

D = 8192
KVW = 1024
R = 64
REPLICAS = 32
F32 = jnp.float32
BF16 = jnp.bfloat16

AXES = ("x_hi", "z", "core", "y", "x_lo")
COLUMN = ("x_hi", "z")
REPLICA = ("x_hi", "z", "core")
TENSOR = ("y", "x_lo")

BLOCKS = 16
ROWS = 256
STEP = 4
PANEL = 8
LIMIT = 16 * 1024 * 1024


def chip_groups():
    def device(x, z, core, y):
        return (((x // 2 * 8 + z) * 2 + core) * 4 + y) * 2 + x % 2

    def line(core, along, across, z):
        x, y = (along, across) if core == 0 else (across, along)
        return device(x, z, core, y)

    near, far = [], []
    for core in range(2):
        pairs = [((2 * k + core) % 8, (2 * k + core + 1) % 8) for k in range(4)]
        for across in range(4):
            for pair in pairs:
                near.append([line(core, i, across, z) for z in pair for i in range(4)])
            for which in range(2):
                far.append([line(core, across, i, p[which]) for p in pairs for i in range(4)])
    return near, far


NEAR, FAR = chip_groups()


def exchange(pieces, groups):
    return lax.all_to_all(pieces, AXES, 0, 0, axis_index_groups=groups, tiled=True)


def in_hbm(value):
    return pltpu.with_memory_space_constraint(value, pltpu.HBM)


def split(value):
    high = value.astype(BF16)
    low = (value - high.astype(F32)).astype(BF16)
    return high, low


def split_dot(a, b, a_dim, b_dim):
    line = jnp.concatenate(split(b), 1 - b_dim)
    both = lax.dot_general(
        jnp.concatenate(split(a), a_dim),
        jnp.concatenate([line, line], b_dim),
        (((a_dim,), (b_dim,)), ((), ())),
        preferred_element_type=F32,
    )
    n = both.shape[1] // 2
    return both[:, :n] + both[:, n:]


def first_projection(shape):
    return lax.broadcasted_iota(jnp.int32, shape, len(shape) - 1) < R


VMEM = pl.BlockSpec(memory_space=pltpu.VMEM)
SMEM = pl.BlockSpec(memory_space=pltpu.SMEM)
ANY = pl.BlockSpec(memory_space=pl.ANY)
HALF_P = (BLOCKS, ROWS, 128)
HALF_X = (BLOCKS, 2 * ROWS, 128)


def in_vmem(value):
    return pltpu.with_memory_space_constraint(value, pltpu.VMEM)


def left_kernel(which, place, g_hbm, e_hbm, qt_hbm, p_ref, g_ref, e_ref, qt, weights, rows, arrived, qt_arrived):
    half = place[which]
    copies = []
    qt_copy = pltpu.make_async_copy(qt_hbm, qt, qt_arrived)
    qt_copy.start()
    for c in range(BLOCKS // STEP):
        blocks = pl.ds(c * STEP, STEP)
        pair = (
            pltpu.make_async_copy(g_hbm.at[blocks, half], g_ref.at[blocks], arrived.at[0, c]),
            pltpu.make_async_copy(e_hbm.at[blocks, half], e_ref.at[blocks], arrived.at[1, c]),
        )
        for copy in pair:
            copy.start()
        copies.append(pair)
    qt_copy.wait()
    high, low = split(qt[...])
    weights[...] = jnp.concatenate(
        [jnp.concatenate([high, high], 1), jnp.concatenate([low, low], 1)], 0
    )
    mask = first_projection((ROWS, 2 * R))
    for c, pair in enumerate(copies):
        for copy in pair:
            copy.wait()
        for j in range(STEP):
            block = c * STEP + j
            x = jnp.concatenate([g_ref[block], e_ref[block]], 1)
            both = lax.dot_general(
                x, weights[...], (((1,), (1,)), ((), ())), preferred_element_type=F32
            )
            rows[j] = both[:, : 2 * R] + both[:, 2 * R :]
            even = rows[j, pl.ds(0, ROWS, stride=2), :]
            odd = rows[j, pl.ds(1, ROWS, stride=2), :]
            p_ref[block] = jnp.where(mask, even, odd)


def left_half(which, place, g, e, qt):
    return pl.pallas_call(
        functools.partial(left_kernel, which),
        in_specs=[SMEM, ANY, ANY, ANY],
        out_specs=[VMEM, VMEM, VMEM],
        out_shape=[
            pltpu.VMEM(HALF_P, F32),
            pltpu.VMEM(HALF_X, BF16),
            pltpu.VMEM(HALF_X, BF16),
        ],
        scratch_shapes=[
            pltpu.VMEM((2 * R, 128), F32),
            pltpu.VMEM((256, 256), BF16),
            pltpu.VMEM((STEP, 2 * ROWS, 128), F32),
            pltpu.SemaphoreType.DMA((2, BLOCKS // STEP)),
            pltpu.SemaphoreType.DMA,
        ],
        compiler_params=pltpu.CompilerParams(vmem_limit_bytes=LIMIT),
        cost_estimate=pl.CostEstimate(
            flops=2 * 8192 * 256 * 256, bytes_accessed=8 * 2**20, transcendentals=0
        ),
        name="left_half",
    )(place, in_hbm(g), in_hbm(e), in_hbm(qt))


def interleave(p, rows, mask):
    rows[pl.ds(0, ROWS, stride=2), :] = jnp.where(mask, p, 0.0)
    rows[pl.ds(1, ROWS, stride=2), :] = jnp.where(mask, 0.0, p)
    return jnp.concatenate(split(rows[...]), 1)


def quadrants(total):
    n = total.shape[0] // 2
    return total[:n, :n] + total[:n, n:] + total[n:, :n] + total[n:, n:]


def add_rows(total, a, b):
    total[...] += lax.dot_general(
        a, b, (((0,), (0,)), ((), ())), preferred_element_type=F32
    )


def right_step(c, p_ref, g_ref, e_ref, q_total, rows, sides, mask):
    for j in range(STEP):
        sides[j] = interleave(p_ref[c * STEP + j], rows.at[j], mask)
    blocks = pl.ds(c * STEP, STEP)
    depth = STEP * 2 * ROWS
    x = jnp.concatenate(
        [g_ref[blocks].reshape(depth, 128), e_ref[blocks].reshape(depth, 128)], 1
    )
    add_rows(q_total, sides[...].reshape(depth, 256), x)


RIGHT_SCRATCH = [
    pltpu.VMEM((256, 256), F32),
    pltpu.VMEM((STEP, 2 * ROWS, 128), F32),
    pltpu.VMEM((STEP, 2 * ROWS, 256), BF16),
]


def right_kernel(p_ref, g_ref, e_ref, q_ref, gram_ref, gram_total, q_total, rows, sides):
    q_total[...] = jnp.zeros_like(q_total)
    gram_total[...] = jnp.zeros_like(gram_total)
    mask = first_projection((ROWS, 2 * R))

    @pl.loop(0, BLOCKS // STEP)
    def _(c):
        right_step(c, p_ref, g_ref, e_ref, q_total, rows, sides, mask)
        for j in range(STEP):
            plain = jnp.concatenate(split(p_ref[c * STEP + j]), 1)
            add_rows(gram_total, plain, plain)

    q_ref[...] = quadrants(q_total[...])
    gram_ref[...] = quadrants(gram_total[...])


def right_half(p, g, e):
    square = jax.ShapeDtypeStruct((128, 128), F32)
    return pl.pallas_call(
        right_kernel,
        in_specs=[VMEM] * 3,
        out_specs=[VMEM] * 2,
        out_shape=[square, square],
        scratch_shapes=[pltpu.VMEM((256, 256), F32), *RIGHT_SCRATCH],
        compiler_params=pltpu.CompilerParams(vmem_limit_bytes=LIMIT),
        cost_estimate=pl.CostEstimate(
            flops=3 * 8192 * 256 * 256, bytes_accessed=6 * 2**20, transcendentals=0
        ),
        name="right_half",
    )(in_vmem(p), in_vmem(g), in_vmem(e))


def inverse_of_factor(gram):
    mask = first_projection((R, 2 * R))
    lane = lax.broadcasted_iota(jnp.int32, (R, 2 * R), 1)
    row = lax.broadcasted_iota(jnp.int32, (R, 2 * R), 0)
    rest = jnp.where(mask, gram[:R], gram[R:])
    inverse = jnp.where(lane % R == row, 1.0, 0.0).astype(F32)
    pivots = jnp.ones((R, 2 * R), F32)
    for start in range(0, R, PANEL):
        panel = [
            jnp.where(mask, rest[:, j : j + 1], rest[:, R + j : R + j + 1])
            for j in range(start, start + PANEL)
        ]
        for i in range(PANEL):
            j = start + i
            pivot = panel[i][j : j + 1, :]
            pivots = jnp.where(row == j, pivot, pivots)
            factor = jnp.where(row > j, panel[i] * (1.0 / pivot), 0.0)
            for m in range(i + 1, PANEL):
                panel[m] = panel[m] - factor * panel[m][j : j + 1, :]
            inverse = inverse - factor * inverse[j : j + 1, :]
            rest = rest - factor * rest[j : j + 1, :]
    return inverse * lax.rsqrt(pivots)


def solve_kernel(place, p_ref, g_ref, e_ref, mine_ref, q_in, gram_in, gram_other, inverse_ref, q_ref, factors_ref, q_total, rows, sides):
    q_total[...] = jnp.zeros_like(q_total)
    mask = first_projection((ROWS, 2 * R))
    for c in range(BLOCKS // STEP):
        right_step(c, p_ref, g_ref, e_ref, q_total, rows, sides, mask)
    solved = inverse_of_factor(gram_in[...] + gram_other[...])
    side = first_projection((R, 2 * R))
    inverse = jnp.concatenate([jnp.where(side, solved, 0.0), jnp.where(side, 0.0, solved)], 0)
    inverse_ref[...] = inverse
    factors_ref[...] = split_dot(inverse, mine_ref[place[2]], 1, 1).astype(BF16)
    q_ref[...] = split_dot(inverse, quadrants(q_total[...]) + q_in[...], 1, 0)


def solve(place, p, g, e, p_mine, q, gram, gram_other):
    square = jax.ShapeDtypeStruct((128, 128), F32)
    return pl.pallas_call(
        solve_kernel,
        in_specs=[SMEM] + [VMEM] * 7,
        out_specs=[VMEM] * 3,
        out_shape=[square, square, jax.ShapeDtypeStruct((128, ROWS), BF16)],
        scratch_shapes=RIGHT_SCRATCH,
        compiler_params=pltpu.CompilerParams(vmem_limit_bytes=LIMIT),
        cost_estimate=pl.CostEstimate(
            flops=3 * 8192 * 256 * 256, bytes_accessed=6 * 2**20, transcendentals=0
        ),
        name="solve",
    )(place, in_vmem(p), in_vmem(g), in_vmem(e), in_vmem(p_mine), q, gram, gram_other)


def error_kernel(place, inverse_ref, q_sum, *rest):
    halves, (out_hbm, q_ref, norm_ref, weights, rows, staged, sent) = (
        (rest[:3], rest[3:6]),
        rest[6:],
    )
    q_mean = q_sum[...] * (1.0 / REPLICAS)
    q_ref[...] = q_mean
    norm_ref[...] = jnp.full(norm_ref.shape, jnp.sum(q_mean * q_mean), F32)
    high, low = split(split_dot(inverse_ref[...], q_mean, 0, 0))
    line = jnp.concatenate([high, low], 1)
    weights[...] = jnp.concatenate([line, line], 0)
    mask = first_projection((ROWS, 2 * R))
    copies = []
    for h, (p_ref, g_ref, e_ref) in enumerate(halves):
        for c in range(BLOCKS // STEP):
            for j in range(STEP):
                block = c * STEP + j
                both = interleave(p_ref[block], rows.at[j], mask)
                approx = jnp.dot(both, weights[...], preferred_element_type=F32)
                compensated = g_ref[block].astype(F32) + e_ref[block].astype(F32)
                left = compensated - (approx[:, :128] + approx[:, 128:])
                staged[h, block] = left.astype(BF16)
            blocks = pl.ds(c * STEP, STEP)
            copies.append(
                pltpu.make_async_copy(
                    staged.at[h, blocks], out_hbm.at[blocks, place[1 - h]], sent.at[h, c]
                )
            )
            copies[-1].start()
    for copy in copies:
        copy.wait()


def errors_out(place, inverse, q_sum, mine, other):
    return pl.pallas_call(
        error_kernel,
        in_specs=[SMEM] + [VMEM] * 8,
        out_specs=[ANY, VMEM, VMEM],
        out_shape=[
            jax.ShapeDtypeStruct((BLOCKS, 2, 2 * ROWS, 128), BF16),
            jax.ShapeDtypeStruct((128, 128), F32),
            jax.ShapeDtypeStruct((8, 128), F32),
        ],
        scratch_shapes=[
            pltpu.VMEM((256, 256), BF16),
            pltpu.VMEM((STEP, 2 * ROWS, 128), F32),
            pltpu.VMEM((2, *HALF_X), BF16),
            pltpu.SemaphoreType.DMA((2, BLOCKS // STEP)),
        ],
        compiler_params=pltpu.CompilerParams(vmem_limit_bytes=LIMIT),
        cost_estimate=pl.CostEstimate(
            flops=2 * 16384 * 256 * 256, bytes_accessed=16 * 2**20, transcendentals=0
        ),
        name="new_errors",
    )(place, inverse, q_sum, *[in_vmem(a) for a in (*mine, *other)])


def sum_kernel(pieces, out_ref):
    total = pieces[0]
    for i in range(1, pieces.shape[0]):
        total = total + pieces[i]
    if len(out_ref.shape) == 2:
        out_ref[...] = total
    else:
        for i in range(out_ref.shape[0]):
            out_ref[i] = total


def sum_pieces(pieces, copies=None):
    shape = pieces.shape[1:] if copies is None else (copies, *pieces.shape[1:])
    return pl.pallas_call(
        sum_kernel,
        in_specs=[VMEM],
        out_specs=VMEM,
        out_shape=jax.ShapeDtypeStruct(shape, F32),
        compiler_params=pltpu.CompilerParams(vmem_limit_bytes=LIMIT),
        name="sum_pieces",
    )(pieces)


def clip_kernel(norm_parts, q_mean, out_ref):
    norm_square = jnp.sum(norm_parts[...], 0, keepdims=True)
    clip_limit = 0.5 * (2 * KVW * R) ** 0.5
    out_ref[...] = q_mean[...] * jnp.minimum(1.0, clip_limit / jnp.sqrt(norm_square))


def clip(norm_parts, q_mean):
    return pl.pallas_call(
        clip_kernel,
        in_specs=[VMEM, VMEM],
        out_specs=VMEM,
        out_shape=jax.ShapeDtypeStruct((128, 128), F32),
        compiler_params=pltpu.CompilerParams(vmem_limit_bytes=LIMIT),
        name="clip",
    )(norm_parts, q_mean)


def to_each(block, count):
    return jnp.broadcast_to(block[None], (count, *block.shape))


def swap(value):
    return lax.ppermute(value, "core", [(0, 1), (1, 0)])


def per_device(grads, errors, q_prev):
    g = grads.reshape(BLOCKS, 2, 2 * ROWS, 128)
    e = errors.reshape(BLOCKS, 2, 2 * ROWS, 128)
    qt = q_prev.transpose(0, 2, 1).reshape(2 * R, 128)
    core = lax.axis_index("core").astype(jnp.int32)
    column = lax.axis_index(COLUMN).astype(jnp.int32)
    place = jnp.stack([1 - core, core, column])

    part_other, g_other, e_other = left_half(0, place, g, e, qt)
    sent = swap(part_other)
    part, g_mine, e_mine = left_half(1, place, g, e, qt)
    part = exchange((part + sent).reshape(8, 512, 128), NEAR)
    part = sum_pieces(part).reshape(16, 32, 128)
    part = sum_pieces(exchange(part, FAR), 16)
    part = exchange(part, FAR).reshape(512, 128)
    p_mine = exchange(to_each(part, 8), NEAR).reshape(HALF_P)
    p_other = swap(p_mine)

    q_part, gram = right_half(p_mine, g_mine, e_mine)
    gram_other = swap(gram)
    inverse, q_part, p_factors = solve(
        place, p_other, g_other, e_other, p_mine, q_part, gram, gram_other
    )
    q_part = q_part.reshape(REPLICAS, 4, 128)
    q_part = sum_pieces(lax.all_to_all(q_part, REPLICA, 0, 0, tiled=True), REPLICAS)
    q_sum = lax.all_to_all(q_part, REPLICA, 0, 0, tiled=True).reshape(2 * R, 128)

    new_errors, q_mean, norm_part = errors_out(
        place, inverse, q_sum, (p_mine, g_mine, e_mine), (p_other, g_other, e_other)
    )
    norm_parts = lax.all_to_all(norm_part.reshape(8, 1, 128), TENSOR, 0, 0, tiled=True)
    q_factors = clip(norm_parts.reshape(8, 128), q_mean)
    return (
        new_errors.reshape(1, D, 2, 128),
        p_factors.reshape(2, R, ROWS).transpose(0, 2, 1),
        q_factors.reshape(2, R, 128).transpose(0, 2, 1),
    )


def solution(mesh):
    named = Mesh(mesh.devices.reshape(2, 8, 2, 4, 2), AXES)
    in_specs = (
        P(REPLICA, None, None, TENSOR),
        P(REPLICA, None, None, TENSOR),
        P(None, TENSOR, None),
    )
    out_specs = (P(REPLICA, None, None, TENSOR), P(None, REPLICA, None), P(None, TENSOR, None))
    return jax.shard_map(
        per_device, mesh=named, in_specs=in_specs, out_specs=out_specs, check_vma=False
    )
```

```python
import functools

import jax
import jax.numpy as jnp
from jax import lax
from jax.experimental import pallas as pl
from jax.experimental.pallas import tpu as pltpu
from jax.sharding import Mesh
from jax.sharding import PartitionSpec as P

D = 8192
KVW = 1024
R = 64
REPLICAS = 32
F32 = jnp.float32
BF16 = jnp.bfloat16

AXES = ("x_hi", "z", "core", "y", "x_lo")
REPLICA = ("x_hi", "z", "core")
TENSOR = ("y", "x_lo")

BLOCKS = 16
ROWS = 256
LOAD = 2
STEP = 4
PANEL = 8
LIMIT = 16 * 1024 * 1024


def chip_groups():
    def device(x, z, core, y):
        return (((x // 2 * 8 + z) * 2 + core) * 4 + y) * 2 + x % 2

    def line(core, along, across, z):
        x, y = (along, across) if core == 0 else (across, along)
        return device(x, z, core, y)

    near, far = [], []
    for core in range(2):
        pairs = [((2 * k + core) % 8, (2 * k + core + 1) % 8) for k in range(4)]
        for across in range(4):
            for pair in pairs:
                near.append([line(core, i, across, z) for z in pair for i in range(4)])
            for which in range(2):
                far.append([line(core, across, i, p[which]) for p in pairs for i in range(4)])
    return near, far


NEAR, FAR = chip_groups()


def exchange(pieces, groups):
    return lax.all_to_all(pieces, AXES, 0, 0, axis_index_groups=groups, tiled=True)


def in_hbm(value):
    return pltpu.with_memory_space_constraint(value, pltpu.HBM)


def split(value):
    high = value.astype(BF16)
    low = (value - high.astype(F32)).astype(BF16)
    return high, low


def split_dot(a, b, a_dim, b_dim):
    line = jnp.concatenate(split(b), 1 - b_dim)
    both = lax.dot_general(
        jnp.concatenate(split(a), a_dim),
        jnp.concatenate([line, line], b_dim),
        (((a_dim,), (b_dim,)), ((), ())),
        preferred_element_type=F32,
    )
    n = both.shape[1] // 2
    return both[:, :n] + both[:, n:]


def first_projection(shape):
    return lax.broadcasted_iota(jnp.int32, shape, len(shape) - 1) < R


VMEM = pl.BlockSpec(memory_space=pltpu.VMEM)
ANY = pl.BlockSpec(memory_space=pl.ANY)
HALF_P = (BLOCKS, ROWS, 128)
HALF_X = (BLOCKS, 2 * ROWS, 128)
HALF_S = (BLOCKS, 2 * ROWS, 256)


def in_vmem(value):
    return pltpu.with_memory_space_constraint(value, pltpu.VMEM)


def left_kernel(mine, g_hbm, e_hbm, qt_hbm, p_ref, g_ref, e_ref, qt, weights, rows, arrived, qt_arrived):
    core = lax.axis_index("core")
    half = core if mine else 1 - core
    qt_copy = pltpu.make_async_copy(qt_hbm, qt, qt_arrived)
    qt_copy.start()
    copies = []
    for c in range(BLOCKS // LOAD):
        blocks = pl.ds(c * LOAD, LOAD)
        pair = (
            pltpu.make_async_copy(g_hbm.at[half, blocks], g_ref.at[blocks], arrived.at[0, c]),
            pltpu.make_async_copy(e_hbm.at[half, blocks], e_ref.at[blocks], arrived.at[1, c]),
        )
        for copy in pair:
            copy.start()
        copies.append(pair)
    qt_copy.wait()
    high, low = split(qt[...])
    weights[...] = jnp.concatenate(
        [jnp.concatenate([high, high], 1), jnp.concatenate([low, low], 1)], 0
    )
    mask = first_projection((ROWS, 2 * R))
    for c, pair in enumerate(copies):
        for copy in pair:
            copy.wait()
        for block in range(c * LOAD, (c + 1) * LOAD):
            x = jnp.concatenate([g_ref[block], e_ref[block]], 1)
            both = lax.dot_general(
                x, weights[...], (((1,), (1,)), ((), ())), preferred_element_type=F32
            )
            slot = rows.at[block % STEP]
            slot[...] = both[:, : 2 * R] + both[:, 2 * R :]
            even = slot[pl.ds(0, ROWS, stride=2), :]
            odd = slot[pl.ds(1, ROWS, stride=2), :]
            p_ref[block] = jnp.where(mask, even, odd)


def left_half(mine, g, e, qt):
    return pl.pallas_call(
        functools.partial(left_kernel, mine),
        in_specs=[ANY, ANY, ANY],
        out_specs=[VMEM, VMEM, VMEM],
        out_shape=[
            pltpu.VMEM(HALF_P, F32),
            pltpu.VMEM(HALF_X, BF16),
            pltpu.VMEM(HALF_X, BF16),
        ],
        scratch_shapes=[
            pltpu.VMEM((2 * R, 128), F32),
            pltpu.VMEM((256, 256), BF16),
            pltpu.VMEM((STEP, 2 * ROWS, 128), F32),
            pltpu.SemaphoreType.DMA((2, BLOCKS // LOAD)),
            pltpu.SemaphoreType.DMA,
        ],
        compiler_params=pltpu.CompilerParams(vmem_limit_bytes=LIMIT),
        cost_estimate=pl.CostEstimate(
            flops=2 * 8192 * 256 * 256, bytes_accessed=8 * 2**20, transcendentals=0
        ),
        name="left_half",
    )(in_hbm(g), in_hbm(e), in_hbm(qt))


def interleave(p, rows, mask):
    rows[pl.ds(0, ROWS, stride=2), :] = jnp.where(mask, p, 0.0)
    rows[pl.ds(1, ROWS, stride=2), :] = jnp.where(mask, 0.0, p)
    return jnp.concatenate(split(rows[...]), 1)


def quadrants(total):
    n = total.shape[0] // 2
    return total[:n, :n] + total[:n, n:] + total[n:, :n] + total[n:, n:]


def add_rows(total, a, b):
    total[...] += lax.dot_general(
        a, b, (((0,), (0,)), ((), ())), preferred_element_type=F32
    )


def right_step(c, p_ref, g_ref, e_ref, sides, q_total, rows, mask, other=()):
    for j in range(STEP):
        sides[c * STEP + j] = interleave(p_ref[c * STEP + j], rows.at[j], mask)
        next(other, None)
    blocks = pl.ds(c * STEP, STEP)
    depth = STEP * 2 * ROWS
    x = jnp.concatenate(
        [g_ref[blocks].reshape(depth, 128), e_ref[blocks].reshape(depth, 128)], 1
    )
    add_rows(q_total, sides[blocks].reshape(depth, 256), x)


RIGHT_SCRATCH = [pltpu.VMEM((256, 256), F32), pltpu.VMEM((STEP, 2 * ROWS, 128), F32)]


def right_kernel(p_ref, g_ref, e_ref, q_ref, gram_ref, sides, gram_total, q_total, rows):
    q_total[...] = jnp.zeros_like(q_total)
    gram_total[...] = jnp.zeros_like(gram_total)
    mask = first_projection((ROWS, 2 * R))
    for c in range(BLOCKS // STEP):
        right_step(c, p_ref, g_ref, e_ref, sides, q_total, rows, mask, iter(()))
        for j in range(STEP):
            plain = jnp.concatenate(split(p_ref[c * STEP + j]), 1)
            add_rows(gram_total, plain, plain)

    q_ref[...] = quadrants(q_total[...])
    gram_ref[...] = quadrants(gram_total[...])


def right_half(p, g, e):
    square = jax.ShapeDtypeStruct((128, 128), F32)
    return pl.pallas_call(
        right_kernel,
        in_specs=[VMEM] * 3,
        out_specs=[VMEM] * 3,
        out_shape=[square, square, pltpu.VMEM(HALF_S, BF16)],
        scratch_shapes=[pltpu.VMEM((256, 256), F32), *RIGHT_SCRATCH],
        compiler_params=pltpu.CompilerParams(vmem_limit_bytes=LIMIT),
        cost_estimate=pl.CostEstimate(
            flops=3 * 8192 * 256 * 256, bytes_accessed=6 * 2**20, transcendentals=0
        ),
        name="right_half",
    )(in_vmem(p), in_vmem(g), in_vmem(e))


def inverse_of_factor(gram, found):
    mask = first_projection((R, 2 * R))
    lane = lax.broadcasted_iota(jnp.int32, (R, 2 * R), 1)
    row = lax.broadcasted_iota(jnp.int32, (R, 2 * R), 0)
    rest = jnp.where(mask, gram[:R], gram[R:])
    inverse = jnp.where(lane % R == row, 1.0, 0.0).astype(F32)
    pivots = jnp.ones((R, 2 * R), F32)
    for start in range(0, R, PANEL):
        panel = [
            jnp.where(mask, rest[:, j : j + 1], rest[:, R + j : R + j + 1])
            for j in range(start, start + PANEL)
        ]
        for i in range(PANEL):
            j = start + i
            pivot = panel[i][j : j + 1, :]
            pivots = jnp.where(row == j, pivot, pivots)
            factor = jnp.where(row > j, panel[i] * (1.0 / pivot), 0.0)
            for m in range(i + 1, PANEL):
                panel[m] = panel[m] - factor * panel[m][j : j + 1, :]
            inverse = inverse - factor * inverse[j : j + 1, :]
            rest = rest - factor * rest[j : j + 1, :]
            if i % 4 == 3:
                yield
    found.append(inverse * lax.rsqrt(pivots))
    yield


def solve_kernel(p_ref, g_ref, e_ref, mine_ref, q_in, gram_in, gram_other, inverse_ref, q_ref, factors_ref, sides, q_total, rows):
    q_total[...] = jnp.zeros_like(q_total)
    mask = first_projection((ROWS, 2 * R))
    found = []
    solving = inverse_of_factor(gram_in[...] + gram_other[...], found)
    for c in range(BLOCKS // STEP):
        right_step(c, p_ref, g_ref, e_ref, sides, q_total, rows, mask, solving)
    for _ in solving:
        pass
    side = first_projection((R, 2 * R))
    inverse = jnp.concatenate([jnp.where(side, found[0], 0.0), jnp.where(side, 0.0, found[0])], 0)
    inverse_ref[...] = inverse
    q_ref[...] = split_dot(inverse, quadrants(q_total[...]) + q_in[...], 1, 0)
    core = lax.axis_index("core")
    block = lax.axis_index("z") * 2 + core
    p = jnp.where(lax.axis_index("x_hi") == core, mine_ref[block], p_ref[block])
    factors_ref[...] = split_dot(inverse, p, 1, 1).astype(BF16)


def solve(p, g, e, p_mine, q, gram, gram_other):
    square = jax.ShapeDtypeStruct((128, 128), F32)
    return pl.pallas_call(
        solve_kernel,
        in_specs=[VMEM] * 7,
        out_specs=[VMEM] * 4,
        out_shape=[
            square,
            square,
            jax.ShapeDtypeStruct((128, ROWS), BF16),
            pltpu.VMEM(HALF_S, BF16),
        ],
        scratch_shapes=RIGHT_SCRATCH,
        compiler_params=pltpu.CompilerParams(vmem_limit_bytes=LIMIT),
        cost_estimate=pl.CostEstimate(
            flops=3 * 8192 * 256 * 256, bytes_accessed=6 * 2**20, transcendentals=0
        ),
        name="solve",
    )(in_vmem(p), in_vmem(g), in_vmem(e), in_vmem(p_mine), q, gram, gram_other)


def error_kernel(inverse_ref, q_sum, *rest):
    halves, (out_hbm, q_ref, norm_ref, weights, staged, sent) = (rest[:3], rest[3:6]), rest[6:]
    core = lax.axis_index("core")
    q_mean = q_sum[...] * (1.0 / REPLICAS)
    q_ref[...] = q_mean
    norm_ref[...] = jnp.full(norm_ref.shape, jnp.sum(q_mean * q_mean), F32)
    high, low = split(split_dot(inverse_ref[...], q_mean, 0, 0))
    line = jnp.concatenate([high, low], 1)
    weights[...] = jnp.concatenate([line, line], 0)
    copies = []
    for h, (sides, g_ref, e_ref) in enumerate(halves):
        for c in range(BLOCKS // STEP):
            for block in range(c * STEP, (c + 1) * STEP):
                approx = jnp.dot(sides[block], weights[...], preferred_element_type=F32)
                compensated = g_ref[block].astype(F32) + e_ref[block].astype(F32)
                left = compensated - (approx[:, :128] + approx[:, 128:])
                staged[h, block] = left.astype(BF16)
            blocks = pl.ds(c * STEP, STEP)
            place = core if h == 0 else 1 - core
            copies.append(
                pltpu.make_async_copy(
                    staged.at[h, blocks], out_hbm.at[place, blocks], sent.at[h, c]
                )
            )
            copies[-1].start()
    for copy in copies:
        copy.wait()


def errors_out(inverse, q_sum, mine, other):
    return pl.pallas_call(
        error_kernel,
        in_specs=[VMEM] * 8,
        out_specs=[ANY, VMEM, VMEM],
        out_shape=[
            jax.ShapeDtypeStruct((2, BLOCKS, 2 * ROWS, 128), BF16),
            jax.ShapeDtypeStruct((128, 128), F32),
            jax.ShapeDtypeStruct((8, 128), F32),
        ],
        scratch_shapes=[
            pltpu.VMEM((256, 256), BF16),
            pltpu.VMEM((2, *HALF_X), BF16),
            pltpu.SemaphoreType.DMA((2, BLOCKS // STEP)),
        ],
        compiler_params=pltpu.CompilerParams(vmem_limit_bytes=LIMIT),
        cost_estimate=pl.CostEstimate(
            flops=2 * 16384 * 256 * 256, bytes_accessed=16 * 2**20, transcendentals=0
        ),
        name="new_errors",
    )(inverse, q_sum, *[in_vmem(a) for a in (*mine, *other)])


def sum_kernel(pieces, out_ref):
    total = pieces[0]
    for i in range(1, pieces.shape[0]):
        total = total + pieces[i]
    if len(out_ref.shape) == 2:
        out_ref[...] = total
    else:
        for i in range(out_ref.shape[0]):
            out_ref[i] = total


def sum_pieces(pieces, copies=None):
    shape = pieces.shape[1:] if copies is None else (copies, *pieces.shape[1:])
    return pl.pallas_call(
        sum_kernel,
        in_specs=[VMEM],
        out_specs=VMEM,
        out_shape=jax.ShapeDtypeStruct(shape, F32),
        compiler_params=pltpu.CompilerParams(vmem_limit_bytes=LIMIT),
        name="sum_pieces",
    )(pieces)


def clip_kernel(norm_parts, q_mean, out_ref):
    norm_square = jnp.sum(norm_parts[...], 0, keepdims=True)
    clip_limit = 0.5 * (2 * KVW * R) ** 0.5
    out_ref[...] = q_mean[...] * jnp.minimum(1.0, clip_limit / jnp.sqrt(norm_square))


def clip(norm_parts, q_mean):
    return pl.pallas_call(
        clip_kernel,
        in_specs=[VMEM, VMEM],
        out_specs=VMEM,
        out_shape=jax.ShapeDtypeStruct((128, 128), F32),
        compiler_params=pltpu.CompilerParams(vmem_limit_bytes=LIMIT),
        name="clip",
    )(norm_parts, q_mean)


def to_each(block, count):
    return jnp.broadcast_to(block[None], (count, *block.shape))


def swap(value):
    return lax.ppermute(value, "core", [(0, 1), (1, 0)])


def per_device(grads, errors, q_prev):
    g = grads.reshape(2, BLOCKS, 2 * ROWS, 128)
    e = errors.reshape(2, BLOCKS, 2 * ROWS, 128)
    qt = q_prev.transpose(0, 2, 1).reshape(2 * R, 128)

    part_other, g_other, e_other = left_half(False, g, e, qt)
    sent = swap(part_other)
    part, g_mine, e_mine = left_half(True, g, e, qt)
    part = exchange((part + sent).reshape(8, 512, 128), NEAR)
    part = sum_pieces(part).reshape(16, 32, 128)
    part = sum_pieces(exchange(part, FAR), 16)
    part = exchange(part, FAR).reshape(512, 128)
    p_mine = exchange(to_each(part, 8), NEAR).reshape(HALF_P)
    p_other = swap(p_mine)

    q_part, gram, sides_mine = right_half(p_mine, g_mine, e_mine)
    gram_other = swap(gram)
    inverse, q_part, p_factors, sides_other = solve(
        p_other, g_other, e_other, p_mine, q_part, gram, gram_other
    )
    q_part = q_part.reshape(REPLICAS, 4, 128)
    q_part = sum_pieces(lax.all_to_all(q_part, REPLICA, 0, 0, tiled=True), REPLICAS)
    q_sum = lax.all_to_all(q_part, REPLICA, 0, 0, tiled=True).reshape(2 * R, 128)

    new_errors, q_mean, norm_part = errors_out(
        inverse, q_sum, (sides_mine, g_mine, e_mine), (sides_other, g_other, e_other)
    )
    norm_parts = lax.all_to_all(norm_part.reshape(8, 1, 128), TENSOR, 0, 0, tiled=True)
    q_factors = clip(norm_parts.reshape(8, 128), q_mean)
    return (
        new_errors.reshape(1, D, 2, 128),
        p_factors.reshape(2, R, ROWS).transpose(0, 2, 1),
        q_factors.reshape(2, R, 128).transpose(0, 2, 1),
    )


def solution(mesh):
    named = Mesh(mesh.devices.reshape(2, 8, 2, 4, 2), AXES)
    in_specs = (
        P(REPLICA, None, None, TENSOR),
        P(REPLICA, None, None, TENSOR),
        P(None, TENSOR, None),
    )
    out_specs = (P(REPLICA, None, None, TENSOR), P(None, REPLICA, None), P(None, TENSOR, None))
    return jax.shard_map(
        per_device, mesh=named, in_specs=in_specs, out_specs=out_specs, check_vma=False
    )
```

```python
import functools

import jax
import jax.numpy as jnp
from jax import lax
from jax.experimental import pallas as pl
from jax.experimental.pallas import tpu as pltpu
from jax.sharding import Mesh
from jax.sharding import PartitionSpec as P

D = 8192
KVW = 1024
R = 64
REPLICAS = 32
F32 = jnp.float32
BF16 = jnp.bfloat16

AXES = ("x_hi", "z", "core", "y", "x_lo")
REPLICA = ("x_hi", "z", "core")
TENSOR = ("y", "x_lo")

BLOCKS = 16
ROWS = 256
LOAD = 4
AHEAD = 2
DEPTH = 4
STEP = 4
PANEL = 8
LIMIT = 16 * 1024 * 1024


def chip_groups():
    def device(x, z, core, y):
        return (((x // 2 * 8 + z) * 2 + core) * 4 + y) * 2 + x % 2

    def line(core, along, across, z):
        x, y = (along, across) if core == 0 else (across, along)
        return device(x, z, core, y)

    near, far = [], []
    for core in range(2):
        pairs = [((2 * k + core) % 8, (2 * k + core + 1) % 8) for k in range(4)]
        for across in range(4):
            for pair in pairs:
                near.append([line(core, i, across, z) for z in pair for i in range(4)])
            for which in range(2):
                far.append([line(core, across, i, p[which]) for p in pairs for i in range(4)])
    return near, far


NEAR, FAR = chip_groups()


def exchange(pieces, groups):
    return lax.all_to_all(pieces, AXES, 0, 0, axis_index_groups=groups, tiled=True)


def in_hbm(value):
    return pltpu.with_memory_space_constraint(value, pltpu.HBM)


def split(value):
    high = value.astype(BF16)
    low = (value - high.astype(F32)).astype(BF16)
    return high, low


def split_dot(a, b, a_dim, b_dim):
    line = jnp.concatenate(split(b), 1 - b_dim)
    both = lax.dot_general(
        jnp.concatenate(split(a), a_dim),
        jnp.concatenate([line, line], b_dim),
        (((a_dim,), (b_dim,)), ((), ())),
        preferred_element_type=F32,
    )
    n = both.shape[1] // 2
    return both[:, :n] + both[:, n:]


def first_projection(shape):
    return lax.broadcasted_iota(jnp.int32, shape, len(shape) - 1) < R


VMEM = pl.BlockSpec(memory_space=pltpu.VMEM)
ANY = pl.BlockSpec(memory_space=pl.ANY)
HALF_P = (BLOCKS, ROWS, 128)
HALF_X = (BLOCKS, 2 * ROWS, 128)
HALF_S = (BLOCKS, 2 * ROWS, 256)


def in_vmem(value):
    return pltpu.with_memory_space_constraint(value, pltpu.VMEM)


def left_kernel(mine, g_hbm, e_hbm, qt_hbm, p_ref, g_ref, e_ref, qt, weights, rows, arrived, qt_arrived):
    core = lax.axis_index("core")
    half = core if mine else 1 - core
    qt_copy = pltpu.make_async_copy(qt_hbm, qt, qt_arrived)
    qt_copy.start()
    copies = []
    for c in range(BLOCKS // LOAD):
        blocks = pl.ds(c * LOAD, LOAD)
        pair = (
            pltpu.make_async_copy(g_hbm.at[half, blocks], g_ref.at[blocks], arrived.at[0, c]),
            pltpu.make_async_copy(e_hbm.at[half, blocks], e_ref.at[blocks], arrived.at[1, c]),
        )
        copies.append(pair)
    for pair in copies[:AHEAD]:
        for copy in pair:
            copy.start()
    qt_copy.wait()
    high, low = split(qt[...])
    weights[...] = jnp.concatenate(
        [jnp.concatenate([high, high], 1), jnp.concatenate([low, low], 1)], 0
    )
    mask = first_projection((ROWS, 2 * R))
    for c, pair in enumerate(copies):
        for copy in pair:
            copy.wait()
        for copy in copies[c + AHEAD] if c + AHEAD < len(copies) else ():
            copy.start()
        for block in range(c * LOAD, (c + 1) * LOAD):
            x = jnp.concatenate([g_ref[block], e_ref[block]], 1)
            both = lax.dot_general(
                x, weights[...], (((1,), (1,)), ((), ())), preferred_element_type=F32
            )
            slot = rows.at[block % STEP]
            slot[...] = both[:, : 2 * R] + both[:, 2 * R :]
            even = slot[pl.ds(0, ROWS, stride=2), :]
            odd = slot[pl.ds(1, ROWS, stride=2), :]
            p_ref[block] = jnp.where(mask, even, odd)


def left_half(mine, g, e, qt):
    return pl.pallas_call(
        functools.partial(left_kernel, mine),
        in_specs=[ANY, ANY, ANY],
        out_specs=[VMEM, VMEM, VMEM],
        out_shape=[
            pltpu.VMEM(HALF_P, F32),
            pltpu.VMEM(HALF_X, BF16),
            pltpu.VMEM(HALF_X, BF16),
        ],
        scratch_shapes=[
            pltpu.VMEM((2 * R, 128), F32),
            pltpu.VMEM((256, 256), BF16),
            pltpu.VMEM((STEP, 2 * ROWS, 128), F32),
            pltpu.SemaphoreType.DMA((2, BLOCKS // LOAD)),
            pltpu.SemaphoreType.DMA,
        ],
        compiler_params=pltpu.CompilerParams(vmem_limit_bytes=LIMIT),
        cost_estimate=pl.CostEstimate(
            flops=2 * 8192 * 256 * 256, bytes_accessed=8 * 2**20, transcendentals=0
        ),
        name="left_half",
    )(in_hbm(g), in_hbm(e), in_hbm(qt))


def interleave(p, rows, mask):
    rows[pl.ds(0, ROWS, stride=2), :] = jnp.where(mask, p, 0.0)
    rows[pl.ds(1, ROWS, stride=2), :] = jnp.where(mask, 0.0, p)
    return jnp.concatenate(split(rows[...]), 1)


def quadrants(total):
    n = total.shape[0] // 2
    return total[:n, :n] + total[:n, n:] + total[n:, :n] + total[n:, n:]


def add_rows(total, a, b):
    total[...] += lax.dot_general(
        a, b, (((0,), (0,)), ((), ())), preferred_element_type=F32
    )


def right_step(c, p_ref, g_ref, e_ref, sides, q_total, rows, mask, other=()):
    for j in range(STEP):
        sides[c * STEP + j] = interleave(p_ref[c * STEP + j], rows.at[j], mask)
        next(other, None)
        if (j + 1) % DEPTH == 0:
            blocks = pl.ds(c * STEP + j + 1 - DEPTH, DEPTH)
            depth = DEPTH * 2 * ROWS
            x = jnp.concatenate(
                [g_ref[blocks].reshape(depth, 128), e_ref[blocks].reshape(depth, 128)], 1
            )
            add_rows(q_total, sides[blocks].reshape(depth, 256), x)


RIGHT_SCRATCH = [pltpu.VMEM((256, 256), F32), pltpu.VMEM((STEP, 2 * ROWS, 128), F32)]


def right_kernel(p_ref, g_ref, e_ref, q_ref, gram_ref, sides, gram_total, q_total, rows):
    q_total[...] = jnp.zeros_like(q_total)
    gram_total[...] = jnp.zeros_like(gram_total)
    mask = first_projection((ROWS, 2 * R))
    for c in range(BLOCKS // STEP):
        right_step(c, p_ref, g_ref, e_ref, sides, q_total, rows, mask, iter(()))
        for j in range(STEP):
            plain = jnp.concatenate(split(p_ref[c * STEP + j]), 1)
            add_rows(gram_total, plain, plain)

    q_ref[...] = quadrants(q_total[...])
    gram_ref[...] = quadrants(gram_total[...])


def right_half(p, g, e):
    square = jax.ShapeDtypeStruct((128, 128), F32)
    return pl.pallas_call(
        right_kernel,
        in_specs=[VMEM] * 3,
        out_specs=[VMEM] * 3,
        out_shape=[square, square, pltpu.VMEM(HALF_S, BF16)],
        scratch_shapes=[pltpu.VMEM((256, 256), F32), *RIGHT_SCRATCH],
        compiler_params=pltpu.CompilerParams(vmem_limit_bytes=LIMIT),
        cost_estimate=pl.CostEstimate(
            flops=3 * 8192 * 256 * 256, bytes_accessed=6 * 2**20, transcendentals=0
        ),
        name="right_half",
    )(in_vmem(p), in_vmem(g), in_vmem(e))


def reciprocal(x):
    return 1.0 / x


def inverse_of_factor(gram, found):
    mask = first_projection((R, 2 * R))
    lane = lax.broadcasted_iota(jnp.int32, (R, 2 * R), 1)
    row = lax.broadcasted_iota(jnp.int32, (R, 2 * R), 0)
    rest = jnp.where(mask, gram[:R], gram[R:])
    inverse = jnp.where(lane % R == row, 1.0, 0.0).astype(F32)
    pivots = jnp.ones((R, 2 * R), F32)
    for start in range(0, R, PANEL):
        panel = [
            jnp.where(mask, rest[:, j : j + 1], rest[:, R + j : R + j + 1])
            for j in range(start, start + PANEL)
        ]
        for i in range(0, PANEL, 2):
            j = start + i
            first, second = panel[i], panel[i + 1]
            a, b, c = first[j : j + 1], first[j + 1 : j + 2], second[j + 1 : j + 2]
            a_inverse = reciprocal(a)
            determinant = a * c - b * b
            pivots = jnp.where(row == j, a, pivots)
            pivots = jnp.where(row == j + 1, determinant * a_inverse, pivots)
            ratio = b * a_inverse
            one = jnp.where(row > j, first * a_inverse, 0.0)
            two = (second - one * b) * (a * reciprocal(determinant))
            two = jnp.where(row > j + 1, two, 0.0)

            def eliminate(matrix):
                upper = matrix[j : j + 1]
                lower = matrix[j + 1 : j + 2] - ratio * upper
                return matrix - one * upper - two * lower

            for m in range(i + 2, PANEL):
                panel[m] = eliminate(panel[m])
            inverse = eliminate(inverse)
            rest = eliminate(rest)
            if i % 4 == 2:
                yield
    found.append(inverse * lax.rsqrt(pivots))
    yield


def by_core(first, second):
    low = lax.axis_index("core") == 0
    return jnp.where(low, first, second), jnp.where(low, second, first)


def solve_kernel(p_ref, g_ref, e_ref, mine_ref, q_in, gram_in, gram_other, inverse_ref, keep_ref, send_ref, factors_ref, sides, q_total, rows):
    q_total[...] = jnp.zeros_like(q_total)
    mask = first_projection((ROWS, 2 * R))
    found = []
    solving = inverse_of_factor(gram_in[...] + gram_other[...], found)
    for c in range(BLOCKS // STEP):
        right_step(c, p_ref, g_ref, e_ref, sides, q_total, rows, mask, solving)
    for _ in solving:
        pass
    side = first_projection((R, 2 * R))
    inverse = jnp.concatenate([jnp.where(side, found[0], 0.0), jnp.where(side, 0.0, found[0])], 0)
    inverse_ref[...] = inverse
    q = split_dot(inverse, quadrants(q_total[...]) + q_in[...], 1, 0)
    keep_ref[...], send_ref[...] = by_core(q[:R], q[R:])
    core = lax.axis_index("core")
    block = lax.axis_index("z") * 2 + core
    p = jnp.where(lax.axis_index("x_hi") == core, mine_ref[block], p_ref[block])
    factors_ref[...] = split_dot(inverse, p, 1, 1).astype(BF16)


def solve(p, g, e, p_mine, q, gram, gram_other):
    return pl.pallas_call(
        solve_kernel,
        in_specs=[VMEM] * 7,
        out_specs=[VMEM] * 5,
        out_shape=[
            jax.ShapeDtypeStruct((128, 128), F32),
            jax.ShapeDtypeStruct((R, 128), F32),
            jax.ShapeDtypeStruct((R, 128), F32),
            jax.ShapeDtypeStruct((128, ROWS), BF16),
            pltpu.VMEM(HALF_S, BF16),
        ],
        scratch_shapes=RIGHT_SCRATCH,
        compiler_params=pltpu.CompilerParams(vmem_limit_bytes=LIMIT),
        cost_estimate=pl.CostEstimate(
            flops=3 * 8192 * 256 * 256, bytes_accessed=6 * 2**20, transcendentals=0
        ),
        name="solve",
    )(in_vmem(p), in_vmem(g), in_vmem(e), in_vmem(p_mine), q, gram, gram_other)


def error_kernel(inverse_ref, q_mine, q_other, *rest):
    halves, (out_hbm, q_ref, norm_ref, weights, staged, sent) = (rest[:3], rest[3:6]), rest[6:]
    core = lax.axis_index("core")
    q_mean = jnp.concatenate(by_core(q_mine[...], q_other[...]), 0) * (1.0 / REPLICAS)
    q_ref[...] = q_mean
    norm_ref[...] = jnp.full(norm_ref.shape, jnp.sum(q_mean * q_mean), F32)
    high, low = split(split_dot(inverse_ref[...], q_mean, 0, 0))
    line = jnp.concatenate([high, low], 1)
    weights[...] = jnp.concatenate([line, line], 0)
    copies = []
    for h, (sides, g_ref, e_ref) in enumerate(halves):
        for c in range(BLOCKS // STEP):
            for block in range(c * STEP, (c + 1) * STEP):
                approx = jnp.dot(sides[block], weights[...], preferred_element_type=F32)
                compensated = g_ref[block].astype(F32) + e_ref[block].astype(F32)
                left = compensated - (approx[:, :128] + approx[:, 128:])
                staged[h, block] = left.astype(BF16)
            blocks = pl.ds(c * STEP, STEP)
            place = core if h == 0 else 1 - core
            copies.append(
                pltpu.make_async_copy(
                    staged.at[h, blocks], out_hbm.at[place, blocks], sent.at[h, c]
                )
            )
            copies[-1].start()
    for copy in copies:
        copy.wait()


def errors_out(inverse, q_mine, q_other, mine, other):
    return pl.pallas_call(
        error_kernel,
        in_specs=[VMEM] * 9,
        out_specs=[ANY, VMEM, VMEM],
        out_shape=[
            jax.ShapeDtypeStruct((2, BLOCKS, 2 * ROWS, 128), BF16),
            jax.ShapeDtypeStruct((128, 128), F32),
            jax.ShapeDtypeStruct((8, 128), F32),
        ],
        scratch_shapes=[
            pltpu.VMEM((256, 256), BF16),
            pltpu.VMEM((2, *HALF_X), BF16),
            pltpu.SemaphoreType.DMA((2, BLOCKS // STEP)),
        ],
        compiler_params=pltpu.CompilerParams(vmem_limit_bytes=LIMIT),
        cost_estimate=pl.CostEstimate(
            flops=2 * 16384 * 256 * 256, bytes_accessed=16 * 2**20, transcendentals=0
        ),
        name="new_errors",
    )(inverse, q_mine, q_other, *[in_vmem(a) for a in (*mine, *other)])


def sum_kernel(pieces, out_ref):
    total = pieces[0]
    for i in range(1, pieces.shape[0]):
        total = total + pieces[i]
    if len(out_ref.shape) == 2:
        out_ref[...] = total
    else:
        for i in range(out_ref.shape[0]):
            out_ref[i] = total


def sum_pieces(pieces, copies=None):
    shape = pieces.shape[1:] if copies is None else (copies, *pieces.shape[1:])
    return pl.pallas_call(
        sum_kernel,
        in_specs=[VMEM],
        out_specs=VMEM,
        out_shape=jax.ShapeDtypeStruct(shape, F32),
        compiler_params=pltpu.CompilerParams(vmem_limit_bytes=LIMIT),
        name="sum_pieces",
    )(pieces)


def add_kernel(a_ref, b_ref, out_ref):
    total = a_ref[...] + b_ref[...]
    for i in range(out_ref.shape[0]):
        out_ref[i] = total


def add_for_each(a, b, copies):
    return pl.pallas_call(
        add_kernel,
        in_specs=[VMEM, VMEM],
        out_specs=VMEM,
        out_shape=jax.ShapeDtypeStruct((copies, *a.shape), F32),
        compiler_params=pltpu.CompilerParams(vmem_limit_bytes=LIMIT),
        name="add_for_each",
    )(a, b)


def clip_kernel(norm_parts, q_mean, out_ref):
    norm_square = jnp.sum(norm_parts[...], 0, keepdims=True)
    clip_limit = 0.5 * (2 * KVW * R) ** 0.5
    out_ref[...] = q_mean[...] * jnp.minimum(1.0, clip_limit / jnp.sqrt(norm_square))


def clip(norm_parts, q_mean):
    return pl.pallas_call(
        clip_kernel,
        in_specs=[VMEM, VMEM],
        out_specs=VMEM,
        out_shape=jax.ShapeDtypeStruct((128, 128), F32),
        compiler_params=pltpu.CompilerParams(vmem_limit_bytes=LIMIT),
        name="clip",
    )(norm_parts, q_mean)


def to_each(block, count):
    return jnp.broadcast_to(block[None], (count, *block.shape))


def swap(value, axis="core"):
    return lax.ppermute(value, axis, [(0, 1), (1, 0)])


def per_device(grads, errors, q_prev):
    g = grads.reshape(2, BLOCKS, 2 * ROWS, 128)
    e = errors.reshape(2, BLOCKS, 2 * ROWS, 128)
    qt = q_prev.transpose(0, 2, 1).reshape(2 * R, 128)

    part_other, g_other, e_other = left_half(False, g, e, qt)
    sent = swap(part_other)
    part, g_mine, e_mine = left_half(True, g, e, qt)
    part = exchange((part + sent).reshape(8, 512, 128), NEAR)
    part = sum_pieces(part).reshape(16, 32, 128)
    part = sum_pieces(exchange(part, FAR), 16)
    part = exchange(part, FAR).reshape(512, 128)
    p_mine = exchange(to_each(part, 8), NEAR).reshape(HALF_P)
    p_other = swap(p_mine)

    q_part, gram, sides_mine = right_half(p_mine, g_mine, e_mine)
    gram_other = swap(gram)
    inverse, q_keep, q_send, p_factors, sides_other = solve(
        p_other, g_other, e_other, p_mine, q_part, gram, gram_other
    )
    q_chip = q_keep + swap(q_send)
    q_chips = add_for_each(q_chip, swap(q_chip, "x_hi"), 8)
    q_mine = sum_pieces(lax.all_to_all(q_chips, "z", 0, 0, tiled=True))
    q_other = swap(q_mine)

    new_errors, q_mean, norm_part = errors_out(
        inverse, q_mine, q_other, (sides_mine, g_mine, e_mine), (sides_other, g_other, e_other)
    )
    norm_parts = lax.all_to_all(norm_part.reshape(8, 1, 128), TENSOR, 0, 0, tiled=True)
    q_factors = clip(norm_parts.reshape(8, 128), q_mean)
    return (
        new_errors.reshape(1, D, 2, 128),
        p_factors.reshape(2, R, ROWS).transpose(0, 2, 1),
        q_factors.reshape(2, R, 128).transpose(0, 2, 1),
    )


def solution(mesh):
    named = Mesh(mesh.devices.reshape(2, 8, 2, 4, 2), AXES)
    in_specs = (
        P(REPLICA, None, None, TENSOR),
        P(REPLICA, None, None, TENSOR),
        P(None, TENSOR, None),
    )
    out_specs = (P(REPLICA, None, None, TENSOR), P(None, REPLICA, None), P(None, TENSOR, None))
    return jax.shard_map(
        per_device, mesh=named, in_specs=in_specs, out_specs=out_specs, check_vma=False
    )
```

```python
import functools

import jax
import jax.numpy as jnp
from jax import lax
from jax.experimental import pallas as pl
from jax.experimental.pallas import tpu as pltpu
from jax.sharding import Mesh
from jax.sharding import PartitionSpec as P

D = 8192
KVW = 1024
R = 64
REPLICAS = 32
F32 = jnp.float32
BF16 = jnp.bfloat16

AXES = ("x_hi", "z", "core", "y", "x_lo")
REPLICA = ("x_hi", "z", "core")
TENSOR = ("y", "x_lo")
BLOCK = ("core", "y", "x_lo")

BLOCKS = 16
ROWS = 256
LOAD = 4
AHEAD = 2
DEPTH = 4
STEP = 4
PANEL = 8
LIMIT = 16 * 1024 * 1024


def chip_groups():
    def device(x, z, core, y):
        return (((x // 2 * 8 + z) * 2 + core) * 4 + y) * 2 + x % 2

    def line(core, along, across, z):
        x, y = (along, across) if core == 0 else (across, along)
        return device(x, z, core, y)

    near, far = [], []
    for core in range(2):
        pairs = [((2 * k + core) % 8, (2 * k + core + 1) % 8) for k in range(4)]
        for across in range(4):
            for pair in pairs:
                near.append([line(core, i, across, z) for z in pair for i in range(4)])
            for which in range(2):
                far.append([line(core, across, i, p[which]) for p in pairs for i in range(4)])
    return near, far


NEAR, FAR = chip_groups()


def exchange(pieces, groups):
    return lax.all_to_all(pieces, AXES, 0, 0, axis_index_groups=groups, tiled=True)


def in_hbm(value):
    return pltpu.with_memory_space_constraint(value, pltpu.HBM)


def split(value):
    high = value.astype(BF16)
    low = (value - high.astype(F32)).astype(BF16)
    return high, low


def split_dot(a, b, a_dim, b_dim):
    line = jnp.concatenate(split(b), 1 - b_dim)
    both = lax.dot_general(
        jnp.concatenate(split(a), a_dim),
        jnp.concatenate([line, line], b_dim),
        (((a_dim,), (b_dim,)), ((), ())),
        preferred_element_type=F32,
    )
    n = both.shape[1] // 2
    return both[:, :n] + both[:, n:]


def first_projection(shape):
    return lax.broadcasted_iota(jnp.int32, shape, len(shape) - 1) < R


VMEM = pl.BlockSpec(memory_space=pltpu.VMEM)
ANY = pl.BlockSpec(memory_space=pl.ANY)
HALF_P = (BLOCKS, ROWS, 128)
HALF_X = (BLOCKS, 2 * ROWS, 128)
HALF_S = (BLOCKS, 2 * ROWS, 256)


def in_vmem(value):
    return pltpu.with_memory_space_constraint(value, pltpu.VMEM)


def left_kernel(mine, g_hbm, e_hbm, qt_hbm, p_ref, g_ref, e_ref, qt, weights, rows, arrived, qt_arrived):
    core = lax.axis_index("core")
    half = core if mine else 1 - core
    qt_copy = pltpu.make_async_copy(qt_hbm, qt, qt_arrived)
    qt_copy.start()
    copies = []
    for c in range(BLOCKS // LOAD):
        blocks = pl.ds(c * LOAD, LOAD)
        pair = (
            pltpu.make_async_copy(g_hbm.at[half, blocks], g_ref.at[blocks], arrived.at[0, c]),
            pltpu.make_async_copy(e_hbm.at[half, blocks], e_ref.at[blocks], arrived.at[1, c]),
        )
        copies.append(pair)
    for pair in copies[:AHEAD]:
        for copy in pair:
            copy.start()
    qt_copy.wait()
    high, low = split(qt[...])
    weights[...] = jnp.concatenate(
        [jnp.concatenate([high, high], 1), jnp.concatenate([low, low], 1)], 0
    )
    mask = first_projection((ROWS, 2 * R))
    for c, pair in enumerate(copies):
        for copy in pair:
            copy.wait()
        for copy in copies[c + AHEAD] if c + AHEAD < len(copies) else ():
            copy.start()
        for block in range(c * LOAD, (c + 1) * LOAD):
            x = jnp.concatenate([g_ref[block], e_ref[block]], 1)
            both = lax.dot_general(
                x, weights[...], (((1,), (1,)), ((), ())), preferred_element_type=F32
            )
            slot = rows.at[block % STEP]
            slot[...] = both[:, : 2 * R] + both[:, 2 * R :]
            even = slot[pl.ds(0, ROWS, stride=2), :]
            odd = slot[pl.ds(1, ROWS, stride=2), :]
            p_ref[block] = jnp.where(mask, even, odd)


def left_half(mine, g, e, qt):
    return pl.pallas_call(
        functools.partial(left_kernel, mine),
        in_specs=[ANY, ANY, ANY],
        out_specs=[VMEM, VMEM, VMEM],
        out_shape=[
            pltpu.VMEM(HALF_P, F32),
            pltpu.VMEM(HALF_X, BF16),
            pltpu.VMEM(HALF_X, BF16),
        ],
        scratch_shapes=[
            pltpu.VMEM((2 * R, 128), F32),
            pltpu.VMEM((256, 256), BF16),
            pltpu.VMEM((STEP, 2 * ROWS, 128), F32),
            pltpu.SemaphoreType.DMA((2, BLOCKS // LOAD)),
            pltpu.SemaphoreType.DMA,
        ],
        compiler_params=pltpu.CompilerParams(vmem_limit_bytes=LIMIT),
        cost_estimate=pl.CostEstimate(
            flops=2 * 8192 * 256 * 256, bytes_accessed=8 * 2**20, transcendentals=0
        ),
        name="left_half",
    )(in_hbm(g), in_hbm(e), in_hbm(qt))


def interleave(p, rows, mask):
    rows[pl.ds(0, ROWS, stride=2), :] = jnp.where(mask, p, 0.0)
    rows[pl.ds(1, ROWS, stride=2), :] = jnp.where(mask, 0.0, p)
    return jnp.concatenate(split(rows[...]), 1)


def quadrants(total):
    n = total.shape[0] // 2
    return total[:n, :n] + total[:n, n:] + total[n:, :n] + total[n:, n:]


def add_rows(total, a, b):
    total[...] += lax.dot_general(
        a, b, (((0,), (0,)), ((), ())), preferred_element_type=F32
    )


def right_step(c, p_ref, g_ref, e_ref, sides, q_total, rows, mask):
    for j in range(STEP):
        sides[c * STEP + j] = interleave(p_ref[c * STEP + j], rows.at[j], mask)
        if (j + 1) % DEPTH == 0:
            blocks = pl.ds(c * STEP + j + 1 - DEPTH, DEPTH)
            depth = DEPTH * 2 * ROWS
            x = jnp.concatenate(
                [g_ref[blocks].reshape(depth, 128), e_ref[blocks].reshape(depth, 128)], 1
            )
            add_rows(q_total, sides[blocks].reshape(depth, 256), x)


RIGHT_SCRATCH = [pltpu.VMEM((256, 256), F32), pltpu.VMEM((STEP, 2 * ROWS, 128), F32)]


def right_kernel(p_ref, g_ref, e_ref, q_ref, gram_ref, sides, gram_total, q_total, rows):
    q_total[...] = jnp.zeros_like(q_total)
    gram_total[...] = jnp.zeros_like(gram_total)
    mask = first_projection((ROWS, 2 * R))
    for c in range(BLOCKS // STEP):
        right_step(c, p_ref, g_ref, e_ref, sides, q_total, rows, mask)
        for j in range(STEP):
            plain = jnp.concatenate(split(p_ref[c * STEP + j]), 1)
            add_rows(gram_total, plain, plain)

    q_ref[...] = quadrants(q_total[...])
    gram_ref[...] = quadrants(gram_total[...])


def right_half(p, g, e):
    square = jax.ShapeDtypeStruct((128, 128), F32)
    return pl.pallas_call(
        right_kernel,
        in_specs=[VMEM] * 3,
        out_specs=[VMEM] * 3,
        out_shape=[square, square, pltpu.VMEM(HALF_S, BF16)],
        scratch_shapes=[pltpu.VMEM((256, 256), F32), *RIGHT_SCRATCH],
        compiler_params=pltpu.CompilerParams(vmem_limit_bytes=LIMIT),
        cost_estimate=pl.CostEstimate(
            flops=3 * 8192 * 256 * 256, bytes_accessed=6 * 2**20, transcendentals=0
        ),
        name="right_half",
    )(in_vmem(p), in_vmem(g), in_vmem(e))


def reciprocal(x):
    return 1.0 / x


def inverse_of_factor(gram):
    mask = first_projection((R, 2 * R))
    lane = lax.broadcasted_iota(jnp.int32, (R, 2 * R), 1)
    row = lax.broadcasted_iota(jnp.int32, (R, 2 * R), 0)
    rest = jnp.where(mask, gram[:R], gram[R:])
    inverse = jnp.where(lane % R == row, 1.0, 0.0).astype(F32)
    pivots = jnp.ones((R, 2 * R), F32)
    for start in range(0, R, PANEL):
        panel = [
            jnp.where(mask, rest[:, j : j + 1], rest[:, R + j : R + j + 1])
            for j in range(start, start + PANEL)
        ]
        for i in range(0, PANEL, 2):
            j = start + i
            first, second = panel[i], panel[i + 1]
            a, b, c = first[j : j + 1], first[j + 1 : j + 2], second[j + 1 : j + 2]
            a_inverse = reciprocal(a)
            determinant = a * c - b * b
            pivots = jnp.where(row == j, a, pivots)
            pivots = jnp.where(row == j + 1, determinant * a_inverse, pivots)
            ratio = b * a_inverse
            one = jnp.where(row > j, first * a_inverse, 0.0)
            two = (second - one * b) * (a * reciprocal(determinant))
            two = jnp.where(row > j + 1, two, 0.0)

            def eliminate(matrix):
                upper = matrix[j : j + 1]
                lower = matrix[j + 1 : j + 2] - ratio * upper
                return matrix - one * upper - two * lower

            for m in range(i + 2, PANEL):
                panel[m] = eliminate(panel[m])
            inverse = eliminate(inverse)
            rest = eliminate(rest)
    return inverse * lax.rsqrt(pivots)


def by_core(first, second):
    low = lax.axis_index("core") == 0
    return jnp.where(low, first, second), jnp.where(low, second, first)


def other_kernel(p_ref, g_ref, e_ref, q_in, keep_ref, send_ref, sides, q_total, rows):
    q_total[...] = jnp.zeros_like(q_total)
    mask = first_projection((ROWS, 2 * R))
    for c in range(BLOCKS // STEP):
        right_step(c, p_ref, g_ref, e_ref, sides, q_total, rows, mask)
    q = quadrants(q_total[...]) + q_in[...]
    keep_ref[...], send_ref[...] = by_core(q[:R], q[R:])


def other_half(p, g, e, q):
    part = jax.ShapeDtypeStruct((R, 128), F32)
    return pl.pallas_call(
        other_kernel,
        in_specs=[VMEM] * 4,
        out_specs=[VMEM] * 3,
        out_shape=[part, part, pltpu.VMEM(HALF_S, BF16)],
        scratch_shapes=RIGHT_SCRATCH,
        compiler_params=pltpu.CompilerParams(vmem_limit_bytes=LIMIT),
        cost_estimate=pl.CostEstimate(
            flops=2 * 8192 * 256 * 256, bytes_accessed=6 * 2**20, transcendentals=0
        ),
        name="other_half",
    )(in_vmem(p), in_vmem(g), in_vmem(e), q)


def solve_kernel(gram_in, gram_other, p_mine, p_other, after, inverse_ref, factors_ref):
    solved = inverse_of_factor(gram_in[...] + gram_other[...])
    side = first_projection((R, 2 * R))
    inverse = jnp.concatenate([jnp.where(side, solved, 0.0), jnp.where(side, 0.0, solved)], 0)
    inverse_ref[...] = inverse
    core = lax.axis_index("core")
    block = lax.axis_index("z") * 2 + core
    p = jnp.where(lax.axis_index("x_hi") == core, p_mine[block], p_other[block])
    factors_ref[...] = split_dot(inverse, p, 1, 1).astype(BF16)


def solve(gram, gram_other, p_mine, p_other, after):
    return pl.pallas_call(
        solve_kernel,
        in_specs=[VMEM] * 5,
        out_specs=[VMEM] * 2,
        out_shape=[
            jax.ShapeDtypeStruct((128, 128), F32),
            jax.ShapeDtypeStruct((128, ROWS), BF16),
        ],
        compiler_params=pltpu.CompilerParams(vmem_limit_bytes=LIMIT),
        cost_estimate=pl.CostEstimate(
            flops=2**30, bytes_accessed=2**20, transcendentals=0
        ),
        name="solve",
    )(gram, gram_other, in_vmem(p_mine), in_vmem(p_other), after)


def mean_kernel(pieces, inverse_ref, q_ref, norm_ref):
    total = pieces[0]
    for i in range(1, pieces.shape[0]):
        total = total + pieces[i]
    upper, _ = by_core(inverse_ref[:R], inverse_ref[R:])
    q_mean = split_dot(upper, jnp.concatenate([total, total], 0), 1, 0) * (1.0 / REPLICAS)
    q_ref[...] = q_mean
    norm_ref[...] = jnp.full(norm_ref.shape, jnp.sum(q_mean * q_mean), F32)


def mean(pieces, inverse):
    return pl.pallas_call(
        mean_kernel,
        in_specs=[VMEM] * 2,
        out_specs=[VMEM] * 2,
        out_shape=[
            jax.ShapeDtypeStruct((R, 128), F32),
            jax.ShapeDtypeStruct((16, 128), F32),
        ],
        compiler_params=pltpu.CompilerParams(vmem_limit_bytes=LIMIT),
        name="mean",
    )(pieces, inverse)


def error_kernel(inverse_ref, q_mine, q_other, norm_parts, *rest):
    halves, (out_hbm, q_ref, weights, staged, sent) = (rest[:3], rest[3:6]), rest[6:]
    core = lax.axis_index("core")
    q_mean = jnp.concatenate(by_core(q_mine[...], q_other[...]), 0)
    norm_square = jnp.sum(norm_parts[...], 0, keepdims=True)
    clip_limit = 0.5 * (2 * KVW * R) ** 0.5
    q_ref[...] = q_mean * jnp.minimum(1.0, clip_limit / jnp.sqrt(norm_square))
    high, low = split(split_dot(inverse_ref[...], q_mean, 0, 0))
    line = jnp.concatenate([high, low], 1)
    weights[...] = jnp.concatenate([line, line], 0)
    copies = []
    for h, (sides, g_ref, e_ref) in enumerate(halves):
        for c in range(BLOCKS // STEP):
            for block in range(c * STEP, (c + 1) * STEP):
                approx = jnp.dot(sides[block], weights[...], preferred_element_type=F32)
                compensated = g_ref[block].astype(F32) + e_ref[block].astype(F32)
                left = compensated - (approx[:, :128] + approx[:, 128:])
                staged[h, block] = left.astype(BF16)
            blocks = pl.ds(c * STEP, STEP)
            place = core if h == 0 else 1 - core
            copies.append(
                pltpu.make_async_copy(
                    staged.at[h, blocks], out_hbm.at[place, blocks], sent.at[h, c]
                )
            )
            copies[-1].start()
    for copy in copies:
        copy.wait()


def errors_out(inverse, q_mine, q_other, norm_parts, mine, other):
    return pl.pallas_call(
        error_kernel,
        in_specs=[VMEM] * 10,
        out_specs=[ANY, VMEM],
        out_shape=[
            jax.ShapeDtypeStruct((2, BLOCKS, 2 * ROWS, 128), BF16),
            jax.ShapeDtypeStruct((128, 128), F32),
        ],
        scratch_shapes=[
            pltpu.VMEM((256, 256), BF16),
            pltpu.VMEM((2, *HALF_X), BF16),
            pltpu.SemaphoreType.DMA((2, BLOCKS // STEP)),
        ],
        compiler_params=pltpu.CompilerParams(vmem_limit_bytes=LIMIT),
        cost_estimate=pl.CostEstimate(
            flops=2 * 16384 * 256 * 256, bytes_accessed=16 * 2**20, transcendentals=0
        ),
        name="new_errors",
    )(inverse, q_mine, q_other, norm_parts, *[in_vmem(a) for a in (*mine, *other)])


def sum_kernel(pieces, out_ref):
    total = pieces[0]
    for i in range(1, pieces.shape[0]):
        total = total + pieces[i]
    if len(out_ref.shape) == 2:
        out_ref[...] = total
    else:
        for i in range(out_ref.shape[0]):
            out_ref[i] = total


def sum_pieces(pieces, copies=None):
    shape = pieces.shape[1:] if copies is None else (copies, *pieces.shape[1:])
    return pl.pallas_call(
        sum_kernel,
        in_specs=[VMEM],
        out_specs=VMEM,
        out_shape=jax.ShapeDtypeStruct(shape, F32),
        compiler_params=pltpu.CompilerParams(vmem_limit_bytes=LIMIT),
        name="sum_pieces",
    )(pieces)


def add_kernel(a_ref, b_ref, after, out_ref):
    total = a_ref[...] + b_ref[...]
    for i in range(out_ref.shape[0]):
        out_ref[i] = total


def add_for_each(a, b, copies, after):
    return pl.pallas_call(
        add_kernel,
        in_specs=[VMEM] * 3,
        out_specs=VMEM,
        out_shape=jax.ShapeDtypeStruct((copies, *a.shape), F32),
        compiler_params=pltpu.CompilerParams(vmem_limit_bytes=LIMIT),
        name="add_for_each",
    )(a, b, after)


def to_each(block, count):
    return jnp.broadcast_to(block[None], (count, *block.shape))


def swap(value, axis="core"):
    return lax.ppermute(value, axis, [(0, 1), (1, 0)])


def per_device(grads, errors, q_prev):
    g = grads.reshape(2, BLOCKS, 2 * ROWS, 128)
    e = errors.reshape(2, BLOCKS, 2 * ROWS, 128)
    qt = q_prev.transpose(0, 2, 1).reshape(2 * R, 128)

    part_other, g_other, e_other = left_half(False, g, e, qt)
    sent = swap(part_other)
    part, g_mine, e_mine = left_half(True, g, e, qt)
    part = exchange((part + sent).reshape(8, 512, 128), NEAR)
    part = sum_pieces(part).reshape(16, 32, 128)
    part = sum_pieces(exchange(part, FAR), 16)
    part = exchange(part, FAR).reshape(512, 128)
    p_mine = exchange(to_each(part, 8), NEAR).reshape(HALF_P)
    p_other = swap(p_mine)

    q_part, gram, sides_mine = right_half(p_mine, g_mine, e_mine)
    gram_other = swap(gram)
    q_keep, q_send, sides_other = other_half(p_other, g_other, e_other, q_part)

    q_chip = q_keep + swap(q_send)
    q_sent = swap(q_chip, "x_hi")
    inverse, p_factors = solve(gram, gram_other, p_mine, p_other, q_chip)
    q_chips = add_for_each(q_chip, q_sent, 8, inverse)
    q_chips = lax.all_to_all(q_chips, "z", 0, 0, tiled=True)
    q_mine, norm_part = mean(q_chips, inverse)
    q_other = swap(q_mine)
    norm_parts = lax.all_to_all(norm_part[:, None], BLOCK, 0, 0, tiled=True)

    new_errors, q_factors = errors_out(
        inverse,
        q_mine,
        q_other,
        norm_parts.reshape(16, 128),
        (sides_mine, g_mine, e_mine),
        (sides_other, g_other, e_other),
    )
    return (
        new_errors.reshape(1, D, 2, 128),
        p_factors.reshape(2, R, ROWS).transpose(0, 2, 1),
        q_factors.reshape(2, R, 128).transpose(0, 2, 1),
    )


def solution(mesh):
    named = Mesh(mesh.devices.reshape(2, 8, 2, 4, 2), AXES)
    in_specs = (
        P(REPLICA, None, None, TENSOR),
        P(REPLICA, None, None, TENSOR),
        P(None, TENSOR, None),
    )
    out_specs = (P(REPLICA, None, None, TENSOR), P(None, REPLICA, None), P(None, TENSOR, None))
    return jax.shard_map(
        per_device, mesh=named, in_specs=in_specs, out_specs=out_specs, check_vma=False
    )
```

```python
import functools

import jax
import jax.numpy as jnp
from jax import lax
from jax.experimental import pallas as pl
from jax.experimental.pallas import tpu as pltpu
from jax.sharding import Mesh
from jax.sharding import PartitionSpec as P

D = 8192
KVW = 1024
R = 64
REPLICAS = 32
F32 = jnp.float32
BF16 = jnp.bfloat16

AXES = ("x_hi", "z", "core", "y", "x_lo")
REPLICA = ("x_hi", "z", "core")
TENSOR = ("y", "x_lo")
BLOCK = ("core", "y", "x_lo")

BLOCKS = 16
ROWS = 256
LOAD = 4
AHEAD = 2
STEP = 4
SEND = 2
PANEL = 8
LIMIT = 16 * 1024 * 1024


def chip_groups():
    def device(x, z, core, y):
        return (((x // 2 * 8 + z) * 2 + core) * 4 + y) * 2 + x % 2

    def line(core, along, across, z):
        x, y = (along, across) if core == 0 else (across, along)
        return device(x, z, core, y)

    near, far = [], []
    for core in range(2):
        pairs = [((2 * k + core) % 8, (2 * k + core + 1) % 8) for k in range(4)]
        for across in range(4):
            for pair in pairs:
                near.append([line(core, i, across, z) for z in pair for i in range(4)])
            for which in range(2):
                far.append([line(core, across, i, p[which]) for p in pairs for i in range(4)])
    return near, far


NEAR, FAR = chip_groups()


def exchange(pieces, groups):
    return lax.all_to_all(pieces, AXES, 0, 0, axis_index_groups=groups, tiled=True)


def in_hbm(value):
    return pltpu.with_memory_space_constraint(value, pltpu.HBM)


def split(value):
    high = value.astype(BF16)
    low = (value - high.astype(F32)).astype(BF16)
    return high, low


def split_dot(a, b, a_dim, b_dim):
    line = jnp.concatenate(split(b), 1 - b_dim)
    both = lax.dot_general(
        jnp.concatenate(split(a), a_dim),
        jnp.concatenate([line, line], b_dim),
        (((a_dim,), (b_dim,)), ((), ())),
        preferred_element_type=F32,
    )
    n = both.shape[1] // 2
    return both[:, :n] + both[:, n:]


def first_projection(shape):
    return lax.broadcasted_iota(jnp.int32, shape, len(shape) - 1) < R


VMEM = pl.BlockSpec(memory_space=pltpu.VMEM)
ANY = pl.BlockSpec(memory_space=pl.ANY)
HALF_P = (BLOCKS, ROWS, 128)
HALF_X = (BLOCKS, 2 * ROWS, 128)
HALF_S = (BLOCKS, 2 * ROWS, 256)


def in_vmem(value):
    return pltpu.with_memory_space_constraint(value, pltpu.VMEM)


def left_kernel(mine, g_hbm, e_hbm, qt_hbm, *rest):
    if mine:
        g_other, e_other, p_ref, g_ref, e_ref, compensated, *rest = rest
    else:
        p_ref, g_ref, e_ref, *rest = rest
    qt, weights, rows, arrived, qt_arrived = rest
    core = lax.axis_index("core")
    half = core if mine else 1 - core
    qt_copy = pltpu.make_async_copy(qt_hbm, qt, qt_arrived)
    qt_copy.start()
    copies = []
    for c in range(BLOCKS // LOAD):
        blocks = pl.ds(c * LOAD, LOAD)
        pair = (
            pltpu.make_async_copy(g_hbm.at[half, blocks], g_ref.at[blocks], arrived.at[0, c]),
            pltpu.make_async_copy(e_hbm.at[half, blocks], e_ref.at[blocks], arrived.at[1, c]),
        )
        copies.append(pair)
    for pair in copies[:AHEAD]:
        for copy in pair:
            copy.start()
    qt_copy.wait()
    high, low = split(qt[...])
    weights[...] = jnp.concatenate(
        [jnp.concatenate([high, high], 1), jnp.concatenate([low, low], 1)], 0
    )
    mask = first_projection((ROWS, 2 * R))
    for c, pair in enumerate(copies):
        for copy in pair:
            copy.wait()
        for copy in copies[c + AHEAD] if c + AHEAD < len(copies) else ():
            copy.start()
        for block in range(c * LOAD, (c + 1) * LOAD):
            x = jnp.concatenate([g_ref[block], e_ref[block]], 1)
            both = lax.dot_general(
                x, weights[...], (((1,), (1,)), ((), ())), preferred_element_type=F32
            )
            slot = rows.at[block % STEP]
            slot[...] = both[:, : 2 * R] + both[:, 2 * R :]
            even = slot[pl.ds(0, ROWS, stride=2), :]
            odd = slot[pl.ds(1, ROWS, stride=2), :]
            p_ref[block] = jnp.where(mask, even, odd)
            if mine:
                compensated[block] = g_other[block].astype(F32) + e_other[block].astype(F32)


def left_half(g, e, qt, others=()):
    mine = len(others) > 0
    return pl.pallas_call(
        functools.partial(left_kernel, mine),
        in_specs=[ANY, ANY, ANY] + [VMEM] * len(others),
        out_specs=[VMEM] * (4 if mine else 3),
        out_shape=[
            pltpu.VMEM(HALF_P, F32),
            pltpu.VMEM(HALF_X, BF16),
            pltpu.VMEM(HALF_X, BF16),
            pltpu.VMEM(HALF_X, F32),
        ][: 4 if mine else 3],
        scratch_shapes=[
            pltpu.VMEM((2 * R, 128), F32),
            pltpu.VMEM((256, 256), BF16),
            pltpu.VMEM((STEP, 2 * ROWS, 128), F32),
            pltpu.SemaphoreType.DMA((2, BLOCKS // LOAD)),
            pltpu.SemaphoreType.DMA,
        ],
        compiler_params=pltpu.CompilerParams(vmem_limit_bytes=LIMIT),
        cost_estimate=pl.CostEstimate(
            flops=2 * 8192 * 256 * 256, bytes_accessed=8 * 2**20, transcendentals=0
        ),
        name="left_half",
    )(in_hbm(g), in_hbm(e), in_hbm(qt), *[in_vmem(a) for a in others])


def interleave(p, rows, mask):
    rows[pl.ds(0, ROWS, stride=2), :] = jnp.where(mask, p, 0.0)
    rows[pl.ds(1, ROWS, stride=2), :] = jnp.where(mask, 0.0, p)
    return jnp.concatenate(split(rows[...]), 1)


def quadrants(total):
    n = total.shape[0] // 2
    return total[:n, :n] + total[:n, n:] + total[n:, :n] + total[n:, n:]


def add_rows(total, a, b):
    total[...] += lax.dot_general(
        a, b, (((0,), (0,)), ((), ())), preferred_element_type=F32
    )


def right_kernel(p_ref, g_ref, e_ref, sibling, keep_ref, send_ref, gram_ref, sides, q_total, gram_total, rows, pairs):
    q_total[...] = jnp.zeros_like(q_total)
    gram_total[...] = jnp.zeros_like(gram_total)
    mask = first_projection((ROWS, 2 * R))
    depth = STEP * 2 * ROWS
    for c in range(BLOCKS // STEP):
        for j in range(STEP):
            block = c * STEP + j
            plain = jnp.concatenate(split(p_ref[block]), 1)
            add_rows(gram_total, plain, plain)
            sides[block] = interleave(p_ref[block], rows.at[j], mask)
            compensated = g_ref[block].astype(F32) + e_ref[block].astype(F32)
            pairs[j] = jnp.concatenate(split(compensated + sibling[block]), 1)
        blocks = pl.ds(c * STEP, STEP)
        add_rows(q_total, sides[blocks].reshape(depth, 256), pairs[...].reshape(depth, 256))
    q = quadrants(q_total[...])
    keep_ref[...], send_ref[...] = by_core(q[:R], q[R:])
    gram_ref[...] = quadrants(gram_total[...])


def right_half(p, g, e, sibling):
    part = jax.ShapeDtypeStruct((R, 128), F32)
    return pl.pallas_call(
        right_kernel,
        in_specs=[VMEM] * 4,
        out_specs=[VMEM] * 4,
        out_shape=[
            part,
            part,
            jax.ShapeDtypeStruct((128, 128), F32),
            pltpu.VMEM(HALF_S, BF16),
        ],
        scratch_shapes=[
            pltpu.VMEM((256, 256), F32),
            pltpu.VMEM((256, 256), F32),
            pltpu.VMEM((STEP, 2 * ROWS, 128), F32),
            pltpu.VMEM((STEP, 2 * ROWS, 256), BF16),
        ],
        compiler_params=pltpu.CompilerParams(vmem_limit_bytes=LIMIT),
        cost_estimate=pl.CostEstimate(
            flops=3 * 8192 * 256 * 256, bytes_accessed=6 * 2**20, transcendentals=0
        ),
        name="right_half",
    )(*[in_vmem(a) for a in (p, g, e, sibling)])


def reciprocal(x):
    return 1.0 / x


def inverse_of_factor(gram):
    mask = first_projection((R, 2 * R))
    lane = lax.broadcasted_iota(jnp.int32, (R, 2 * R), 1)
    row = lax.broadcasted_iota(jnp.int32, (R, 2 * R), 0)
    rest = jnp.where(mask, gram[:R], gram[R:])
    inverse = jnp.where(lane % R == row, 1.0, 0.0).astype(F32)
    pivots = jnp.ones((R, 2 * R), F32)
    for start in range(0, R, PANEL):
        panel = [
            jnp.where(mask, rest[:, j : j + 1], rest[:, R + j : R + j + 1])
            for j in range(start, start + PANEL)
        ]
        for i in range(0, PANEL, 2):
            j = start + i
            first, second = panel[i], panel[i + 1]
            a, b, c = first[j : j + 1], first[j + 1 : j + 2], second[j + 1 : j + 2]
            a_inverse = reciprocal(a)
            determinant = a * c - b * b
            pivots = jnp.where(row == j, a, pivots)
            pivots = jnp.where(row == j + 1, determinant * a_inverse, pivots)
            ratio = b * a_inverse
            one = jnp.where(row > j, first * a_inverse, 0.0)
            two = (second - one * b) * (a * reciprocal(determinant))
            two = jnp.where(row > j + 1, two, 0.0)

            def eliminate(matrix):
                upper = matrix[j : j + 1]
                lower = matrix[j + 1 : j + 2] - ratio * upper
                return matrix - one * upper - two * lower

            for m in range(i + 2, PANEL):
                panel[m] = eliminate(panel[m])
            inverse = eliminate(inverse)
            rest = eliminate(rest)
    return inverse * lax.rsqrt(pivots)


def by_core(first, second):
    low = lax.axis_index("core") == 0
    return jnp.where(low, first, second), jnp.where(low, second, first)


def solve_kernel(gram_in, gram_other, p_mine, p_other, after, inverse_ref, factors_ref, sides, rows):
    mask = first_projection((ROWS, 2 * R))
    for block in range(BLOCKS):
        sides[block] = interleave(p_other[block], rows.at[block % STEP], mask)
    solved = inverse_of_factor(gram_in[...] + gram_other[...])
    side = first_projection((R, 2 * R))
    inverse = jnp.concatenate([jnp.where(side, solved, 0.0), jnp.where(side, 0.0, solved)], 0)
    inverse_ref[...] = inverse
    core = lax.axis_index("core")
    block = lax.axis_index("z") * 2 + core
    p = jnp.where(lax.axis_index("x_hi") == core, p_mine[block], p_other[block])
    factors_ref[...] = split_dot(inverse, p, 1, 1).astype(BF16)


def solve(gram, gram_other, p_mine, p_other, after):
    return pl.pallas_call(
        solve_kernel,
        in_specs=[VMEM] * 5,
        out_specs=[VMEM] * 3,
        out_shape=[
            jax.ShapeDtypeStruct((128, 128), F32),
            jax.ShapeDtypeStruct((128, ROWS), BF16),
            pltpu.VMEM(HALF_S, BF16),
        ],
        scratch_shapes=[pltpu.VMEM((STEP, 2 * ROWS, 128), F32)],
        compiler_params=pltpu.CompilerParams(vmem_limit_bytes=LIMIT),
        cost_estimate=pl.CostEstimate(
            flops=2**30, bytes_accessed=2**20, transcendentals=0
        ),
        name="solve",
    )(gram, gram_other, in_vmem(p_mine), in_vmem(p_other), after)


def mean_kernel(pieces, inverse_ref, q_ref, norm_ref):
    total = pieces[0]
    for i in range(1, pieces.shape[0]):
        total = total + pieces[i]
    upper, _ = by_core(inverse_ref[:R], inverse_ref[R:])
    q_mean = split_dot(upper, jnp.concatenate([total, total], 0), 1, 0) * (1.0 / REPLICAS)
    q_ref[...] = q_mean
    norm_ref[...] = jnp.full(norm_ref.shape, jnp.sum(q_mean * q_mean), F32)


def mean(pieces, inverse):
    return pl.pallas_call(
        mean_kernel,
        in_specs=[VMEM] * 2,
        out_specs=[VMEM] * 2,
        out_shape=[
            jax.ShapeDtypeStruct((R, 128), F32),
            jax.ShapeDtypeStruct((16, 128), F32),
        ],
        compiler_params=pltpu.CompilerParams(vmem_limit_bytes=LIMIT),
        name="mean",
    )(pieces, inverse)


def error_kernel(inverse_ref, q_mine, q_other, norm_parts, *rest):
    halves, (out_hbm, q_ref, weights, staged, sent) = (rest[:3], rest[3:6]), rest[6:]
    core = lax.axis_index("core")
    q_mean = jnp.concatenate(by_core(q_mine[...], q_other[...]), 0)
    high, low = split(split_dot(inverse_ref[...], q_mean, 0, 0))
    line = jnp.concatenate([high, low], 1)
    weights[...] = jnp.concatenate([line, line], 0)
    copies = []
    for h, (sides, g_ref, e_ref) in enumerate(halves):
        for block in range(BLOCKS):
            approx = jnp.dot(sides[block], weights[...], preferred_element_type=F32)
            compensated = g_ref[block].astype(F32) + e_ref[block].astype(F32)
            left = compensated - (approx[:, :128] + approx[:, 128:])
            staged[h, block] = left.astype(BF16)
            if (block + 1) % SEND == 0:
                blocks = pl.ds(block + 1 - SEND, SEND)
                place = core if h == 0 else 1 - core
                copies.append(
                    pltpu.make_async_copy(
                        staged.at[h, blocks], out_hbm.at[place, blocks], sent.at[h, block // SEND]
                    )
                )
                copies[-1].start()
    norm_square = jnp.sum(norm_parts[...], 0, keepdims=True)
    clip_limit = 0.5 * (2 * KVW * R) ** 0.5
    q_ref[...] = q_mean * jnp.minimum(1.0, clip_limit / jnp.sqrt(norm_square))
    for copy in copies:
        copy.wait()


def errors_out(inverse, q_mine, q_other, norm_parts, mine, other):
    return pl.pallas_call(
        error_kernel,
        in_specs=[VMEM] * 10,
        out_specs=[ANY, VMEM],
        out_shape=[
            jax.ShapeDtypeStruct((2, BLOCKS, 2 * ROWS, 128), BF16),
            jax.ShapeDtypeStruct((128, 128), F32),
        ],
        scratch_shapes=[
            pltpu.VMEM((256, 256), BF16),
            pltpu.VMEM((2, *HALF_X), BF16),
            pltpu.SemaphoreType.DMA((2, BLOCKS // SEND)),
        ],
        compiler_params=pltpu.CompilerParams(vmem_limit_bytes=LIMIT),
        cost_estimate=pl.CostEstimate(
            flops=2 * 16384 * 256 * 256, bytes_accessed=16 * 2**20, transcendentals=0
        ),
        name="new_errors",
    )(inverse, q_mine, q_other, norm_parts, *[in_vmem(a) for a in (*mine, *other)])


def sum_kernel(pieces, out_ref):
    total = pieces[0]
    for i in range(1, pieces.shape[0]):
        total = total + pieces[i]
    if len(out_ref.shape) == 2:
        out_ref[...] = total
    else:
        for i in range(out_ref.shape[0]):
            out_ref[i] = total


def sum_pieces(pieces, copies=None):
    shape = pieces.shape[1:] if copies is None else (copies, *pieces.shape[1:])
    return pl.pallas_call(
        sum_kernel,
        in_specs=[VMEM],
        out_specs=VMEM,
        out_shape=jax.ShapeDtypeStruct(shape, F32),
        compiler_params=pltpu.CompilerParams(vmem_limit_bytes=LIMIT),
        name="sum_pieces",
    )(pieces)


def add_kernel(a_ref, b_ref, after, out_ref):
    total = a_ref[...] + b_ref[...]
    for i in range(out_ref.shape[0]):
        out_ref[i] = total


def add_for_each(a, b, copies, after):
    return pl.pallas_call(
        add_kernel,
        in_specs=[VMEM] * 3,
        out_specs=VMEM,
        out_shape=jax.ShapeDtypeStruct((copies, *a.shape), F32),
        compiler_params=pltpu.CompilerParams(vmem_limit_bytes=LIMIT),
        name="add_for_each",
    )(a, b, after)


def to_each(block, count):
    return jnp.broadcast_to(block[None], (count, *block.shape))


def swap(value, axis="core"):
    return lax.ppermute(value, axis, [(0, 1), (1, 0)])


def per_device(grads, errors, q_prev):
    g = grads.reshape(2, BLOCKS, 2 * ROWS, 128)
    e = errors.reshape(2, BLOCKS, 2 * ROWS, 128)
    qt = q_prev.transpose(0, 2, 1).reshape(2 * R, 128)

    part_other, g_other, e_other = left_half(g, e, qt)
    sent = swap(part_other)
    part, g_mine, e_mine, compensated = left_half(g, e, qt, (g_other, e_other))
    sibling = swap(compensated)
    part = exchange((part + sent).reshape(8, 512, 128), NEAR)
    part = sum_pieces(part).reshape(16, 32, 128)
    part = sum_pieces(exchange(part, FAR), 16)
    part = exchange(part, FAR).reshape(512, 128)
    p_mine = exchange(to_each(part, 8), NEAR).reshape(HALF_P)
    p_other = swap(p_mine)

    q_keep, q_send, gram, sides_mine = right_half(p_mine, g_mine, e_mine, sibling)
    gram_other = swap(gram)

    q_chip = q_keep + swap(q_send)
    q_sent = swap(q_chip, "x_hi")
    inverse, p_factors, sides_other = solve(gram, gram_other, p_mine, p_other, q_chip)
    q_chips = add_for_each(q_chip, q_sent, 8, inverse)
    q_chips = lax.all_to_all(q_chips, "z", 0, 0, tiled=True)
    q_mine, norm_part = mean(q_chips, inverse)
    q_other = swap(q_mine)
    norm_parts = lax.all_to_all(norm_part[:, None], BLOCK, 0, 0, tiled=True)

    new_errors, q_factors = errors_out(
        inverse,
        q_mine,
        q_other,
        norm_parts.reshape(16, 128),
        (sides_mine, g_mine, e_mine),
        (sides_other, g_other, e_other),
    )
    return (
        new_errors.reshape(1, D, 2, 128),
        p_factors.reshape(2, R, ROWS).transpose(0, 2, 1),
        q_factors.reshape(2, R, 128).transpose(0, 2, 1),
    )


def solution(mesh):
    named = Mesh(mesh.devices.reshape(2, 8, 2, 4, 2), AXES)
    in_specs = (
        P(REPLICA, None, None, TENSOR),
        P(REPLICA, None, None, TENSOR),
        P(None, TENSOR, None),
    )
    out_specs = (P(REPLICA, None, None, TENSOR), P(None, REPLICA, None), P(None, TENSOR, None))
    return jax.shard_map(
        per_device, mesh=named, in_specs=in_specs, out_specs=out_specs, check_vma=False
    )
```

```python
import functools

import jax
import jax.numpy as jnp
from jax import lax
from jax.experimental import pallas as pl
from jax.experimental.pallas import tpu as pltpu
from jax.sharding import Mesh
from jax.sharding import PartitionSpec as P

D = 8192
KVW = 1024
R = 64
REPLICAS = 32
F32 = jnp.float32
BF16 = jnp.bfloat16

AXES = ("x_hi", "z", "core", "y", "x_lo")
REPLICA = ("x_hi", "z", "core")
TENSOR = ("y", "x_lo")
BLOCK = ("core", "y", "x_lo")

BLOCKS = 16
ROWS = 256
LOADS = (8, 8)
AHEAD = 2
STEP = 4
SEND = 2
PANEL = 8
LIMIT = 16 * 1024 * 1024


def chip_groups():
    def device(x, z, core, y):
        return (((x // 2 * 8 + z) * 2 + core) * 4 + y) * 2 + x % 2

    def line(core, along, across, z):
        x, y = (along, across) if core == 0 else (across, along)
        return device(x, z, core, y)

    near, far = [], []
    for core in range(2):
        pairs = [((2 * k + core) % 8, (2 * k + core + 1) % 8) for k in range(4)]
        for across in range(4):
            for pair in pairs:
                near.append([line(core, i, across, z) for z in pair for i in range(4)])
            for which in range(2):
                far.append([line(core, across, i, p[which]) for p in pairs for i in range(4)])
    return near, far


NEAR, FAR = chip_groups()


def exchange(pieces, groups):
    return lax.all_to_all(pieces, AXES, 0, 0, axis_index_groups=groups, tiled=True)


def in_hbm(value):
    return pltpu.with_memory_space_constraint(value, pltpu.HBM)


def split(value):
    high = value.astype(BF16)
    low = (value - high.astype(F32)).astype(BF16)
    return high, low


def split_dot(a, b, a_dim, b_dim):
    line = jnp.concatenate(split(b), 1 - b_dim)
    both = lax.dot_general(
        jnp.concatenate(split(a), a_dim),
        jnp.concatenate([line, line], b_dim),
        (((a_dim,), (b_dim,)), ((), ())),
        preferred_element_type=F32,
    )
    n = both.shape[1] // 2
    return both[:, :n] + both[:, n:]


def first_projection(shape):
    return lax.broadcasted_iota(jnp.int32, shape, len(shape) - 1) < R


VMEM = pl.BlockSpec(memory_space=pltpu.VMEM)
ANY = pl.BlockSpec(memory_space=pl.ANY)
HALF_P = (BLOCKS, ROWS, 128)
HALF_X = (BLOCKS, 2 * ROWS, 128)
HALF_S = (BLOCKS, 2 * ROWS, 256)


def in_vmem(value):
    return pltpu.with_memory_space_constraint(value, pltpu.VMEM)


def left_kernel(mine, g_hbm, e_hbm, qt_hbm, p_ref, g_ref, e_ref, qt, weights, rows, arrived, qt_arrived):
    core = lax.axis_index("core")
    half = core if mine else 1 - core
    qt_copy = pltpu.make_async_copy(qt_hbm, qt, qt_arrived)
    qt_copy.start()
    copies = []
    for c, count in enumerate(LOADS):
        blocks = pl.ds(sum(LOADS[:c]), count)
        pair = (
            pltpu.make_async_copy(g_hbm.at[half, blocks], g_ref.at[blocks], arrived.at[0, c]),
            pltpu.make_async_copy(e_hbm.at[half, blocks], e_ref.at[blocks], arrived.at[1, c]),
        )
        copies.append(pair)
    for pair in copies[:AHEAD]:
        for copy in pair:
            copy.start(priority=1)
    qt_copy.wait()
    high, low = split(qt[...])
    weights[...] = jnp.concatenate(
        [jnp.concatenate([high, high], 1), jnp.concatenate([low, low], 1)], 0
    )
    mask = first_projection((ROWS, 2 * R))
    for c, pair in enumerate(copies):
        for copy in pair:
            copy.wait()
        for copy in copies[c + AHEAD] if c + AHEAD < len(copies) else ():
            copy.start(priority=1)
        for block in range(sum(LOADS[:c]), sum(LOADS[: c + 1])):
            x = jnp.concatenate([g_ref[block], e_ref[block]], 1)
            both = lax.dot_general(
                x, weights[...], (((1,), (1,)), ((), ())), preferred_element_type=F32
            )
            slot = rows.at[block % STEP]
            slot[...] = both[:, : 2 * R] + both[:, 2 * R :]
            even = slot[pl.ds(0, ROWS, stride=2), :]
            odd = slot[pl.ds(1, ROWS, stride=2), :]
            p_ref[block] = jnp.where(mask, even, odd)


def left_half(mine, g, e, qt):
    return pl.pallas_call(
        functools.partial(left_kernel, mine),
        in_specs=[ANY, ANY, ANY],
        out_specs=[VMEM, VMEM, VMEM],
        out_shape=[
            pltpu.VMEM(HALF_P, F32),
            pltpu.VMEM(HALF_X, BF16),
            pltpu.VMEM(HALF_X, BF16),
        ],
        scratch_shapes=[
            pltpu.VMEM((2 * R, 128), F32),
            pltpu.VMEM((256, 256), BF16),
            pltpu.VMEM((STEP, 2 * ROWS, 128), F32),
            pltpu.SemaphoreType.DMA((2, len(LOADS))),
            pltpu.SemaphoreType.DMA,
        ],
        compiler_params=pltpu.CompilerParams(vmem_limit_bytes=LIMIT),
        cost_estimate=pl.CostEstimate(
            flops=2 * 8192 * 256 * 256, bytes_accessed=8 * 2**20, transcendentals=0
        ),
        name="left_half",
    )(in_hbm(g), in_hbm(e), in_hbm(qt))


def interleave(p, rows, mask):
    rows[pl.ds(0, ROWS, stride=2), :] = jnp.where(mask, p, 0.0)
    rows[pl.ds(1, ROWS, stride=2), :] = jnp.where(mask, 0.0, p)
    return jnp.concatenate(split(rows[...]), 1)


def quadrants(total):
    n = total.shape[0] // 2
    return total[:n, :n] + total[:n, n:] + total[n:, :n] + total[n:, n:]


def add_rows(total, a, b):
    total[...] += lax.dot_general(
        a, b, (((0,), (0,)), ((), ())), preferred_element_type=F32
    )


def right_step(c, p_ref, g_ref, e_ref, sides, q_total, rows, mask):
    for j in range(STEP):
        sides[c * STEP + j] = interleave(p_ref[c * STEP + j], rows.at[j], mask)
    blocks = pl.ds(c * STEP, STEP)
    depth = STEP * 2 * ROWS
    x = jnp.concatenate(
        [g_ref[blocks].reshape(depth, 128), e_ref[blocks].reshape(depth, 128)], 1
    )
    add_rows(q_total, sides[blocks].reshape(depth, 256), x)


RIGHT_SCRATCH = [pltpu.VMEM((256, 256), F32), pltpu.VMEM((STEP, 2 * ROWS, 128), F32)]


def right_kernel(p_ref, g_ref, e_ref, q_ref, gram_ref, sides, gram_total, q_total, rows):
    q_total[...] = jnp.zeros_like(q_total)
    gram_total[...] = jnp.zeros_like(gram_total)
    mask = first_projection((ROWS, 2 * R))
    for c in range(BLOCKS // STEP):
        right_step(c, p_ref, g_ref, e_ref, sides, q_total, rows, mask)
        for j in range(STEP):
            plain = jnp.concatenate(split(p_ref[c * STEP + j]), 1)
            add_rows(gram_total, plain, plain)

    q_ref[...] = quadrants(q_total[...])
    gram_ref[...] = quadrants(gram_total[...])


def right_half(p, g, e):
    square = jax.ShapeDtypeStruct((128, 128), F32)
    return pl.pallas_call(
        right_kernel,
        in_specs=[VMEM] * 3,
        out_specs=[VMEM] * 3,
        out_shape=[square, square, pltpu.VMEM(HALF_S, BF16)],
        scratch_shapes=[pltpu.VMEM((256, 256), F32), *RIGHT_SCRATCH],
        compiler_params=pltpu.CompilerParams(vmem_limit_bytes=LIMIT),
        cost_estimate=pl.CostEstimate(
            flops=3 * 8192 * 256 * 256, bytes_accessed=6 * 2**20, transcendentals=0
        ),
        name="right_half",
    )(in_vmem(p), in_vmem(g), in_vmem(e))


def reciprocal(x):
    return 1.0 / x


def inverse_of_factor(gram):
    mask = first_projection((R, 2 * R))
    lane = lax.broadcasted_iota(jnp.int32, (R, 2 * R), 1)
    row = lax.broadcasted_iota(jnp.int32, (R, 2 * R), 0)
    rest = jnp.where(mask, gram[:R], gram[R:])
    inverse = jnp.where(lane % R == row, 1.0, 0.0).astype(F32)
    pivots = jnp.ones((R, 2 * R), F32)
    for start in range(0, R, PANEL):
        panel = [
            jnp.where(mask, rest[:, j : j + 1], rest[:, R + j : R + j + 1])
            for j in range(start, start + PANEL)
        ]
        for i in range(0, PANEL, 2):
            j = start + i
            first, second = panel[i], panel[i + 1]
            a, b, c = first[j : j + 1], first[j + 1 : j + 2], second[j + 1 : j + 2]
            a_inverse = reciprocal(a)
            determinant = a * c - b * b
            pivots = jnp.where(row == j, a, pivots)
            pivots = jnp.where(row == j + 1, determinant * a_inverse, pivots)
            ratio = b * a_inverse
            one = jnp.where(row > j, first * a_inverse, 0.0)
            two = (second - one * b) * (a * reciprocal(determinant))
            two = jnp.where(row > j + 1, two, 0.0)

            def eliminate(matrix):
                upper = matrix[j : j + 1]
                lower = matrix[j + 1 : j + 2] - ratio * upper
                return matrix - one * upper - two * lower

            for m in range(i + 2, PANEL):
                panel[m] = eliminate(panel[m])
            inverse = eliminate(inverse)
            rest = eliminate(rest)
    return inverse * lax.rsqrt(pivots)


def by_core(first, second):
    low = lax.axis_index("core") == 0
    return jnp.where(low, first, second), jnp.where(low, second, first)


def other_kernel(p_ref, g_ref, e_ref, q_in, keep_ref, send_ref, sides, q_total, rows):
    q_total[...] = jnp.zeros_like(q_total)
    mask = first_projection((ROWS, 2 * R))
    for c in range(BLOCKS // STEP):
        right_step(c, p_ref, g_ref, e_ref, sides, q_total, rows, mask)
    q = quadrants(q_total[...]) + q_in[...]
    keep_ref[...], send_ref[...] = by_core(q[:R], q[R:])


def other_half(p, g, e, q):
    part = jax.ShapeDtypeStruct((R, 128), F32)
    return pl.pallas_call(
        other_kernel,
        in_specs=[VMEM] * 4,
        out_specs=[VMEM] * 3,
        out_shape=[part, part, pltpu.VMEM(HALF_S, BF16)],
        scratch_shapes=RIGHT_SCRATCH,
        compiler_params=pltpu.CompilerParams(vmem_limit_bytes=LIMIT),
        cost_estimate=pl.CostEstimate(
            flops=2 * 8192 * 256 * 256, bytes_accessed=6 * 2**20, transcendentals=0
        ),
        name="other_half",
    )(in_vmem(p), in_vmem(g), in_vmem(e), q)


def solve_kernel(gram_in, gram_other, p_mine, p_other, after, inverse_ref, factors_ref):
    solved = inverse_of_factor(gram_in[...] + gram_other[...])
    side = first_projection((R, 2 * R))
    inverse = jnp.concatenate([jnp.where(side, solved, 0.0), jnp.where(side, 0.0, solved)], 0)
    inverse_ref[...] = inverse
    core = lax.axis_index("core")
    block = lax.axis_index("z") * 2 + core
    p = jnp.where(lax.axis_index("x_hi") == core, p_mine[block], p_other[block])
    factors_ref[...] = split_dot(inverse, p, 1, 1).astype(BF16)


def solve(gram, gram_other, p_mine, p_other, after):
    return pl.pallas_call(
        solve_kernel,
        in_specs=[VMEM] * 5,
        out_specs=[VMEM] * 2,
        out_shape=[
            jax.ShapeDtypeStruct((128, 128), F32),
            jax.ShapeDtypeStruct((128, ROWS), BF16),
        ],
        compiler_params=pltpu.CompilerParams(vmem_limit_bytes=LIMIT),
        cost_estimate=pl.CostEstimate(
            flops=2**30, bytes_accessed=2**20, transcendentals=0
        ),
        name="solve",
    )(gram, gram_other, in_vmem(p_mine), in_vmem(p_other), after)


def mean_kernel(pieces, inverse_ref, q_ref, norm_ref):
    total = pieces[0]
    for i in range(1, pieces.shape[0]):
        total = total + pieces[i]
    upper, _ = by_core(inverse_ref[:R], inverse_ref[R:])
    q_mean = split_dot(upper, jnp.concatenate([total, total], 0), 1, 0) * (1.0 / REPLICAS)
    q_ref[...] = q_mean
    norm_ref[...] = jnp.full(norm_ref.shape, jnp.sum(q_mean * q_mean), F32)


def mean(pieces, inverse):
    return pl.pallas_call(
        mean_kernel,
        in_specs=[VMEM] * 2,
        out_specs=[VMEM] * 2,
        out_shape=[
            jax.ShapeDtypeStruct((R, 128), F32),
            jax.ShapeDtypeStruct((16, 128), F32),
        ],
        compiler_params=pltpu.CompilerParams(vmem_limit_bytes=LIMIT),
        name="mean",
    )(pieces, inverse)


def error_kernel(inverse_ref, q_mine, q_other, norm_parts, *rest):
    halves, (out_hbm, q_hbm, q_staged, q_sent, weights, staged, sent) = (rest[:3], rest[3:6]), rest[6:]
    core = lax.axis_index("core")
    q_mean = jnp.concatenate(by_core(q_mine[...], q_other[...]), 0)
    norm_square = jnp.sum(norm_parts[...], 0, keepdims=True)
    clip_limit = 0.5 * (2 * KVW * R) ** 0.5
    q_staged[...] = q_mean * jnp.minimum(1.0, clip_limit / jnp.sqrt(norm_square))
    copies = [pltpu.make_async_copy(q_staged, q_hbm, q_sent)]
    copies[0].start()
    high, low = split(split_dot(inverse_ref[...], q_mean, 0, 0))
    line = jnp.concatenate([high, low], 1)
    weights[...] = jnp.concatenate([line, line], 0)
    for h, (sides, g_ref, e_ref) in enumerate(halves):
        for block in range(BLOCKS):
            approx = jnp.dot(sides[block], weights[...], preferred_element_type=F32)
            compensated = g_ref[block].astype(F32) + e_ref[block].astype(F32)
            left = compensated - (approx[:, :128] + approx[:, 128:])
            staged[h, block] = left.astype(BF16)
            if (block + 1) % SEND == 0:
                blocks = pl.ds(block + 1 - SEND, SEND)
                place = core if h == 0 else 1 - core
                copies.append(
                    pltpu.make_async_copy(
                        staged.at[h, blocks], out_hbm.at[place, blocks], sent.at[h, block // SEND]
                    )
                )
                copies[-1].start()
    for copy in copies:
        copy.wait()


def errors_out(inverse, q_mine, q_other, norm_parts, mine, other):
    return pl.pallas_call(
        error_kernel,
        in_specs=[VMEM] * 10,
        out_specs=[ANY, ANY],
        out_shape=[
            jax.ShapeDtypeStruct((2, BLOCKS, 2 * ROWS, 128), BF16),
            jax.ShapeDtypeStruct((128, 128), F32),
        ],
        scratch_shapes=[
            pltpu.VMEM((128, 128), F32),
            pltpu.SemaphoreType.DMA,
            pltpu.VMEM((256, 256), BF16),
            pltpu.VMEM((2, *HALF_X), BF16),
            pltpu.SemaphoreType.DMA((2, BLOCKS // SEND)),
        ],
        compiler_params=pltpu.CompilerParams(vmem_limit_bytes=LIMIT),
        cost_estimate=pl.CostEstimate(
            flops=2 * 16384 * 256 * 256, bytes_accessed=16 * 2**20, transcendentals=0
        ),
        name="new_errors",
    )(inverse, q_mine, q_other, norm_parts, *[in_vmem(a) for a in (*mine, *other)])


def sum_kernel(pieces, out_ref):
    total = pieces[0]
    for i in range(1, pieces.shape[0]):
        total = total + pieces[i]
    if len(out_ref.shape) == 2:
        out_ref[...] = total
    else:
        for i in range(out_ref.shape[0]):
            out_ref[i] = total


def sum_pieces(pieces, copies=None):
    shape = pieces.shape[1:] if copies is None else (copies, *pieces.shape[1:])
    return pl.pallas_call(
        sum_kernel,
        in_specs=[VMEM],
        out_specs=VMEM,
        out_shape=jax.ShapeDtypeStruct(shape, F32),
        compiler_params=pltpu.CompilerParams(vmem_limit_bytes=LIMIT),
        name="sum_pieces",
    )(pieces)


def add_kernel(a_ref, b_ref, after, out_ref):
    total = a_ref[...] + b_ref[...]
    for i in range(out_ref.shape[0]):
        out_ref[i] = total


def add_for_each(a, b, copies, after):
    return pl.pallas_call(
        add_kernel,
        in_specs=[VMEM] * 3,
        out_specs=VMEM,
        out_shape=jax.ShapeDtypeStruct((copies, *a.shape), F32),
        compiler_params=pltpu.CompilerParams(vmem_limit_bytes=LIMIT),
        name="add_for_each",
    )(a, b, after)


def to_each(block, count):
    return jnp.broadcast_to(block[None], (count, *block.shape))


def swap(value, axis="core"):
    return lax.ppermute(value, axis, [(0, 1), (1, 0)])


def per_device(grads, errors, q_prev):
    g = grads.reshape(2, BLOCKS, 2 * ROWS, 128)
    e = errors.reshape(2, BLOCKS, 2 * ROWS, 128)
    qt = q_prev.transpose(0, 2, 1).reshape(2 * R, 128)

    part_other, g_other, e_other = left_half(False, g, e, qt)
    sent = swap(part_other)
    part, g_mine, e_mine = left_half(True, g, e, qt)
    part = exchange((part + sent).reshape(8, 512, 128), NEAR)
    part = sum_pieces(part).reshape(16, 32, 128)
    part = sum_pieces(exchange(part, FAR), 16)
    part = exchange(part, FAR).reshape(512, 128)
    p_mine = exchange(to_each(part, 8), NEAR).reshape(HALF_P)
    p_other = swap(p_mine)

    q_part, gram, sides_mine = right_half(p_mine, g_mine, e_mine)
    gram_other = swap(gram)
    q_keep, q_send, sides_other = other_half(p_other, g_other, e_other, q_part)

    q_chip = q_keep + swap(q_send)
    q_sent = swap(q_chip, "x_hi")
    inverse, p_factors = solve(gram, gram_other, p_mine, p_other, q_chip)
    q_chips = add_for_each(q_chip, q_sent, 8, inverse)
    q_chips = lax.all_to_all(q_chips, "z", 0, 0, tiled=True)
    q_mine, norm_part = mean(q_chips, inverse)
    q_other = swap(q_mine)
    norm_parts = lax.all_to_all(norm_part[:, None], BLOCK, 0, 0, tiled=True)

    new_errors, q_factors = errors_out(
        inverse,
        q_mine,
        q_other,
        norm_parts.reshape(16, 128),
        (sides_mine, g_mine, e_mine),
        (sides_other, g_other, e_other),
    )
    return (
        new_errors.reshape(1, D, 2, 128),
        p_factors.reshape(2, R, ROWS).transpose(0, 2, 1),
        q_factors.reshape(2, R, 128).transpose(0, 2, 1),
    )


def solution(mesh):
    named = Mesh(mesh.devices.reshape(2, 8, 2, 4, 2), AXES)
    in_specs = (
        P(REPLICA, None, None, TENSOR),
        P(REPLICA, None, None, TENSOR),
        P(None, TENSOR, None),
    )
    out_specs = (P(REPLICA, None, None, TENSOR), P(None, REPLICA, None), P(None, TENSOR, None))
    return jax.shard_map(
        per_device, mesh=named, in_specs=in_specs, out_specs=out_specs, check_vma=False
    )
```

```python
import functools

import jax
import jax.numpy as jnp
from jax import lax
from jax.experimental import pallas as pl
from jax.experimental.pallas import tpu as pltpu
from jax.sharding import Mesh
from jax.sharding import PartitionSpec as P

D = 8192
KVW = 1024
R = 64
REPLICAS = 32
F32 = jnp.float32
BF16 = jnp.bfloat16

AXES = ("x_hi", "z", "core", "y", "x_lo")
REPLICA = ("x_hi", "z", "core")
TENSOR = ("y", "x_lo")
BLOCK = ("core", "y", "x_lo")

BLOCKS = 16
ROWS = 256
LOADS = (8, 8)
AHEAD = 2
STEP = 4
SEND = 2
PANEL = 8
LIMIT = 16 * 1024 * 1024


def chip_groups():
    def device(x, z, core, y):
        return (((x // 2 * 8 + z) * 2 + core) * 4 + y) * 2 + x % 2

    def line(core, along, across, z):
        x, y = (along, across) if core == 0 else (across, along)
        return device(x, z, core, y)

    near, far = [], []
    for core in range(2):
        pairs = [((2 * k + core) % 8, (2 * k + core + 1) % 8) for k in range(4)]
        for across in range(4):
            for pair in pairs:
                near.append([line(core, i, across, z) for z in pair for i in range(4)])
            for which in range(2):
                far.append([line(core, across, i, p[which]) for p in pairs for i in range(4)])
    return near, far


NEAR, FAR = chip_groups()


def exchange(pieces, groups):
    return lax.all_to_all(pieces, AXES, 0, 0, axis_index_groups=groups, tiled=True)


def in_hbm(value):
    return pltpu.with_memory_space_constraint(value, pltpu.HBM)


def split(value):
    high = value.astype(BF16)
    low = (value - high.astype(F32)).astype(BF16)
    return high, low


def split_dot(a, b, a_dim, b_dim):
    line = jnp.concatenate(split(b), 1 - b_dim)
    both = lax.dot_general(
        jnp.concatenate(split(a), a_dim),
        jnp.concatenate([line, line], b_dim),
        (((a_dim,), (b_dim,)), ((), ())),
        preferred_element_type=F32,
    )
    n = both.shape[1] // 2
    return both[:, :n] + both[:, n:]


def first_projection(shape):
    return lax.broadcasted_iota(jnp.int32, shape, len(shape) - 1) < R


VMEM = pl.BlockSpec(memory_space=pltpu.VMEM)
ANY = pl.BlockSpec(memory_space=pl.ANY)
HALF_P = (BLOCKS, ROWS, 128)
HALF_X = (BLOCKS, 2 * ROWS, 128)
HALF_S = (BLOCKS, 2 * ROWS, 256)


def in_vmem(value):
    return pltpu.with_memory_space_constraint(value, pltpu.VMEM)


def left_kernel(mine, g_hbm, e_hbm, qt_hbm, p_ref, g_ref, e_ref, qt, weights, rows, arrived, qt_arrived):
    core = lax.axis_index("core")
    half = core if mine else 1 - core
    qt_copy = pltpu.make_async_copy(qt_hbm, qt, qt_arrived)
    qt_copy.start()
    copies = []
    for c, count in enumerate(LOADS):
        blocks = pl.ds(sum(LOADS[:c]), count)
        pair = (
            pltpu.make_async_copy(g_hbm.at[half, blocks], g_ref.at[blocks], arrived.at[0, c]),
            pltpu.make_async_copy(e_hbm.at[half, blocks], e_ref.at[blocks], arrived.at[1, c]),
        )
        copies.append(pair)
    for pair in copies[:AHEAD]:
        for copy in pair:
            copy.start(priority=1)
    qt_copy.wait()
    high, low = split(qt[...])
    weights[...] = jnp.concatenate(
        [jnp.concatenate([high, high], 1), jnp.concatenate([low, low], 1)], 0
    )
    mask = first_projection((ROWS, 2 * R))
    for c, pair in enumerate(copies):
        for copy in pair:
            copy.wait()
        for copy in copies[c + AHEAD] if c + AHEAD < len(copies) else ():
            copy.start(priority=1)
        for block in range(sum(LOADS[:c]), sum(LOADS[: c + 1])):
            x = jnp.concatenate([g_ref[block], e_ref[block]], 1)
            both = lax.dot_general(
                x, weights[...], (((1,), (1,)), ((), ())), preferred_element_type=F32
            )
            slot = rows.at[block % STEP]
            slot[...] = both[:, : 2 * R] + both[:, 2 * R :]
            even = slot[pl.ds(0, ROWS, stride=2), :]
            odd = slot[pl.ds(1, ROWS, stride=2), :]
            p_ref[block] = jnp.where(mask, even, odd)


def left_half(mine, g, e, qt):
    return pl.pallas_call(
        functools.partial(left_kernel, mine),
        in_specs=[ANY, ANY, ANY],
        out_specs=[VMEM, VMEM, VMEM],
        out_shape=[
            pltpu.VMEM(HALF_P, F32),
            pltpu.VMEM(HALF_X, BF16),
            pltpu.VMEM(HALF_X, BF16),
        ],
        scratch_shapes=[
            pltpu.VMEM((2 * R, 128), F32),
            pltpu.VMEM((256, 256), BF16),
            pltpu.VMEM((STEP, 2 * ROWS, 128), F32),
            pltpu.SemaphoreType.DMA((2, len(LOADS))),
            pltpu.SemaphoreType.DMA,
        ],
        compiler_params=pltpu.CompilerParams(vmem_limit_bytes=LIMIT),
        cost_estimate=pl.CostEstimate(
            flops=2 * 8192 * 256 * 256, bytes_accessed=8 * 2**20, transcendentals=0
        ),
        name="left_half",
    )(in_hbm(g), in_hbm(e), in_hbm(qt))


def interleave(p, rows, mask):
    rows[pl.ds(0, ROWS, stride=2), :] = jnp.where(mask, p, 0.0)
    rows[pl.ds(1, ROWS, stride=2), :] = jnp.where(mask, 0.0, p)
    return jnp.concatenate(split(rows[...]), 1)


def quadrants(total):
    n = total.shape[0] // 2
    return total[:n, :n] + total[:n, n:] + total[n:, :n] + total[n:, n:]


def add_rows(total, a, b):
    total[...] += lax.dot_general(
        a, b, (((0,), (0,)), ((), ())), preferred_element_type=F32
    )


def right_step(c, p_ref, g_ref, e_ref, sides, q_total, rows, mask):
    for j in range(STEP):
        sides[c * STEP + j] = interleave(p_ref[c * STEP + j], rows.at[j], mask)
    blocks = pl.ds(c * STEP, STEP)
    depth = STEP * 2 * ROWS
    x = jnp.concatenate(
        [g_ref[blocks].reshape(depth, 128), e_ref[blocks].reshape(depth, 128)], 1
    )
    add_rows(q_total, sides[blocks].reshape(depth, 256), x)


RIGHT_SCRATCH = [pltpu.VMEM((256, 256), F32), pltpu.VMEM((STEP, 2 * ROWS, 128), F32)]


def right_kernel(p_ref, g_ref, e_ref, q_ref, gram_ref, sides, gram_total, q_total, rows):
    q_total[...] = jnp.zeros_like(q_total)
    gram_total[...] = jnp.zeros_like(gram_total)
    mask = first_projection((ROWS, 2 * R))
    for c in range(BLOCKS // STEP):
        right_step(c, p_ref, g_ref, e_ref, sides, q_total, rows, mask)
        for j in range(STEP):
            plain = jnp.concatenate(split(p_ref[c * STEP + j]), 1)
            add_rows(gram_total, plain, plain)

    q_ref[...] = quadrants(q_total[...])
    gram_ref[...] = quadrants(gram_total[...])


def right_half(p, g, e):
    square = jax.ShapeDtypeStruct((128, 128), F32)
    return pl.pallas_call(
        right_kernel,
        in_specs=[VMEM] * 3,
        out_specs=[VMEM] * 3,
        out_shape=[square, square, pltpu.VMEM(HALF_S, BF16)],
        scratch_shapes=[pltpu.VMEM((256, 256), F32), *RIGHT_SCRATCH],
        compiler_params=pltpu.CompilerParams(vmem_limit_bytes=LIMIT),
        cost_estimate=pl.CostEstimate(
            flops=3 * 8192 * 256 * 256, bytes_accessed=6 * 2**20, transcendentals=0
        ),
        name="right_half",
    )(in_vmem(p), in_vmem(g), in_vmem(e))


def inverse_of_factor(gram):
    mask = first_projection((R, 2 * R))
    lane = lax.broadcasted_iota(jnp.int32, (R, 2 * R), 1)
    row = lax.broadcasted_iota(jnp.int32, (R, 2 * R), 0)
    rest = jnp.where(mask, gram[:R], gram[R:])
    inverse = jnp.where(lane % R == row, 1.0, 0.0).astype(F32)
    pivots = jnp.ones((R, 2 * R), F32)
    for start in range(0, R, PANEL):
        panel = [
            jnp.where(mask, rest[:, j : j + 1], rest[:, R + j : R + j + 1])
            for j in range(start, start + PANEL)
        ]
        for i in range(0, PANEL, 2):
            j = start + i
            first, second = panel[i], panel[i + 1]
            a, b, c = first[j : j + 1], first[j + 1 : j + 2], second[j + 1 : j + 2]
            a_inverse = 1.0 / a
            ratio = b * a_inverse
            rest_c = c - b * ratio
            pivots = jnp.where(row == j, a, pivots)
            pivots = jnp.where(row == j + 1, rest_c, pivots)
            one = jnp.where(row > j, first * a_inverse, 0.0)
            two = (second - one * b) * (1.0 / rest_c)
            two = jnp.where(row > j + 1, two, 0.0)

            def eliminate(matrix):
                upper = matrix[j : j + 1]
                lower = matrix[j + 1 : j + 2] - ratio * upper
                return matrix - one * upper - two * lower

            for m in range(i + 2, PANEL):
                panel[m] = eliminate(panel[m])
            inverse = eliminate(inverse)
            rest = eliminate(rest)
    return inverse * lax.rsqrt(pivots)


def by_core(first, second):
    low = lax.axis_index("core") == 0
    return jnp.where(low, first, second), jnp.where(low, second, first)


def other_kernel(p_ref, g_ref, e_ref, q_in, keep_ref, send_ref, sides, q_total, rows):
    q_total[...] = jnp.zeros_like(q_total)
    mask = first_projection((ROWS, 2 * R))
    for c in range(BLOCKS // STEP):
        right_step(c, p_ref, g_ref, e_ref, sides, q_total, rows, mask)
    q = quadrants(q_total[...]) + q_in[...]
    keep_ref[...], send_ref[...] = by_core(q[:R], q[R:])


def other_half(p, g, e, q):
    part = jax.ShapeDtypeStruct((R, 128), F32)
    return pl.pallas_call(
        other_kernel,
        in_specs=[VMEM] * 4,
        out_specs=[VMEM] * 3,
        out_shape=[part, part, pltpu.VMEM(HALF_S, BF16)],
        scratch_shapes=RIGHT_SCRATCH,
        compiler_params=pltpu.CompilerParams(vmem_limit_bytes=LIMIT),
        cost_estimate=pl.CostEstimate(
            flops=2 * 8192 * 256 * 256, bytes_accessed=6 * 2**20, transcendentals=0
        ),
        name="other_half",
    )(in_vmem(p), in_vmem(g), in_vmem(e), q)


def solve_kernel(gram_in, gram_other, p_mine, p_other, after, inverse_ref, factors_ref):
    solved = inverse_of_factor(gram_in[...] + gram_other[...])
    side = first_projection((R, 2 * R))
    inverse = jnp.concatenate([jnp.where(side, solved, 0.0), jnp.where(side, 0.0, solved)], 0)
    inverse_ref[...] = inverse
    core = lax.axis_index("core")
    block = lax.axis_index("z") * 2 + core
    p = jnp.where(lax.axis_index("x_hi") == core, p_mine[block], p_other[block])
    factors_ref[...] = split_dot(inverse, p, 1, 1).astype(BF16)


def solve(gram, gram_other, p_mine, p_other, after):
    return pl.pallas_call(
        solve_kernel,
        in_specs=[VMEM] * 5,
        out_specs=[VMEM] * 2,
        out_shape=[
            jax.ShapeDtypeStruct((128, 128), F32),
            jax.ShapeDtypeStruct((128, ROWS), BF16),
        ],
        compiler_params=pltpu.CompilerParams(vmem_limit_bytes=LIMIT),
        cost_estimate=pl.CostEstimate(
            flops=2**30, bytes_accessed=2**20, transcendentals=0
        ),
        name="solve",
    )(gram, gram_other, in_vmem(p_mine), in_vmem(p_other), after)


def mean_kernel(pieces, inverse_ref, q_ref, norm_ref):
    total = pieces[0]
    for i in range(1, pieces.shape[0]):
        total = total + pieces[i]
    upper, _ = by_core(inverse_ref[:R], inverse_ref[R:])
    q_mean = split_dot(upper, jnp.concatenate([total, total], 0), 1, 0) * (1.0 / REPLICAS)
    q_ref[...] = q_mean
    norm_ref[...] = jnp.full(norm_ref.shape, jnp.sum(q_mean * q_mean), F32)


def mean(pieces, inverse):
    return pl.pallas_call(
        mean_kernel,
        in_specs=[VMEM] * 2,
        out_specs=[VMEM] * 2,
        out_shape=[
            jax.ShapeDtypeStruct((R, 128), F32),
            jax.ShapeDtypeStruct((16, 128), F32),
        ],
        compiler_params=pltpu.CompilerParams(vmem_limit_bytes=LIMIT),
        name="mean",
    )(pieces, inverse)


def error_kernel(inverse_ref, q_mine, q_other, norm_parts, *rest):
    halves, (out_hbm, q_hbm, q_staged, q_sent, weights, staged, sent) = (rest[:3], rest[3:6]), rest[6:]
    core = lax.axis_index("core")
    q_mean = jnp.concatenate(by_core(q_mine[...], q_other[...]), 0)
    norm_square = jnp.sum(norm_parts[...], 0, keepdims=True)
    clip_limit = 0.5 * (2 * KVW * R) ** 0.5
    q_staged[...] = q_mean * jnp.minimum(1.0, clip_limit / jnp.sqrt(norm_square))
    copies = [pltpu.make_async_copy(q_staged, q_hbm, q_sent)]
    copies[0].start()
    high, low = split(split_dot(inverse_ref[...], q_mean, 0, 0))
    line = jnp.concatenate([high, low], 1)
    weights[...] = jnp.concatenate([line, line], 0)
    for h, (sides, g_ref, e_ref) in enumerate(halves):
        for block in range(BLOCKS):
            approx = jnp.dot(sides[block], weights[...], preferred_element_type=F32)
            compensated = g_ref[block].astype(F32) + e_ref[block].astype(F32)
            left = compensated - (approx[:, :128] + approx[:, 128:])
            staged[h, block] = left.astype(BF16)
            if (block + 1) % SEND == 0:
                blocks = pl.ds(block + 1 - SEND, SEND)
                place = core if h == 0 else 1 - core
                copies.append(
                    pltpu.make_async_copy(
                        staged.at[h, blocks], out_hbm.at[place, blocks], sent.at[h, block // SEND]
                    )
                )
                copies[-1].start()
    for copy in copies:
        copy.wait()


def errors_out(inverse, q_mine, q_other, norm_parts, mine, other):
    return pl.pallas_call(
        error_kernel,
        in_specs=[VMEM] * 10,
        out_specs=[ANY, ANY],
        out_shape=[
            jax.ShapeDtypeStruct((2, BLOCKS, 2 * ROWS, 128), BF16),
            jax.ShapeDtypeStruct((128, 128), F32),
        ],
        scratch_shapes=[
            pltpu.VMEM((128, 128), F32),
            pltpu.SemaphoreType.DMA,
            pltpu.VMEM((256, 256), BF16),
            pltpu.VMEM((2, *HALF_X), BF16),
            pltpu.SemaphoreType.DMA((2, BLOCKS // SEND)),
        ],
        compiler_params=pltpu.CompilerParams(vmem_limit_bytes=LIMIT),
        cost_estimate=pl.CostEstimate(
            flops=2 * 16384 * 256 * 256, bytes_accessed=16 * 2**20, transcendentals=0
        ),
        name="new_errors",
    )(inverse, q_mine, q_other, norm_parts, *[in_vmem(a) for a in (*mine, *other)])


def sum_kernel(pieces, out_ref):
    total = pieces[0]
    for i in range(1, pieces.shape[0]):
        total = total + pieces[i]
    if len(out_ref.shape) == 2:
        out_ref[...] = total
    else:
        for i in range(out_ref.shape[0]):
            out_ref[i] = total


def sum_pieces(pieces, copies=None):
    shape = pieces.shape[1:] if copies is None else (copies, *pieces.shape[1:])
    return pl.pallas_call(
        sum_kernel,
        in_specs=[VMEM],
        out_specs=VMEM,
        out_shape=jax.ShapeDtypeStruct(shape, F32),
        compiler_params=pltpu.CompilerParams(vmem_limit_bytes=LIMIT),
        name="sum_pieces",
    )(pieces)


def add_kernel(a_ref, b_ref, after, out_ref):
    total = a_ref[...] + b_ref[...]
    for i in range(out_ref.shape[0]):
        out_ref[i] = total


def add_for_each(a, b, copies, after):
    return pl.pallas_call(
        add_kernel,
        in_specs=[VMEM] * 3,
        out_specs=VMEM,
        out_shape=jax.ShapeDtypeStruct((copies, *a.shape), F32),
        compiler_params=pltpu.CompilerParams(vmem_limit_bytes=LIMIT),
        name="add_for_each",
    )(a, b, after)


def to_each(block, count):
    return jnp.broadcast_to(block[None], (count, *block.shape))


def swap(value, axis="core"):
    return lax.ppermute(value, axis, [(0, 1), (1, 0)])


def per_device(grads, errors, q_prev):
    g = grads.reshape(2, BLOCKS, 2 * ROWS, 128)
    e = errors.reshape(2, BLOCKS, 2 * ROWS, 128)
    qt = q_prev.transpose(0, 2, 1).reshape(2 * R, 128)

    part_other, g_other, e_other = left_half(False, g, e, qt)
    sent = swap(part_other)
    part, g_mine, e_mine = left_half(True, g, e, qt)
    part = exchange((part + sent).reshape(8, 512, 128), NEAR)
    part = sum_pieces(part).reshape(16, 32, 128)
    part = sum_pieces(exchange(part, FAR), 16)
    part = exchange(part, FAR).reshape(512, 128)
    p_mine = exchange(to_each(part, 8), NEAR).reshape(HALF_P)
    p_other = swap(p_mine)

    q_part, gram, sides_mine = right_half(p_mine, g_mine, e_mine)
    gram_other = swap(gram)
    q_keep, q_send, sides_other = other_half(p_other, g_other, e_other, q_part)

    q_chip = q_keep + swap(q_send)
    q_sent = swap(q_chip, "x_hi")
    inverse, p_factors = solve(gram, gram_other, p_mine, p_other, q_chip)
    q_chips = add_for_each(q_chip, q_sent, 8, inverse)
    q_chips = lax.all_to_all(q_chips, "z", 0, 0, tiled=True)
    q_mine, norm_part = mean(q_chips, inverse)
    q_other = swap(q_mine)
    norm_parts = lax.all_to_all(norm_part[:, None], BLOCK, 0, 0, tiled=True)

    new_errors, q_factors = errors_out(
        inverse,
        q_mine,
        q_other,
        norm_parts.reshape(16, 128),
        (sides_mine, g_mine, e_mine),
        (sides_other, g_other, e_other),
    )
    return (
        new_errors.reshape(1, D, 2, 128),
        p_factors.reshape(2, R, ROWS).transpose(0, 2, 1),
        q_factors.reshape(2, R, 128).transpose(0, 2, 1),
    )


def solution(mesh):
    named = Mesh(mesh.devices.reshape(2, 8, 2, 4, 2), AXES)
    in_specs = (
        P(REPLICA, None, None, TENSOR),
        P(REPLICA, None, None, TENSOR),
        P(None, TENSOR, None),
    )
    out_specs = (P(REPLICA, None, None, TENSOR), P(None, REPLICA, None), P(None, TENSOR, None))
    return jax.shard_map(
        per_device, mesh=named, in_specs=in_specs, out_specs=out_specs, check_vma=False
    )
```

```python
import functools

import jax
import jax.numpy as jnp
from jax import lax
from jax.experimental import pallas as pl
from jax.experimental.pallas import tpu as pltpu
from jax.sharding import Mesh
from jax.sharding import PartitionSpec as P

D = 8192
KVW = 1024
R = 64
REPLICAS = 32
F32 = jnp.float32
BF16 = jnp.bfloat16

AXES = ("x_hi", "z", "core", "y", "x_lo")
REPLICA = ("x_hi", "z", "core")
TENSOR = ("y", "x_lo")
BLOCK = ("core", "y", "x_lo")

BLOCKS = 16
ROWS = 256
LOADS = (8, 8)
AHEAD = 2
STEP = 4
SEND = 2
PANEL = 8
LIMIT = 16 * 1024 * 1024


def chip_groups():
    def device(x, z, core, y):
        return (((x // 2 * 8 + z) * 2 + core) * 4 + y) * 2 + x % 2

    def line(core, along, across, z):
        x, y = (along, across) if core == 0 else (across, along)
        return device(x, z, core, y)

    near, far = [], []
    for core in range(2):
        pairs = [((2 * k + core) % 8, (2 * k + core + 1) % 8) for k in range(4)]
        for across in range(4):
            for pair in pairs:
                near.append([line(core, i, across, z) for z in pair for i in range(4)])
            for which in range(2):
                far.append([line(core, across, i, p[which]) for p in pairs for i in range(4)])
    return near, far


NEAR, FAR = chip_groups()


WAYS = ((1, 0), (0, 1), (0, 3), (0, 2), (1, 1), (1, 3), (1, 2))


def way_pairs(flip, shift):
    pairs = []
    for group in NEAR:
        for at in range(8):
            there = (at // 4 ^ flip) * 4 + (at + shift) % 4
            pairs.append((group[at], group[there]))
    return pairs


def exchange(pieces, groups):
    return lax.all_to_all(pieces, AXES, 0, 0, axis_index_groups=groups, tiled=True)


def in_hbm(value):
    return pltpu.with_memory_space_constraint(value, pltpu.HBM)


def split(value):
    high = value.astype(BF16)
    low = (value - high.astype(F32)).astype(BF16)
    return high, low


def split_dot(a, b, a_dim, b_dim):
    line = jnp.concatenate(split(b), 1 - b_dim)
    both = lax.dot_general(
        jnp.concatenate(split(a), a_dim),
        jnp.concatenate([line, line], b_dim),
        (((a_dim,), (b_dim,)), ((), ())),
        preferred_element_type=F32,
    )
    n = both.shape[1] // 2
    return both[:, :n] + both[:, n:]


def first_projection(shape):
    return lax.broadcasted_iota(jnp.int32, shape, len(shape) - 1) < R


VMEM = pl.BlockSpec(memory_space=pltpu.VMEM)
ANY = pl.BlockSpec(memory_space=pl.ANY)
HALF_P = (BLOCKS, ROWS, 128)
HALF_X = (BLOCKS, 2 * ROWS, 128)
HALF_S = (BLOCKS, 2 * ROWS, 256)


def in_vmem(value):
    return pltpu.with_memory_space_constraint(value, pltpu.VMEM)


def left_kernel(mine, g_hbm, e_hbm, qt_hbm, p_ref, g_ref, e_ref, qt, weights, rows, arrived, qt_arrived):
    core = lax.axis_index("core")
    half = core if mine else 1 - core
    qt_copy = pltpu.make_async_copy(qt_hbm, qt, qt_arrived)
    qt_copy.start()
    copies = []
    for c, count in enumerate(LOADS):
        blocks = pl.ds(sum(LOADS[:c]), count)
        pair = (
            pltpu.make_async_copy(g_hbm.at[half, blocks], g_ref.at[blocks], arrived.at[0, c]),
            pltpu.make_async_copy(e_hbm.at[half, blocks], e_ref.at[blocks], arrived.at[1, c]),
        )
        copies.append(pair)
    for pair in copies[:AHEAD]:
        for copy in pair:
            copy.start(priority=1)
    qt_copy.wait()
    high, low = split(qt[...])
    weights[...] = jnp.concatenate(
        [jnp.concatenate([high, high], 1), jnp.concatenate([low, low], 1)], 0
    )
    mask = first_projection((ROWS, 2 * R))
    for c, pair in enumerate(copies):
        for copy in pair:
            copy.wait()
        for copy in copies[c + AHEAD] if c + AHEAD < len(copies) else ():
            copy.start(priority=1)
        for block in range(sum(LOADS[:c]), sum(LOADS[: c + 1])):
            x = jnp.concatenate([g_ref[block], e_ref[block]], 1)
            both = lax.dot_general(
                x, weights[...], (((1,), (1,)), ((), ())), preferred_element_type=F32
            )
            slot = rows.at[block % STEP]
            slot[...] = both[:, : 2 * R] + both[:, 2 * R :]
            even = slot[pl.ds(0, ROWS, stride=2), :]
            odd = slot[pl.ds(1, ROWS, stride=2), :]
            p_ref[block] = jnp.where(mask, even, odd)


def left_half(mine, g, e, qt):
    return pl.pallas_call(
        functools.partial(left_kernel, mine),
        in_specs=[ANY, ANY, ANY],
        out_specs=[VMEM, VMEM, VMEM],
        out_shape=[
            pltpu.VMEM(HALF_P, F32),
            pltpu.VMEM(HALF_X, BF16),
            pltpu.VMEM(HALF_X, BF16),
        ],
        scratch_shapes=[
            pltpu.VMEM((2 * R, 128), F32),
            pltpu.VMEM((256, 256), BF16),
            pltpu.VMEM((STEP, 2 * ROWS, 128), F32),
            pltpu.SemaphoreType.DMA((2, len(LOADS))),
            pltpu.SemaphoreType.DMA,
        ],
        compiler_params=pltpu.CompilerParams(vmem_limit_bytes=LIMIT),
        cost_estimate=pl.CostEstimate(
            flops=2 * 8192 * 256 * 256, bytes_accessed=8 * 2**20, transcendentals=0
        ),
        name="left_half",
    )(in_hbm(g), in_hbm(e), in_hbm(qt))


def interleave(p, rows, mask):
    rows[pl.ds(0, ROWS, stride=2), :] = jnp.where(mask, p, 0.0)
    rows[pl.ds(1, ROWS, stride=2), :] = jnp.where(mask, 0.0, p)
    return jnp.concatenate(split(rows[...]), 1)


def quadrants(total):
    n = total.shape[0] // 2
    return total[:n, :n] + total[:n, n:] + total[n:, :n] + total[n:, n:]


def add_rows(total, a, b):
    total[...] += lax.dot_general(
        a, b, (((0,), (0,)), ((), ())), preferred_element_type=F32
    )


def right_step(c, p_ref, g_ref, e_ref, sides, q_total, rows, mask):
    for j in range(STEP):
        sides[c * STEP + j] = interleave(p_ref[c * STEP + j], rows.at[j], mask)
    blocks = pl.ds(c * STEP, STEP)
    depth = STEP * 2 * ROWS
    x = jnp.concatenate(
        [g_ref[blocks].reshape(depth, 128), e_ref[blocks].reshape(depth, 128)], 1
    )
    add_rows(q_total, sides[blocks].reshape(depth, 256), x)


RIGHT_SCRATCH = [pltpu.VMEM((256, 256), F32), pltpu.VMEM((STEP, 2 * ROWS, 128), F32)]


def right_kernel(p_ref, g_ref, e_ref, q_ref, gram_ref, sides, gram_total, q_total, rows):
    q_total[...] = jnp.zeros_like(q_total)
    gram_total[...] = jnp.zeros_like(gram_total)
    mask = first_projection((ROWS, 2 * R))
    for c in range(BLOCKS // STEP):
        right_step(c, p_ref, g_ref, e_ref, sides, q_total, rows, mask)
        for j in range(STEP):
            plain = jnp.concatenate(split(p_ref[c * STEP + j]), 1)
            add_rows(gram_total, plain, plain)

    q_ref[...] = quadrants(q_total[...])
    gram_ref[...] = quadrants(gram_total[...])


def right_half(p, g, e):
    square = jax.ShapeDtypeStruct((128, 128), F32)
    return pl.pallas_call(
        right_kernel,
        in_specs=[VMEM] * 3,
        out_specs=[VMEM] * 3,
        out_shape=[square, square, pltpu.VMEM(HALF_S, BF16)],
        scratch_shapes=[pltpu.VMEM((256, 256), F32), *RIGHT_SCRATCH],
        compiler_params=pltpu.CompilerParams(vmem_limit_bytes=LIMIT),
        cost_estimate=pl.CostEstimate(
            flops=3 * 8192 * 256 * 256, bytes_accessed=6 * 2**20, transcendentals=0
        ),
        name="right_half",
    )(in_vmem(p), in_vmem(g), in_vmem(e))


def inverse_of_factor(gram):
    mask = first_projection((R, 2 * R))
    lane = lax.broadcasted_iota(jnp.int32, (R, 2 * R), 1)
    row = lax.broadcasted_iota(jnp.int32, (R, 2 * R), 0)
    rest = jnp.where(mask, gram[:R], gram[R:])
    inverse = jnp.where(lane % R == row, 1.0, 0.0).astype(F32)
    pivots = jnp.ones((R, 2 * R), F32)
    for start in range(0, R, PANEL):
        panel = [
            jnp.where(mask, rest[:, j : j + 1], rest[:, R + j : R + j + 1])
            for j in range(start, start + PANEL)
        ]
        for i in range(0, PANEL, 2):
            j = start + i
            first, second = panel[i], panel[i + 1]
            a, b, c = first[j : j + 1], first[j + 1 : j + 2], second[j + 1 : j + 2]
            a_inverse = 1.0 / a
            ratio = b * a_inverse
            rest_c = c - b * ratio
            pivots = jnp.where(row == j, a, pivots)
            pivots = jnp.where(row == j + 1, rest_c, pivots)
            one = jnp.where(row > j, first * a_inverse, 0.0)
            two = (second - one * b) * (1.0 / rest_c)
            two = jnp.where(row > j + 1, two, 0.0)

            def eliminate(matrix):
                upper = matrix[j : j + 1]
                lower = matrix[j + 1 : j + 2] - ratio * upper
                return matrix - one * upper - two * lower

            for m in range(i + 2, PANEL):
                panel[m] = eliminate(panel[m])
            inverse = eliminate(inverse)
            rest = eliminate(rest)
    return inverse * lax.rsqrt(pivots)


def by_core(first, second):
    low = lax.axis_index("core") == 0
    return jnp.where(low, first, second), jnp.where(low, second, first)


def other_kernel(p_ref, g_ref, e_ref, q_in, keep_ref, send_ref, sides, q_total, rows):
    q_total[...] = jnp.zeros_like(q_total)
    mask = first_projection((ROWS, 2 * R))
    for c in range(BLOCKS // STEP):
        right_step(c, p_ref, g_ref, e_ref, sides, q_total, rows, mask)
    q = quadrants(q_total[...]) + q_in[...]
    keep_ref[...], send_ref[...] = by_core(q[:R], q[R:])


def other_half(p, g, e, q):
    part = jax.ShapeDtypeStruct((R, 128), F32)
    return pl.pallas_call(
        other_kernel,
        in_specs=[VMEM] * 4,
        out_specs=[VMEM] * 3,
        out_shape=[part, part, pltpu.VMEM(HALF_S, BF16)],
        scratch_shapes=RIGHT_SCRATCH,
        compiler_params=pltpu.CompilerParams(vmem_limit_bytes=LIMIT),
        cost_estimate=pl.CostEstimate(
            flops=2 * 8192 * 256 * 256, bytes_accessed=6 * 2**20, transcendentals=0
        ),
        name="other_half",
    )(in_vmem(p), in_vmem(g), in_vmem(e), q)


def solve_kernel(gram_in, gram_other, p_mine, p_other, after, inverse_ref, factors_ref):
    solved = inverse_of_factor(gram_in[...] + gram_other[...])
    side = first_projection((R, 2 * R))
    inverse = jnp.concatenate([jnp.where(side, solved, 0.0), jnp.where(side, 0.0, solved)], 0)
    inverse_ref[...] = inverse
    core = lax.axis_index("core")
    block = lax.axis_index("z") * 2 + core
    p = jnp.where(lax.axis_index("x_hi") == core, p_mine[block], p_other[block])
    factors_ref[...] = split_dot(inverse, p, 1, 1).astype(BF16)


def solve(gram, gram_other, p_mine, p_other, after):
    return pl.pallas_call(
        solve_kernel,
        in_specs=[VMEM] * 5,
        out_specs=[VMEM] * 2,
        out_shape=[
            jax.ShapeDtypeStruct((128, 128), F32),
            jax.ShapeDtypeStruct((128, ROWS), BF16),
        ],
        compiler_params=pltpu.CompilerParams(vmem_limit_bytes=LIMIT),
        cost_estimate=pl.CostEstimate(
            flops=2**30, bytes_accessed=2**20, transcendentals=0
        ),
        name="solve",
    )(gram, gram_other, in_vmem(p_mine), in_vmem(p_other), after)


def mean_kernel(pieces, inverse_ref, q_ref, norm_ref):
    total = pieces[0]
    for i in range(1, pieces.shape[0]):
        total = total + pieces[i]
    upper, _ = by_core(inverse_ref[:R], inverse_ref[R:])
    q_mean = split_dot(upper, jnp.concatenate([total, total], 0), 1, 0) * (1.0 / REPLICAS)
    q_ref[...] = q_mean
    norm_ref[...] = jnp.full(norm_ref.shape, jnp.sum(q_mean * q_mean), F32)


def mean(pieces, inverse):
    return pl.pallas_call(
        mean_kernel,
        in_specs=[VMEM] * 2,
        out_specs=[VMEM] * 2,
        out_shape=[
            jax.ShapeDtypeStruct((R, 128), F32),
            jax.ShapeDtypeStruct((16, 128), F32),
        ],
        compiler_params=pltpu.CompilerParams(vmem_limit_bytes=LIMIT),
        name="mean",
    )(pieces, inverse)


def error_kernel(inverse_ref, q_mine, q_other, norm_parts, *rest):
    halves, (out_hbm, q_hbm, q_staged, q_sent, weights, staged, sent) = (rest[:3], rest[3:6]), rest[6:]
    core = lax.axis_index("core")
    q_mean = jnp.concatenate(by_core(q_mine[...], q_other[...]), 0)
    norm_square = jnp.sum(norm_parts[...], 0, keepdims=True)
    clip_limit = 0.5 * (2 * KVW * R) ** 0.5
    q_staged[...] = q_mean * jnp.minimum(1.0, clip_limit / jnp.sqrt(norm_square))
    copies = [pltpu.make_async_copy(q_staged, q_hbm, q_sent)]
    copies[0].start()
    high, low = split(split_dot(inverse_ref[...], q_mean, 0, 0))
    line = jnp.concatenate([high, low], 1)
    weights[...] = jnp.concatenate([line, line], 0)
    for h, (sides, g_ref, e_ref) in enumerate(halves):
        for block in range(BLOCKS):
            approx = jnp.dot(sides[block], weights[...], preferred_element_type=F32)
            compensated = g_ref[block].astype(F32) + e_ref[block].astype(F32)
            left = compensated - (approx[:, :128] + approx[:, 128:])
            staged[h, block] = left.astype(BF16)
            if (block + 1) % SEND == 0:
                blocks = pl.ds(block + 1 - SEND, SEND)
                place = core if h == 0 else 1 - core
                copies.append(
                    pltpu.make_async_copy(
                        staged.at[h, blocks], out_hbm.at[place, blocks], sent.at[h, block // SEND]
                    )
                )
                copies[-1].start()
    for copy in copies:
        copy.wait()


def errors_out(inverse, q_mine, q_other, norm_parts, mine, other):
    return pl.pallas_call(
        error_kernel,
        in_specs=[VMEM] * 10,
        out_specs=[ANY, ANY],
        out_shape=[
            jax.ShapeDtypeStruct((2, BLOCKS, 2 * ROWS, 128), BF16),
            jax.ShapeDtypeStruct((128, 128), F32),
        ],
        scratch_shapes=[
            pltpu.VMEM((128, 128), F32),
            pltpu.SemaphoreType.DMA,
            pltpu.VMEM((256, 256), BF16),
            pltpu.VMEM((2, *HALF_X), BF16),
            pltpu.SemaphoreType.DMA((2, BLOCKS // SEND)),
        ],
        compiler_params=pltpu.CompilerParams(vmem_limit_bytes=LIMIT),
        cost_estimate=pl.CostEstimate(
            flops=2 * 16384 * 256 * 256, bytes_accessed=16 * 2**20, transcendentals=0
        ),
        name="new_errors",
    )(inverse, q_mine, q_other, norm_parts, *[in_vmem(a) for a in (*mine, *other)])


def sum_kernel(pieces, out_ref):
    total = pieces[0]
    for i in range(1, pieces.shape[0]):
        total = total + pieces[i]
    if len(out_ref.shape) == 2:
        out_ref[...] = total
    else:
        for i in range(out_ref.shape[0]):
            out_ref[i] = total


def sum_pieces(pieces, copies=None):
    shape = pieces.shape[1:] if copies is None else (copies, *pieces.shape[1:])
    return pl.pallas_call(
        sum_kernel,
        in_specs=[VMEM],
        out_specs=VMEM,
        out_shape=jax.ShapeDtypeStruct(shape, F32),
        compiler_params=pltpu.CompilerParams(vmem_limit_bytes=LIMIT),
        name="sum_pieces",
    )(pieces)


def place_kernel(own, *rest):
    *others, out_ref = rest
    core, z = lax.axis_index("core"), lax.axis_index("z")
    pair = (z + core) % 2
    place = jnp.where(core == 0, lax.axis_index("x_hi") * 2 + lax.axis_index("x_lo"), lax.axis_index("y"))
    out_ref[pair * 4 + place] = own[...]
    for (flip, shift), block in zip(WAYS, others):
        out_ref[(pair + flip) % 2 * 4 + (place + 4 - shift) % 4] = block[...]


def gather_near(block):
    others = [lax.ppermute(block, AXES, way_pairs(*way)) for way in WAYS]
    return pl.pallas_call(
        place_kernel,
        in_specs=[VMEM] * 8,
        out_specs=VMEM,
        out_shape=pltpu.VMEM((8, *block.shape), F32),
        compiler_params=pltpu.CompilerParams(vmem_limit_bytes=LIMIT),
        name="gather_near",
    )(block, *others)


def add_kernel(a_ref, b_ref, after, out_ref):
    total = a_ref[...] + b_ref[...]
    for i in range(out_ref.shape[0]):
        out_ref[i] = total


def add_for_each(a, b, copies, after):
    return pl.pallas_call(
        add_kernel,
        in_specs=[VMEM] * 3,
        out_specs=VMEM,
        out_shape=jax.ShapeDtypeStruct((copies, *a.shape), F32),
        compiler_params=pltpu.CompilerParams(vmem_limit_bytes=LIMIT),
        name="add_for_each",
    )(a, b, after)


def swap(value, axis="core"):
    return lax.ppermute(value, axis, [(0, 1), (1, 0)])


def per_device(grads, errors, q_prev):
    g = grads.reshape(2, BLOCKS, 2 * ROWS, 128)
    e = errors.reshape(2, BLOCKS, 2 * ROWS, 128)
    qt = q_prev.transpose(0, 2, 1).reshape(2 * R, 128)

    part_other, g_other, e_other = left_half(False, g, e, qt)
    sent = swap(part_other)
    part, g_mine, e_mine = left_half(True, g, e, qt)
    part = exchange((part + sent).reshape(8, 512, 128), NEAR)
    part = sum_pieces(part).reshape(16, 32, 128)
    part = sum_pieces(exchange(part, FAR), 16)
    part = exchange(part, FAR).reshape(512, 128)
    p_mine = gather_near(part).reshape(HALF_P)
    p_other = swap(p_mine)

    q_part, gram, sides_mine = right_half(p_mine, g_mine, e_mine)
    gram_other = swap(gram)
    q_keep, q_send, sides_other = other_half(p_other, g_other, e_other, q_part)

    q_chip = q_keep + swap(q_send)
    q_sent = swap(q_chip, "x_hi")
    inverse, p_factors = solve(gram, gram_other, p_mine, p_other, q_chip)
    q_chips = add_for_each(q_chip, q_sent, 8, inverse)
    q_chips = lax.all_to_all(q_chips, "z", 0, 0, tiled=True)
    q_mine, norm_part = mean(q_chips, inverse)
    q_other = swap(q_mine)
    norm_parts = lax.all_to_all(norm_part[:, None], BLOCK, 0, 0, tiled=True)

    new_errors, q_factors = errors_out(
        inverse,
        q_mine,
        q_other,
        norm_parts.reshape(16, 128),
        (sides_mine, g_mine, e_mine),
        (sides_other, g_other, e_other),
    )
    return (
        new_errors.reshape(1, D, 2, 128),
        p_factors.reshape(2, R, ROWS).transpose(0, 2, 1),
        q_factors.reshape(2, R, 128).transpose(0, 2, 1),
    )


def solution(mesh):
    named = Mesh(mesh.devices.reshape(2, 8, 2, 4, 2), AXES)
    in_specs = (
        P(REPLICA, None, None, TENSOR),
        P(REPLICA, None, None, TENSOR),
        P(None, TENSOR, None),
    )
    out_specs = (P(REPLICA, None, None, TENSOR), P(None, REPLICA, None), P(None, TENSOR, None))
    return jax.shard_map(
        per_device, mesh=named, in_specs=in_specs, out_specs=out_specs, check_vma=False
    )
```

```python
import functools

import jax
import jax.numpy as jnp
from jax import lax
from jax.experimental import pallas as pl
from jax.experimental.pallas import tpu as pltpu
from jax.sharding import Mesh
from jax.sharding import PartitionSpec as P

D = 8192
KVW = 1024
R = 64
REPLICAS = 32
F32 = jnp.float32
BF16 = jnp.bfloat16

AXES = ("x_hi", "z", "core", "y", "x_lo")
REPLICA = ("x_hi", "z", "core")
TENSOR = ("y", "x_lo")
BLOCK = ("core", "y", "x_lo")

BLOCKS = 16
ROWS = 256
LOADS = (8, 8)
AHEAD = 2
STEP = 4
SEND = 2
PANEL = 8
LIMIT = 16 * 1024 * 1024


def chip_groups():
    def device(x, z, core, y):
        return (((x // 2 * 8 + z) * 2 + core) * 4 + y) * 2 + x % 2

    def line(core, along, across, z):
        x, y = (along, across) if core == 0 else (across, along)
        return device(x, z, core, y)

    near, far = [], []
    for core in range(2):
        pairs = [((2 * k + core) % 8, (2 * k + core + 1) % 8) for k in range(4)]
        for across in range(4):
            for pair in pairs:
                near.append([line(core, i, across, z) for z in pair for i in range(4)])
            for which in range(2):
                far.append([line(core, across, i, p[which]) for p in pairs for i in range(4)])
    return near, far


NEAR, FAR = chip_groups()


WAYS = ((1, 0), (0, 1), (0, 3), (0, 2), (1, 1), (1, 3), (1, 2))


def way_pairs(flip, shift):
    pairs = []
    for group in NEAR:
        for at in range(8):
            there = (at // 4 ^ flip) * 4 + (at + shift) % 4
            pairs.append((group[at], group[there]))
    return pairs


def exchange(pieces, groups):
    return lax.all_to_all(pieces, AXES, 0, 0, axis_index_groups=groups, tiled=True)


def in_hbm(value):
    return pltpu.with_memory_space_constraint(value, pltpu.HBM)


def split(value):
    high = value.astype(BF16)
    low = (value - high.astype(F32)).astype(BF16)
    return high, low


def split_dot(a, b, a_dim, b_dim):
    line = jnp.concatenate(split(b), 1 - b_dim)
    both = lax.dot_general(
        jnp.concatenate(split(a), a_dim),
        jnp.concatenate([line, line], b_dim),
        (((a_dim,), (b_dim,)), ((), ())),
        preferred_element_type=F32,
    )
    n = both.shape[1] // 2
    return both[:, :n] + both[:, n:]


def first_projection(shape):
    return lax.broadcasted_iota(jnp.int32, shape, len(shape) - 1) < R


VMEM = pl.BlockSpec(memory_space=pltpu.VMEM)
ANY = pl.BlockSpec(memory_space=pl.ANY)
HALF_P = (BLOCKS, ROWS, 128)
HALF_X = (BLOCKS, 2 * ROWS, 128)
HALF_S = (BLOCKS, 2 * ROWS, 256)


def in_vmem(value):
    return pltpu.with_memory_space_constraint(value, pltpu.VMEM)


def left_kernel(mine, g_hbm, e_hbm, qt_hbm, p_ref, g_ref, e_ref, qt, weights, rows, arrived, qt_arrived):
    core = lax.axis_index("core")
    half = core if mine else 1 - core
    qt_copy = pltpu.make_async_copy(qt_hbm, qt, qt_arrived)
    qt_copy.start()
    copies = []
    for c, count in enumerate(LOADS):
        blocks = pl.ds(sum(LOADS[:c]), count)
        pair = (
            pltpu.make_async_copy(g_hbm.at[half, blocks], g_ref.at[blocks], arrived.at[0, c]),
            pltpu.make_async_copy(e_hbm.at[half, blocks], e_ref.at[blocks], arrived.at[1, c]),
        )
        copies.append(pair)
    for pair in copies[:AHEAD]:
        for copy in pair:
            copy.start(priority=1)
    qt_copy.wait()
    high, low = split(qt[...])
    weights[...] = jnp.concatenate(
        [jnp.concatenate([high, high], 1), jnp.concatenate([low, low], 1)], 0
    )
    mask = first_projection((ROWS, 2 * R))
    for c, pair in enumerate(copies):
        for copy in pair:
            copy.wait()
        for copy in copies[c + AHEAD] if c + AHEAD < len(copies) else ():
            copy.start(priority=1)
        for block in range(sum(LOADS[:c]), sum(LOADS[: c + 1])):
            x = jnp.concatenate([g_ref[block], e_ref[block]], 1)
            both = lax.dot_general(
                x, weights[...], (((1,), (1,)), ((), ())), preferred_element_type=F32
            )
            slot = rows.at[block % STEP]
            slot[...] = both[:, : 2 * R] + both[:, 2 * R :]
            even = slot[pl.ds(0, ROWS, stride=2), :]
            odd = slot[pl.ds(1, ROWS, stride=2), :]
            p_ref[block] = jnp.where(mask, even, odd)


def left_half(mine, g, e, qt):
    return pl.pallas_call(
        functools.partial(left_kernel, mine),
        in_specs=[ANY, ANY, ANY],
        out_specs=[VMEM, VMEM, VMEM],
        out_shape=[
            pltpu.VMEM(HALF_P, F32),
            pltpu.VMEM(HALF_X, BF16),
            pltpu.VMEM(HALF_X, BF16),
        ],
        scratch_shapes=[
            pltpu.VMEM((2 * R, 128), F32),
            pltpu.VMEM((256, 256), BF16),
            pltpu.VMEM((STEP, 2 * ROWS, 128), F32),
            pltpu.SemaphoreType.DMA((2, len(LOADS))),
            pltpu.SemaphoreType.DMA,
        ],
        compiler_params=pltpu.CompilerParams(vmem_limit_bytes=LIMIT),
        cost_estimate=pl.CostEstimate(
            flops=2 * 8192 * 256 * 256, bytes_accessed=8 * 2**20, transcendentals=0
        ),
        name="left_half",
    )(in_hbm(g), in_hbm(e), in_hbm(qt))


def interleave(p, rows, mask):
    rows[pl.ds(0, ROWS, stride=2), :] = jnp.where(mask, p, 0.0)
    rows[pl.ds(1, ROWS, stride=2), :] = jnp.where(mask, 0.0, p)
    return jnp.concatenate(split(rows[...]), 1)


def quadrants(total):
    n = total.shape[0] // 2
    return total[:n, :n] + total[:n, n:] + total[n:, :n] + total[n:, n:]


def add_rows(total, a, b):
    total[...] += lax.dot_general(
        a, b, (((0,), (0,)), ((), ())), preferred_element_type=F32
    )


def right_step(c, p_ref, g_ref, e_ref, sides, q_total, rows, mask):
    for j in range(STEP):
        sides[c * STEP + j] = interleave(p_ref[c * STEP + j], rows.at[j], mask)
    blocks = pl.ds(c * STEP, STEP)
    depth = STEP * 2 * ROWS
    x = jnp.concatenate(
        [g_ref[blocks].reshape(depth, 128), e_ref[blocks].reshape(depth, 128)], 1
    )
    add_rows(q_total, sides[blocks].reshape(depth, 256), x)


RIGHT_SCRATCH = [pltpu.VMEM((256, 256), F32), pltpu.VMEM((STEP, 2 * ROWS, 128), F32)]


def right_kernel(p_ref, g_ref, e_ref, q_ref, gram_ref, sides, gram_total, q_total, rows):
    q_total[...] = jnp.zeros_like(q_total)
    gram_total[...] = jnp.zeros_like(gram_total)
    mask = first_projection((ROWS, 2 * R))
    for c in range(BLOCKS // STEP):
        right_step(c, p_ref, g_ref, e_ref, sides, q_total, rows, mask)
        for j in range(STEP):
            plain = jnp.concatenate(split(p_ref[c * STEP + j]), 1)
            add_rows(gram_total, plain, plain)

    q_ref[...] = quadrants(q_total[...])
    gram_ref[...] = quadrants(gram_total[...])


def right_half(p, g, e):
    square = jax.ShapeDtypeStruct((128, 128), F32)
    return pl.pallas_call(
        right_kernel,
        in_specs=[VMEM] * 3,
        out_specs=[VMEM] * 3,
        out_shape=[square, square, pltpu.VMEM(HALF_S, BF16)],
        scratch_shapes=[pltpu.VMEM((256, 256), F32), *RIGHT_SCRATCH],
        compiler_params=pltpu.CompilerParams(vmem_limit_bytes=LIMIT),
        cost_estimate=pl.CostEstimate(
            flops=3 * 8192 * 256 * 256, bytes_accessed=6 * 2**20, transcendentals=0
        ),
        name="right_half",
    )(in_vmem(p), in_vmem(g), in_vmem(e))


def inverse_of_factor(gram):
    mask = first_projection((R, 2 * R))
    lane = lax.broadcasted_iota(jnp.int32, (R, 2 * R), 1)
    row = lax.broadcasted_iota(jnp.int32, (R, 2 * R), 0)
    rest = jnp.where(mask, gram[:R], gram[R:])
    inverse = jnp.where(lane % R == row, 1.0, 0.0).astype(F32)
    pivots = jnp.ones((R, 2 * R), F32)
    for start in range(0, R, PANEL):
        panel = [
            jnp.where(mask, rest[:, j : j + 1], rest[:, R + j : R + j + 1])
            for j in range(start, start + PANEL)
        ]
        for i in range(0, PANEL, 2):
            j = start + i
            first, second = panel[i], panel[i + 1]
            a, b, c = first[j : j + 1], first[j + 1 : j + 2], second[j + 1 : j + 2]
            a_inverse = 1.0 / a
            ratio = b * a_inverse
            rest_c = c - b * ratio
            pivots = jnp.where(row == j, a, pivots)
            pivots = jnp.where(row == j + 1, rest_c, pivots)
            one = jnp.where(row > j, first * a_inverse, 0.0)
            two = (second - one * b) * (1.0 / rest_c)
            two = jnp.where(row > j + 1, two, 0.0)

            def eliminate(matrix):
                upper = matrix[j : j + 1]
                lower = matrix[j + 1 : j + 2] - ratio * upper
                return matrix - one * upper - two * lower

            for m in range(i + 2, PANEL):
                panel[m] = eliminate(panel[m])
            inverse = eliminate(inverse)
            rest = eliminate(rest)
    return inverse * lax.rsqrt(pivots)


def by_core(first, second):
    low = lax.axis_index("core") == 0
    return jnp.where(low, first, second), jnp.where(low, second, first)


def other_kernel(p_ref, g_ref, e_ref, q_in, keep_ref, send_ref, sides, q_total, rows):
    q_total[...] = jnp.zeros_like(q_total)
    mask = first_projection((ROWS, 2 * R))
    for c in range(BLOCKS // STEP):
        right_step(c, p_ref, g_ref, e_ref, sides, q_total, rows, mask)
    q = quadrants(q_total[...]) + q_in[...]
    keep_ref[...], send_ref[...] = by_core(q[:R], q[R:])


def other_half(p, g, e, q):
    part = jax.ShapeDtypeStruct((R, 128), F32)
    return pl.pallas_call(
        other_kernel,
        in_specs=[VMEM] * 4,
        out_specs=[VMEM] * 3,
        out_shape=[part, part, pltpu.VMEM(HALF_S, BF16)],
        scratch_shapes=RIGHT_SCRATCH,
        compiler_params=pltpu.CompilerParams(vmem_limit_bytes=LIMIT),
        cost_estimate=pl.CostEstimate(
            flops=2 * 8192 * 256 * 256, bytes_accessed=6 * 2**20, transcendentals=0
        ),
        name="other_half",
    )(in_vmem(p), in_vmem(g), in_vmem(e), q)


def solve_kernel(gram_in, gram_other, p_mine, p_other, after, inverse_ref, factors_ref):
    solved = inverse_of_factor(gram_in[...] + gram_other[...])
    side = first_projection((R, 2 * R))
    inverse = jnp.concatenate([jnp.where(side, solved, 0.0), jnp.where(side, 0.0, solved)], 0)
    inverse_ref[...] = inverse
    core = lax.axis_index("core")
    block = lax.axis_index("z") * 2 + core
    p = jnp.where(lax.axis_index("x_hi") == core, p_mine[block], p_other[block])
    factors_ref[...] = split_dot(inverse, p, 1, 1).astype(BF16)


def solve(gram, gram_other, p_mine, p_other, after):
    return pl.pallas_call(
        solve_kernel,
        in_specs=[VMEM] * 5,
        out_specs=[VMEM] * 2,
        out_shape=[
            jax.ShapeDtypeStruct((128, 128), F32),
            jax.ShapeDtypeStruct((128, ROWS), BF16),
        ],
        compiler_params=pltpu.CompilerParams(vmem_limit_bytes=LIMIT),
        cost_estimate=pl.CostEstimate(
            flops=2**30, bytes_accessed=2**20, transcendentals=0
        ),
        name="solve",
    )(gram, gram_other, in_vmem(p_mine), in_vmem(p_other), after)


def mean_kernel(pieces, inverse_ref, q_ref, norm_ref):
    total = pieces[0]
    for i in range(1, pieces.shape[0]):
        total = total + pieces[i]
    upper, _ = by_core(inverse_ref[:R], inverse_ref[R:])
    q_mean = split_dot(upper, jnp.concatenate([total, total], 0), 1, 0) * (1.0 / REPLICAS)
    q_ref[...] = q_mean
    norm_ref[...] = jnp.full(norm_ref.shape, jnp.sum(q_mean * q_mean), F32)


def mean(pieces, inverse):
    return pl.pallas_call(
        mean_kernel,
        in_specs=[VMEM] * 2,
        out_specs=[VMEM] * 2,
        out_shape=[
            jax.ShapeDtypeStruct((R, 128), F32),
            jax.ShapeDtypeStruct((16, 128), F32),
        ],
        compiler_params=pltpu.CompilerParams(vmem_limit_bytes=LIMIT),
        name="mean",
    )(pieces, inverse)


def error_kernel(inverse_ref, q_mine, q_other, norm_parts, *rest):
    halves, (out_hbm, q_hbm, q_staged, q_sent, weights, staged, sent) = (rest[:3], rest[3:6]), rest[6:]
    core = lax.axis_index("core")
    q_mean = jnp.concatenate(by_core(q_mine[...], q_other[...]), 0)
    norm_square = jnp.sum(norm_parts[...], 0, keepdims=True)
    clip_limit = 0.5 * (2 * KVW * R) ** 0.5
    q_staged[...] = q_mean * jnp.minimum(1.0, clip_limit / jnp.sqrt(norm_square))
    copies = [pltpu.make_async_copy(q_staged, q_hbm, q_sent)]
    copies[0].start()
    high, low = split(split_dot(inverse_ref[...], q_mean, 0, 0))
    line = jnp.concatenate([high, low], 1)
    weights[...] = jnp.concatenate([line, line], 0)
    for h, (sides, g_ref, e_ref) in enumerate(halves):
        for block in range(BLOCKS):
            approx = jnp.dot(sides[block], weights[...], preferred_element_type=F32)
            compensated = g_ref[block].astype(F32) + e_ref[block].astype(F32)
            left = compensated - (approx[:, :128] + approx[:, 128:])
            staged[h, block] = left.astype(BF16)
            if (block + 1) % SEND == 0:
                blocks = pl.ds(block + 1 - SEND, SEND)
                place = core if h == 0 else 1 - core
                copies.append(
                    pltpu.make_async_copy(
                        staged.at[h, blocks], out_hbm.at[place, blocks], sent.at[h, block // SEND]
                    )
                )
                copies[-1].start()
    for copy in copies:
        copy.wait()


def errors_out(inverse, q_mine, q_other, norm_parts, mine, other):
    return pl.pallas_call(
        error_kernel,
        in_specs=[VMEM] * 10,
        out_specs=[ANY, ANY],
        out_shape=[
            jax.ShapeDtypeStruct((2, BLOCKS, 2 * ROWS, 128), BF16),
            jax.ShapeDtypeStruct((128, 128), F32),
        ],
        scratch_shapes=[
            pltpu.VMEM((128, 128), F32),
            pltpu.SemaphoreType.DMA,
            pltpu.VMEM((256, 256), BF16),
            pltpu.VMEM((2, *HALF_X), BF16),
            pltpu.SemaphoreType.DMA((2, BLOCKS // SEND)),
        ],
        compiler_params=pltpu.CompilerParams(vmem_limit_bytes=LIMIT),
        cost_estimate=pl.CostEstimate(
            flops=2 * 16384 * 256 * 256, bytes_accessed=16 * 2**20, transcendentals=0
        ),
        name="new_errors",
    )(inverse, q_mine, q_other, norm_parts, *[in_vmem(a) for a in (*mine, *other)])


def sum_kernel(pieces, out_ref):
    total = pieces[0]
    for i in range(1, pieces.shape[0]):
        total = total + pieces[i]
    if len(out_ref.shape) == 2:
        out_ref[...] = total
    else:
        for i in range(out_ref.shape[0]):
            out_ref[i] = total


def sum_pieces(pieces, copies=None):
    shape = pieces.shape[1:] if copies is None else (copies, *pieces.shape[1:])
    return pl.pallas_call(
        sum_kernel,
        in_specs=[VMEM],
        out_specs=VMEM,
        out_shape=jax.ShapeDtypeStruct(shape, F32),
        compiler_params=pltpu.CompilerParams(vmem_limit_bytes=LIMIT),
        name="sum_pieces",
    )(pieces)


def place_kernel(own, *rest):
    *others, out_ref = rest
    core, z = lax.axis_index("core"), lax.axis_index("z")
    pair = (z + core) % 2
    place = jnp.where(core == 0, lax.axis_index("x_hi") * 2 + lax.axis_index("x_lo"), lax.axis_index("y"))
    out_ref[pair * 4 + place] = own[...]
    for (flip, shift), block in zip(WAYS, others):
        out_ref[(pair + flip) % 2 * 4 + (place + 4 - shift) % 4] = block[...]


def gather_near(block):
    others = [lax.ppermute(block, AXES, way_pairs(*way)) for way in WAYS]
    return pl.pallas_call(
        place_kernel,
        in_specs=[VMEM] * 8,
        out_specs=VMEM,
        out_shape=pltpu.VMEM((8, *block.shape), F32),
        compiler_params=pltpu.CompilerParams(vmem_limit_bytes=LIMIT),
        name="gather_near",
    )(block, *others)


def pieces_kernel(a_ref, b_ref, own, *others):
    core, z = lax.axis_index("core"), lax.axis_index("z")
    pair = (z + core) % 2
    place = jnp.where(core == 0, lax.axis_index("x_hi") * 2 + lax.axis_index("x_lo"), lax.axis_index("y"))
    at = pair * 4 + place
    own[...] = a_ref[at] + b_ref[at]
    for (flip, shift), out_ref in zip(WAYS, others):
        there = (pair + flip) % 2 * 4 + (place + shift) % 4
        out_ref[...] = a_ref[there] + b_ref[there]


def total_kernel(*refs):
    total = refs[0][...]
    for ref in refs[1:-1]:
        total = total + ref[...]
    refs[-1][...] = total


def sum_near(a, b):
    piece = pltpu.VMEM(a.shape[1:], F32)
    own, *others = pl.pallas_call(
        pieces_kernel,
        in_specs=[VMEM] * 2,
        out_specs=[VMEM] * 8,
        out_shape=[piece] * 8,
        compiler_params=pltpu.CompilerParams(vmem_limit_bytes=LIMIT),
        name="near_pieces",
    )(a, b)
    others = [lax.ppermute(o, AXES, way_pairs(*way)) for o, way in zip(others, WAYS)]
    return pl.pallas_call(
        total_kernel,
        in_specs=[VMEM] * 8,
        out_specs=VMEM,
        out_shape=jax.ShapeDtypeStruct(a.shape[1:], F32),
        compiler_params=pltpu.CompilerParams(vmem_limit_bytes=LIMIT),
        name="sum_near",
    )(own, *others)


def add_kernel(a_ref, b_ref, after, out_ref):
    total = a_ref[...] + b_ref[...]
    for i in range(out_ref.shape[0]):
        out_ref[i] = total


def add_for_each(a, b, copies, after):
    return pl.pallas_call(
        add_kernel,
        in_specs=[VMEM] * 3,
        out_specs=VMEM,
        out_shape=jax.ShapeDtypeStruct((copies, *a.shape), F32),
        compiler_params=pltpu.CompilerParams(vmem_limit_bytes=LIMIT),
        name="add_for_each",
    )(a, b, after)


def swap(value, axis="core"):
    return lax.ppermute(value, axis, [(0, 1), (1, 0)])


def per_device(grads, errors, q_prev):
    g = grads.reshape(2, BLOCKS, 2 * ROWS, 128)
    e = errors.reshape(2, BLOCKS, 2 * ROWS, 128)
    qt = q_prev.transpose(0, 2, 1).reshape(2 * R, 128)

    part_other, g_other, e_other = left_half(False, g, e, qt)
    sent = swap(part_other)
    part, g_mine, e_mine = left_half(True, g, e, qt)
    part = sum_near(part.reshape(8, 512, 128), sent.reshape(8, 512, 128)).reshape(16, 32, 128)
    part = sum_pieces(exchange(part, FAR), 16)
    part = exchange(part, FAR).reshape(512, 128)
    p_mine = gather_near(part).reshape(HALF_P)
    p_other = swap(p_mine)

    q_part, gram, sides_mine = right_half(p_mine, g_mine, e_mine)
    gram_other = swap(gram)
    q_keep, q_send, sides_other = other_half(p_other, g_other, e_other, q_part)

    q_chip = q_keep + swap(q_send)
    q_sent = swap(q_chip, "x_hi")
    inverse, p_factors = solve(gram, gram_other, p_mine, p_other, q_chip)
    q_chips = add_for_each(q_chip, q_sent, 8, inverse)
    q_chips = lax.all_to_all(q_chips, "z", 0, 0, tiled=True)
    q_mine, norm_part = mean(q_chips, inverse)
    q_other = swap(q_mine)
    norm_parts = lax.all_to_all(norm_part[:, None], BLOCK, 0, 0, tiled=True)

    new_errors, q_factors = errors_out(
        inverse,
        q_mine,
        q_other,
        norm_parts.reshape(16, 128),
        (sides_mine, g_mine, e_mine),
        (sides_other, g_other, e_other),
    )
    return (
        new_errors.reshape(1, D, 2, 128),
        p_factors.reshape(2, R, ROWS).transpose(0, 2, 1),
        q_factors.reshape(2, R, 128).transpose(0, 2, 1),
    )


def solution(mesh):
    named = Mesh(mesh.devices.reshape(2, 8, 2, 4, 2), AXES)
    in_specs = (
        P(REPLICA, None, None, TENSOR),
        P(REPLICA, None, None, TENSOR),
        P(None, TENSOR, None),
    )
    out_specs = (P(REPLICA, None, None, TENSOR), P(None, REPLICA, None), P(None, TENSOR, None))
    return jax.shard_map(
        per_device, mesh=named, in_specs=in_specs, out_specs=out_specs, check_vma=False
    )
```
